32 devices in a mesh: dp: 8 (over y, x, core), mod: 4 (over z).
Axes of the slice: x: 2, y: 2, z: 4, core: 2. Of those that a mesh axis runs over, the one named last changes fastest.
Arguments:
- block_input: bfloat16 [2, 16384, 768], P(None, ('dp', 'mod')), may hold values from -6 to 6
- grad_out: bfloat16 [2, 16384, 768], P(None, ('dp', 'mod')), may hold values from -6 to 6
- long_flag: int32 [2, 32], P(None, ('dp', 'mod')), may hold values from 0 to 1, as said below
- valid_mask: int32 [2, 16384], P(None, ('dp', 'mod')), may hold values from 0 to 1, as said below
- labels: int32 [2, 128], P(None, ('dp', 'mod')), may hold values from 0 to 999
- tsteps: int32 [2, 128], P(None, ('dp', 'mod')), may hold values from 0 to 999
- time_table: bfloat16 [1000, 768], replicated, may hold values from -5 to 5
- class_table: bfloat16 [1000, 768], replicated, may hold values from -5 to 5
- w_ada: bfloat16 [768, 4608], P(None, 'mod'), may hold values from -0.21875 to 0.21875
- b_ada: bfloat16 [4608], P('mod'), may hold values from -3 to 3
- w_qkv: bfloat16 [768, 2304], P('mod'), may hold values from -0.21875 to 0.21875
- qv_bias: bfloat16 [1536], P('mod'), may hold values from -2 to 2
- w_proj: bfloat16 [768, 768], P('mod'), may hold values from -0.875 to 0.875
- proj_bias: bfloat16 [768], P('mod'), may hold values from -2 to 2
- w_fc1: bfloat16 [768, 3072], P('mod'), may hold values from -0.21875 to 0.21875
- fc1_bias: bfloat16 [3072], P('mod'), may hold values from -2 to 2
- w_fc2: bfloat16 [3072, 768], P('mod'), may hold values from -0.109375 to 0.109375
- fc2_bias: bfloat16 [768], P('mod'), may hold values from -2 to 2
- rel_table: bfloat16 [12, 1023], P('mod'), may hold values from -5 to 5
Outputs:
- block_output: bfloat16 [2, 16384, 768], P(None, ('dp', 'mod'))
- grad_input: bfloat16 [2, 16384, 768], P(None, ('dp', 'mod'))
- grad_time_table: float32 [1000, 768], P('mod')
- grad_class_table: float32 [1000, 768], P('mod')
- grad_w_ada: float32 [768, 4608], P(None, 'mod')
- grad_b_ada: float32 [4608], P('mod')
- grad_w_qkv: float32 [768, 2304], P('mod')
- grad_qv_bias: float32 [1536], P('mod')
- grad_w_proj: float32 [768, 768], P('mod')
- grad_proj_bias: float32 [768], P('mod')
- grad_w_fc1: float32 [768, 3072], P('mod')
- grad_fc1_bias: float32 [3072], P('mod')
- grad_w_fc2: float32 [3072, 768], P('mod')
- grad_fc2_bias: float32 [768], P('mod')
- grad_rel_table: float32 [12, 1023], P('mod')
The draws below stay inside these ranges and needn't reach their ends.
Inputs may be any that keep to these rules, and one draw needn't show every extreme that they name: `long_flag`: 1 marks a buffer holding one sample of 512 tokens; 0 a buffer holding 4 samples of 128 tokens. `valid_mask`: each segment of 128 tokens of a buffer is valid or padding as a whole; the first segment of every buffer is valid, and all of a buffer with long_flag 1 is valid.
All inputs are finite; a program needn't handle non-finite values.
Results may differ from the reference program's by a relative error of at most 0.015.
Values may be sent and summed in bfloat16 or wider, within the bound.
No kernel may reach another device: no remote copies, remote signals or barrier semaphores. Data moves between devices by JAX's collectives and lax.ppermute only.
A program may use at most 256 MiB of HBM per device.

```python
import jax
import jax.numpy as jnp
from jax import lax

D = 768
H = 12
HD = 64
FF = 3072
NCLS = 1000
NT = 1000
LLONG = 512
LSHORT = 128
MICRO = 2
SEGS = 4
N_DP = 8
N_MOD = 4


def layout_draw(key):
    buffers = N_DP * N_MOD
    long_key = jax.random.fold_in(key, 11)
    segment_key = jax.random.fold_in(key, 12)
    longs = jax.random.randint(long_key, (MICRO, buffers), 0, 2).astype(jnp.int32)
    keeps = jax.random.randint(segment_key, (MICRO, buffers, LLONG // LSHORT), 0, 4) > 0
    first = jnp.arange(LLONG // LSHORT)[None, None, :] == 0
    segment_ok = keeps | first | (longs[:, :, None] > 0)
    tokens_ok = jnp.repeat(segment_ok, LSHORT, axis=2).astype(jnp.int32)
    return (longs, tokens_ok.reshape(MICRO, buffers * LLONG))


def draw_long_flag(key, part):
    return layout_draw(key)[0]


def draw_valid_mask(key, part):
    return layout_draw(key)[1]


def with_ends(entries, rng, least, high):
    dims = entries.shape
    place = [jax.random.randint(jax.random.fold_in(rng, axis), (), 0, dims[axis]) for axis in range(len(dims))]
    entries = entries.at[tuple(place)].set(least)
    longest = dims.index(max(dims))
    place[longest] = (place[longest] + 1) % dims[longest]
    return entries.at[tuple(place)].set(high)


def block_levels(key, dims, shards, low, high):
    def one(dim, blocks):
        heights = jax.random.uniform(jax.random.fold_in(jax.random.fold_in(key, 6), dim), (blocks,), jnp.float32, low / len(shards), high / len(shards))
        return jnp.repeat(jnp.exp(heights), dims[dim] // blocks).reshape((-1,) + (1,) * (len(dims) - dim - 1))

    level = one(*shards[0])
    for cut in shards[1:]:
        level = level * one(*cut)
    return level


def noise(own_key, dims, width, limit, cuts=(), held_as=jnp.bfloat16):
    values = width * jax.random.normal(own_key, dims, jnp.float32)
    if cuts:
        values = values * block_levels(own_key, dims, cuts, -0.22, 0.18)
    return jnp.clip(values, -limit, limit).astype(held_as)


def setup_inputs(seed: int = 0) -> dict:
    key_list = jax.random.split(jax.random.key(seed), 20)
    block_input = noise(key_list[0], (MICRO, N_DP * N_MOD * LLONG, D), 1.0, 6.0, ((1, 32),))
    grad_out = noise(key_list[1], (MICRO, N_DP * N_MOD * LLONG, D), 1.0, 6.0, ((1, 32),))
    long_flag = draw_long_flag(jax.random.fold_in(key_list[19], 71), 0)
    valid_mask = draw_valid_mask(jax.random.fold_in(key_list[19], 71), 0)
    labels = with_ends(jax.random.randint(key_list[4], (MICRO, N_DP * N_MOD * SEGS), 0, NCLS), jax.random.fold_in(key_list[4], 1), 0, NCLS - 1).astype(jnp.int32)
    tsteps = with_ends(jax.random.randint(key_list[5], (MICRO, N_DP * N_MOD * SEGS), 0, NT), jax.random.fold_in(key_list[5], 1), 0, NT - 1).astype(jnp.int32)
    time_table = noise(key_list[6], (NT, D), 0.7, 5.0)
    class_table = noise(key_list[7], (NCLS, D), 0.7, 5.0)
    w_ada = noise(key_list[8], (D, 6 * D), D ** -0.5, 0.21875, ((1, 4),))
    b_ada = noise(key_list[9], (6 * D,), 0.5, 3.0, ((0, 4),))
    w_qkv = noise(key_list[10], (D, 3 * D), D ** -0.5, 0.21875, ((0, 4),))
    qv_bias = noise(key_list[11], (2 * D,), 0.3, 2.0, ((0, 4),))
    w_proj = noise(key_list[12], (D, D), (D // 16) ** -0.5, 0.875, ((0, 4),))
    proj_bias = noise(key_list[13], (D,), 0.3, 2.0, ((0, 4),))
    w_fc1 = noise(key_list[14], (D, FF), D ** -0.5, 0.21875, ((0, 4),))
    fc1_bias = noise(key_list[15], (FF,), 0.3, 2.0, ((0, 4),))
    w_fc2 = noise(key_list[16], (FF, D), FF ** -0.5, 0.109375, ((0, 4),))
    fc2_bias = noise(key_list[17], (D,), 0.3, 2.0, ((0, 4),))
    rel_table = noise(key_list[18], (H, 2 * LLONG - 1), 1.0, 5.0, ((0, 4),))
    return dict(block_input=block_input, grad_out=grad_out, long_flag=long_flag, valid_mask=valid_mask, labels=labels, tsteps=tsteps, time_table=time_table, class_table=class_table, w_ada=w_ada, b_ada=b_ada, w_qkv=w_qkv, qv_bias=qv_bias, w_proj=w_proj, proj_bias=proj_bias, w_fc1=w_fc1, fc1_bias=fc1_bias, w_fc2=w_fc2, fc2_bias=fc2_bias, rel_table=rel_table)


@jax.custom_vjp
def low(v):
    return lax.optimization_barrier(v.astype(jnp.bfloat16)).astype(jnp.float32)

@jax.custom_vjp
def low_back(v):
    return v

def low_keep(v):
    return (low(v), None)

def low_pass(kept, grad):
    return (grad,)

def back_keep(v):
    return (v, None)

def back_low(kept, grad):
    return (low(grad),)
low.defvjp(low_keep, low_pass)
low_back.defvjp(back_keep, back_low)
HIGH = lax.Precision.HIGHEST

def layer_norm(values):
    centred = values - lax.optimization_barrier(jnp.mean(values, axis=1, keepdims=True))
    return centred * lax.rsqrt(lax.optimization_barrier(jnp.mean(centred * centred, axis=1, keepdims=True)) + 1e-06)

def buffer_block(params, inputs):
    w_qkv, qv_bias, w_proj, proj_bias, w_fc1, fc1_bias, w_fc2, fc2_bias, rel_table = params
    tokens, modulation, long_one, valid_one = inputs
    slots = jnp.arange(SEGS)
    owner = jnp.where(long_one > 0, 0, slots)
    select = (owner[:, None] == slots[None, :]).astype(jnp.float32)
    mod_seg = jnp.dot(select, modulation, precision=HIGH)
    mod_tok = jnp.repeat(mod_seg, LSHORT, axis=0)
    shift1, scale1, gate1, shift2, scale2, gate2 = jnp.split(mod_tok, 6, axis=1)
    valid = valid_one.astype(jnp.float32)[:, None]
    norm1 = layer_norm(tokens)
    entry = low(norm1 * (1.0 + scale1) + shift1)
    full_bias = jnp.concatenate([qv_bias[:D], jnp.zeros((D,), jnp.float32), qv_bias[D:]])
    qkv = low(low_back(jnp.dot(entry, w_qkv, precision=HIGH) + full_bias))
    query = qkv[:, :D].reshape(LLONG, H, HD)
    keys = qkv[:, D:2 * D].reshape(LLONG, H, HD)
    values = qkv[:, 2 * D:].reshape(LLONG, H, HD)
    positions = jnp.arange(LLONG)
    offsets = (positions[None, :] - positions[:, None] + LLONG - 1).astype(jnp.int32)
    scores = jnp.einsum('qhd,khd->hqk', query, keys, precision=HIGH) * HD ** (-0.5) + rel_table[:, offsets]
    scores = low_back(scores)
    sample = jnp.where(long_one > 0, 0, positions // LSHORT)
    allowed = (sample[:, None] == sample[None, :]) & (valid_one[None, :] > 0)
    scores = jnp.where(allowed[None], scores, -1e+30)
    probs = jax.nn.softmax(scores, axis=-1)
    attended = jnp.einsum('hqk,khd->qhd', low(probs), values, precision=HIGH).reshape(LLONG, D)
    attended = low(low_back(attended))
    attn = low_back(jnp.dot(attended, w_proj, precision=HIGH) + proj_bias)
    hidden = tokens + valid * gate1 * attn
    norm2 = layer_norm(hidden)
    m_in = low(norm2 * (1.0 + scale2) + shift2)
    upper = low_back(jnp.dot(m_in, w_fc1, precision=HIGH) + fc1_bias)
    gelu_low = low(jax.nn.gelu(upper, approximate=True))
    mlp = low_back(jnp.dot(gelu_low, w_fc2, precision=HIGH) + fc2_bias)
    return hidden + valid * gate2 * mlp

def forward(tokens, params, labels, tsteps, long_flag, valid_mask):
    time_table, class_table, w_ada, b_ada = params[:4]
    block_params = params[4:]
    cond = time_table[tsteps] + class_table[labels]
    act = low(jax.nn.silu(cond))
    modulation = jnp.einsum('bsd,de->bse', act, w_ada, precision=HIGH) + b_ada
    step_fn = jax.checkpoint(lambda inputs: buffer_block(block_params, inputs))
    return lax.map(step_fn, (tokens, modulation, long_flag, valid_mask))

def reference(block_input, grad_out, long_flag, valid_mask, labels, tsteps, time_table, class_table, w_ada, b_ada, w_qkv, qv_bias, w_proj, proj_bias, w_fc1, fc1_bias, w_fc2, fc2_bias, rel_table):
    buffers = MICRO * N_DP * N_MOD
    tokens = block_input.astype(jnp.float32).reshape(buffers, LLONG, D)
    cotangent = grad_out.astype(jnp.float32).reshape(buffers, LLONG, D)
    long_all = long_flag.reshape(buffers)
    valid_all = valid_mask.reshape(buffers, LLONG)
    label_all = labels.reshape(buffers, SEGS)
    time_all = tsteps.reshape(buffers, SEGS)
    params = tuple((p.astype(jnp.float32) for p in (time_table, class_table, w_ada, b_ada, w_qkv, qv_bias, w_proj, proj_bias, w_fc1, fc1_bias, w_fc2, fc2_bias, rel_table)))

    def run(tokens_in, params_in):
        return forward(tokens_in, params_in, label_all, time_all, long_all, valid_all)
    result, pull = jax.vjp(run, tokens, params)
    grad_tokens, grads = pull(cotangent)
    return (result.reshape(block_input.shape).astype(jnp.bfloat16), grad_tokens.reshape(block_input.shape).astype(jnp.bfloat16), grads[0], grads[1], grads[2], grads[3], grads[4], grads[5], grads[6], grads[7], grads[8], grads[9], grads[10], grads[11], grads[12])
```

```python
from functools import partial
import jax
import jax.numpy as jnp
from jax import lax
from jax.experimental import pallas as pl
from jax.experimental.pallas import tpu as pltpu
from jax.sharding import PartitionSpec as P

f32 = jnp.float32
bf16 = jnp.bfloat16
D = 768
H = 12
HD = 64
FF = 3072
L = 512
SEG = 128
NSEG = 4
MICRO = 2
T = MICRO * L
HALF = 384
FH = 1536
VMEM_LIMIT = 56 * 1024 * 1024


def params(*sem):
    return pltpu.CompilerParams(vmem_limit_bytes=VMEM_LIMIT, dimension_semantics=sem)


def dot(a, b, ca=1, cb=0):
    return lax.dot_general(a, b, (((ca,), (cb,)), ((), ())), preferred_element_type=f32)


def norm_of(values):
    centred = values - jnp.mean(values, axis=1, keepdims=True)
    inverse = lax.rsqrt(jnp.mean(centred * centred, axis=1, keepdims=True) + 1e-6)
    return centred * inverse, inverse


def norm_back(grad, normed, inverse):
    return inverse * (
        grad
        - jnp.mean(grad, axis=1, keepdims=True)
        - normed * jnp.mean(grad * normed, axis=1, keepdims=True)
    )


def qkv_first_body(x_ref, mod_ref, w_ref, b_ref, a_ref, qkv_ref):
    for s in range(NSEG):
        rows = pl.ds(s * SEG, SEG)
        norm, _ = norm_of(x_ref[rows, :].astype(f32))
        a_ref[rows, :] = (norm * (1.0 + mod_ref[s, 1:2, :]) + mod_ref[s, 0:1, :]).astype(bf16)
    qkv_ref[...] = (dot(a_ref[...], w_ref[...]) + b_ref[...]).astype(bf16)


def qkv_first(x, mods, w, b):
    return pl.pallas_call(
        qkv_first_body,
        grid=(MICRO,),
        in_specs=[
            pl.BlockSpec((L, D), lambda i: (i, 0)),
            pl.BlockSpec((NSEG, 6, D), lambda i: (i, 0, 0)),
            pl.BlockSpec((D, 3 * HALF), lambda i: (0, 0)),
            pl.BlockSpec((1, 3 * HALF), lambda i: (0, 0)),
        ],
        out_specs=[
            pl.BlockSpec((L, D), lambda i: (i, 0)),
            pl.BlockSpec((L, 3 * HALF), lambda i: (i, 0)),
        ],
        out_shape=[
            jax.ShapeDtypeStruct((T, D), bf16),
            jax.ShapeDtypeStruct((T, 3 * HALF), bf16),
        ],
        compiler_params=params("arbitrary"),
        cost_estimate=pl.CostEstimate(flops=2 * T * D * 3 * HALF, bytes_accessed=8_000_000, transcendentals=0),
        name="qkv_first",
    )(x, mods, w, b)


def qkv_second_body(a_ref, w_ref, b_ref, qkv_ref):
    qkv_ref[...] = (dot(a_ref[...], w_ref[...]) + b_ref[...]).astype(bf16)


def qkv_second(a, w, b):
    return pl.pallas_call(
        qkv_second_body,
        grid=(MICRO,),
        in_specs=[
            pl.BlockSpec((L, D), lambda i: (i, 0)),
            pl.BlockSpec((D, 3 * HALF), lambda i: (0, 0)),
            pl.BlockSpec((1, 3 * HALF), lambda i: (0, 0)),
        ],
        out_specs=pl.BlockSpec((L, 3 * HALF), lambda i: (i, 0)),
        out_shape=jax.ShapeDtypeStruct((T, 3 * HALF), bf16),
        compiler_params=params("arbitrary"),
        cost_estimate=pl.CostEstimate(flops=2 * T * D * 3 * HALF, bytes_accessed=6_000_000, transcendentals=0),
        name="qkv_second",
    )(a, w, b)


def attend_body(long_ref, valid_ref, q_ref, k_ref, v_ref, t_ref, o_ref, p_ref, bias_ref):
    b = pl.program_id(1)

    @pl.when(b == 0)
    def _():
        for h in range(2):
            for d in range(7):
                row = jnp.broadcast_to(t_ref[h, d : d + 1, :], (SEG, 2 * SEG))
                bias_ref[h, d] = pltpu.roll(row, SEG + 1, 1, stride=1, stride_axis=0)[:, :SEG]

    is_long = long_ref[b]
    lane = lax.broadcasted_iota(jnp.int32, (L, 2 * HD), 1)
    query = q_ref[...] * jnp.asarray(HD**-0.5, bf16)
    keys = k_ref[...]
    values_t = v_ref[...].T
    outs = []
    for h in range(2):
        mine = (lane < HD) if h == 0 else (lane >= HD)
        key_h = jnp.where(mine, keys, jnp.zeros_like(keys))
        for qb in range(NSEG):
            cols = pl.ds(qb * SEG, SEG)
            scores = dot(key_h, query[qb * SEG : (qb + 1) * SEG, :], 1, 1)
            parts = []
            for kb in range(NSEG):
                open_ = (valid_ref[b, kb] > 0) if kb == qb else ((valid_ref[b, kb] > 0) & (is_long > 0))
                shut = jnp.where(open_, 0.0, -1e30).astype(f32)
                parts.append(scores[kb * SEG : (kb + 1) * SEG, :] + (bias_ref[h, kb - qb + 3] + shut))
            scores = jnp.concatenate(parts, axis=0)
            top = jnp.max(scores, axis=0, keepdims=True)
            expo = jnp.exp(scores - top)
            total = jnp.sum(expo, axis=0, keepdims=True)
            p_ref[0, h, :, cols] = (expo * (1.0 / total)).astype(bf16)
        outs.append(dot(values_t[h * HD : (h + 1) * HD, :], p_ref[0, h]))
    o_ref[...] = jnp.concatenate(outs, axis=0).T.astype(bf16)


def attend(qkv, table, long_flag, valid_seg):
    pairs = 3
    return pl.pallas_call(
        attend_body,
        grid_spec=pltpu.PrefetchScalarGridSpec(
            num_scalar_prefetch=2,
            grid=(pairs, MICRO),
            in_specs=[
                pl.BlockSpec((L, 2 * HD), lambda g, b, *_: (b, g)),
                pl.BlockSpec((L, 2 * HD), lambda g, b, *_: (b, 3 + g)),
                pl.BlockSpec((L, 2 * HD), lambda g, b, *_: (b, 6 + g)),
                pl.BlockSpec((2, 8, 2 * SEG), lambda g, b, *_: (g, 0, 0)),
            ],
            out_specs=[
                pl.BlockSpec((L, 2 * HD), lambda g, b, *_: (b, g)),
                pl.BlockSpec((1, 2, L, L), lambda g, b, *_: (b, g, 0, 0)),
            ],
            scratch_shapes=[pltpu.VMEM((2, 7, SEG, SEG), f32)],
        ),
        out_shape=[
            jax.ShapeDtypeStruct((T, HALF), bf16),
            jax.ShapeDtypeStruct((MICRO, 6, L, L), bf16),
        ],
        compiler_params=params("arbitrary", "arbitrary"),
        cost_estimate=pl.CostEstimate(flops=16_000_000_000, bytes_accessed=10_000_000, transcendentals=0),
        name="attend",
    )(long_flag, valid_seg, qkv, qkv, qkv, table)


def middle_body(half_ref, o1_ref, o2_ref, w_ref, b_ref, x_ref, dy_ref, mod_ref,
                h_ref, m_ref, attn_ref, dmlp_ref, db_ref):
    first = pl.multiple_of(half_ref[0] * HALF, HALF)
    second = pl.multiple_of((1 - half_ref[0]) * HALF, HALF)
    attn = dot(o1_ref[...], w_ref[pl.ds(first, HALF), :]) + dot(o2_ref[...], w_ref[pl.ds(second, HALF), :])
    attn = attn + b_ref[...]
    attn_ref[...] = attn.astype(bf16)
    total = jnp.zeros((1, D), f32)
    for s in range(NSEG):
        rows = pl.ds(s * SEG, SEG)
        hidden = x_ref[rows, :].astype(f32) + mod_ref[s, 2:3, :] * attn[s * SEG : (s + 1) * SEG, :]
        h_ref[rows, :] = hidden
        norm, _ = norm_of(hidden)
        m_ref[rows, :] = (norm * (1.0 + mod_ref[s, 4:5, :]) + mod_ref[s, 3:4, :]).astype(bf16)
        dmlp = (dy_ref[rows, :].astype(f32) * mod_ref[s, 5:6, :]).astype(bf16)
        dmlp_ref[rows, :] = dmlp
        total = total + jnp.sum(dmlp.astype(f32), axis=0, keepdims=True)

    @pl.when(pl.program_id(0) == 0)
    def _():
        db_ref[...] = jnp.zeros_like(db_ref)

    db_ref[0:1, :] += total


def middle(half, o1, o2, w, b, x, dy, mods):
    row = lambda i, *_: (i, 0)
    zero = lambda i, *_: (0, 0)
    return pl.pallas_call(
        middle_body,
        grid_spec=pltpu.PrefetchScalarGridSpec(
            num_scalar_prefetch=1,
            grid=(MICRO,),
            in_specs=[
                pl.BlockSpec((L, HALF), row),
                pl.BlockSpec((L, HALF), row),
                pl.BlockSpec((D, D), zero),
                pl.BlockSpec((1, D), zero),
                pl.BlockSpec((L, D), row),
                pl.BlockSpec((L, D), row),
                pl.BlockSpec((NSEG, 6, D), lambda i, *_: (i, 0, 0)),
            ],
            out_specs=[
                pl.BlockSpec((L, D), row),
                pl.BlockSpec((L, D), row),
                pl.BlockSpec((L, D), row),
                pl.BlockSpec((L, D), row),
                pl.BlockSpec((8, D), zero),
            ],
        ),
        out_shape=[
            jax.ShapeDtypeStruct((T, D), f32),
            jax.ShapeDtypeStruct((T, D), bf16),
            jax.ShapeDtypeStruct((T, D), bf16),
            jax.ShapeDtypeStruct((T, D), bf16),
            jax.ShapeDtypeStruct((8, D), f32),
        ],
        compiler_params=params("arbitrary"),
        cost_estimate=pl.CostEstimate(flops=4 * T * D * D, bytes_accessed=16_000_000, transcendentals=0),
        name="middle",
    )(half, o1, o2, w, b, x, dy, mods)


FB = 512


def mlp_body(has_acc, m_ref, dmlp_ref, w1_ref, w2_ref, b_ref, *refs):
    if has_acc:
        acc_o, acc_d, out_o, out_d, dw1_ref, dw2_ref, db_ref, g_s, du_s = refs
    else:
        out_o, out_d, dw1_ref, dw2_ref, db_ref, g_s, du_s = refs
    f = pl.program_id(0)
    w1 = w1_ref[...]
    w2 = w2_ref[...]
    bias = b_ref[0:1, :]
    chunk = 256
    total = jnp.zeros((1, FB), f32)
    c0 = (2.0 / jnp.pi) ** 0.5
    for r in range(T // chunk):
        rows = pl.ds(r * chunk, chunk)
        u = dot(m_ref[rows, :], w1) + bias
        dg = dot(dmlp_ref[rows, :], w2, 1, 1)
        u2 = u * u
        th = jnp.tanh(u * (c0 + (c0 * 0.044715) * u2))
        half = 0.5 + 0.5 * th
        g_s[rows, :] = (u * half).astype(bf16)
        slope = half + u * (0.5 - 0.5 * th * th) * (c0 + (3.0 * c0 * 0.044715) * u2)
        du = (dg * slope).astype(bf16)
        du_s[rows, :] = du
        total = total + jnp.sum(du.astype(f32), axis=0, keepdims=True)
    db_ref[0:1, :] = total

    @pl.when(f == 0)
    def _():
        if has_acc:
            out_o[...] = acc_o[...] + dot(g_s[...], w2)
            out_d[...] = acc_d[...] + dot(du_s[...], w1, 1, 1)
        else:
            out_o[...] = dot(g_s[...], w2)
            out_d[...] = dot(du_s[...], w1, 1, 1)

    @pl.when(f > 0)
    def _():
        out_o[...] += dot(g_s[...], w2)
        out_d[...] += dot(du_s[...], w1, 1, 1)

    dw2_ref[...] = dot(g_s[...], dmlp_ref[...], 0, 0).astype(bf16)
    dw1_ref[...] = dot(m_ref[...], du_s[...], 0, 0).astype(bf16)


def mlp(m_in, dmlp, w1, w2, b1, acc=None):
    zero = lambda f: (0, 0)
    col = lambda f: (0, f)
    once = pl.Buffered(1)
    specs = [
        pl.BlockSpec((T, D), zero, pipeline_mode=once),
        pl.BlockSpec((T, D), zero, pipeline_mode=once),
        pl.BlockSpec((D, FB), col),
        pl.BlockSpec((FB, D), lambda f: (f, 0)),
        pl.BlockSpec((1, FB), col),
    ]
    args = [m_in, dmlp, w1, w2, b1]
    alias = {}
    if acc is not None:
        specs += [pl.BlockSpec((T, D), zero, pipeline_mode=once)] * 2
        args += list(acc)
    return pl.pallas_call(
        partial(mlp_body, acc is not None),
        grid=(FH // FB,),
        in_specs=specs,
        out_specs=[
            pl.BlockSpec((T, D), zero),
            pl.BlockSpec((T, D), zero),
            pl.BlockSpec((D, FB), col),
            pl.BlockSpec((FB, D), lambda f: (f, 0)),
            pl.BlockSpec((8, FB), col),
        ],
        out_shape=[
            jax.ShapeDtypeStruct((T, D), f32),
            jax.ShapeDtypeStruct((T, D), f32),
            jax.ShapeDtypeStruct((D, FH), bf16),
            jax.ShapeDtypeStruct((FH, D), bf16),
            jax.ShapeDtypeStruct((8, FH), f32),
        ],
        scratch_shapes=[pltpu.VMEM((T, FB), bf16), pltpu.VMEM((T, FB), bf16)],
        compiler_params=params("arbitrary"),
        cost_estimate=pl.CostEstimate(flops=12 * T * D * FH, bytes_accessed=24_000_000, transcendentals=0),
        name="mlp",
    )(*args)


def back_middle_body(half_ref, h_ref, dy_ref, mlp_ref, b2_ref, dm_ref, attn_ref, mod_ref, o1_ref, o2_ref, w_ref,
                     y_ref, dh_ref, do1_ref, do2_ref, dws_ref, dwk_ref, dmod_ref, db_ref, dattn_s, dw_s):
    i = pl.program_id(0)
    first = pl.multiple_of(half_ref[0] * HALF, HALF)
    second = pl.multiple_of((1 - half_ref[0]) * HALF, HALF)
    total = jnp.zeros((1, D), f32)
    for s in range(NSEG):
        rows = pl.ds(s * SEG, SEG)
        hidden = h_ref[rows, :]
        dy = dy_ref[rows, :].astype(f32)
        ff = mlp_ref[rows, :] + b2_ref[...]
        y_ref[rows, :] = (hidden + mod_ref[s, 5:6, :] * ff).astype(bf16)
        dmod_ref[s, 5:6, :] = jnp.sum(dy * ff, axis=0, keepdims=True)
        norm, inverse = norm_of(hidden)
        dm = dm_ref[rows, :]
        dmod_ref[s, 3:4, :] = jnp.sum(dm, axis=0, keepdims=True)
        dmod_ref[s, 4:5, :] = jnp.sum(dm * norm, axis=0, keepdims=True)
        dh = dy + norm_back(dm * (1.0 + mod_ref[s, 4:5, :]), norm, inverse)
        dh_ref[rows, :] = dh
        dmod_ref[s, 2:3, :] = jnp.sum(dh * attn_ref[rows, :].astype(f32), axis=0, keepdims=True)
        dattn = (dh * mod_ref[s, 2:3, :]).astype(bf16)
        dattn_s[rows, :] = dattn
        total = total + jnp.sum(dattn.astype(f32), axis=0, keepdims=True)
    dmod_ref[:, 0:2, :] = jnp.zeros((NSEG, 2, D), f32)
    dattn = dattn_s[...]
    do1_ref[...] = dot(dattn, w_ref[pl.ds(first, HALF), :], 1, 1).astype(bf16)
    do2_ref[...] = dot(dattn, w_ref[pl.ds(second, HALF), :], 1, 1).astype(bf16)

    @pl.when(i == 0)
    def _():
        db_ref[...] = jnp.zeros_like(db_ref)
        dw_s[...] = jnp.zeros_like(dw_s)

    db_ref[0:1, :] += total
    dw_s[pl.ds(first, HALF), :] += dot(o1_ref[...], dattn, 0, 0)
    dw_s[pl.ds(second, HALF), :] += dot(o2_ref[...], dattn, 0, 0)

    @pl.when(i == MICRO - 1)
    def _():
        dws_ref[...] = dw_s[:, pl.ds(first, HALF)].astype(bf16)
        dwk_ref[...] = dw_s[:, pl.ds(second, HALF)].astype(bf16)


def back_middle(half, h, dy, ff, b2, dm, attn, mods, o1, o2, w):
    row = lambda i, *_: (i, 0)
    zero = lambda i, *_: (0, 0)
    full = pl.BlockSpec((L, D), row)
    part = pl.BlockSpec((L, HALF), row)
    modspec = pl.BlockSpec((NSEG, 6, D), lambda i, *_: (i, 0, 0))
    return pl.pallas_call(
        back_middle_body,
        grid_spec=pltpu.PrefetchScalarGridSpec(
            num_scalar_prefetch=1,
            grid=(MICRO,),
            in_specs=[full, full, full, pl.BlockSpec((1, D), zero), full, full, modspec, part, part,
                      pl.BlockSpec((D, D), zero)],
            out_specs=[full, full, part, part, pl.BlockSpec((D, HALF), zero), pl.BlockSpec((D, HALF), zero),
                       modspec, pl.BlockSpec((8, D), zero)],
            scratch_shapes=[pltpu.VMEM((L, D), bf16), pltpu.VMEM((D, D), f32)],
        ),
        out_shape=[
            jax.ShapeDtypeStruct((T, D), bf16),
            jax.ShapeDtypeStruct((T, D), f32),
            jax.ShapeDtypeStruct((T, HALF), bf16),
            jax.ShapeDtypeStruct((T, HALF), bf16),
            jax.ShapeDtypeStruct((D, HALF), bf16),
            jax.ShapeDtypeStruct((D, HALF), bf16),
            jax.ShapeDtypeStruct((MICRO * NSEG, 6, D), f32),
            jax.ShapeDtypeStruct((8, D), f32),
        ],
        compiler_params=params("arbitrary"),
        cost_estimate=pl.CostEstimate(flops=8 * T * D * D, bytes_accessed=24_000_000, transcendentals=0),
        name="back_middle",
    )(half, h, dy, ff, b2, dm, attn, mods, o1, o2, w)


def attend_back_body(q_ref, k_ref, v_ref, p_ref, do_ref, o_ref, dq_ref, dk_ref, dv_ref, dt_ref, db_ref, acc_ref, ds_s):
    b = pl.program_id(1)

    @pl.when(b == 0)
    def _():
        acc_ref[...] = jnp.zeros_like(acc_ref)
        db_ref[...] = jnp.zeros_like(db_ref)

    lane = lax.broadcasted_iota(jnp.int32, (L, 2 * HD), 1)
    query = q_ref[...]
    keys_t = k_ref[...].T
    values = v_ref[...]
    dout = do_ref[...]
    prod = (dout.astype(f32) * o_ref[...].astype(f32)).T
    dqs, dks, dvs = [], [], []
    for h in range(2):
        mine = (lane < HD) if h == 0 else (lane >= HD)
        value_h = jnp.where(mine, values, jnp.zeros_like(values))
        delta = jnp.sum(prod[h * HD : (h + 1) * HD, :], axis=0, keepdims=True)
        for qb in range(NSEG):
            cols = slice(qb * SEG, (qb + 1) * SEG)
            dp = dot(value_h, dout[cols, :], 1, 1)
            ds = (p_ref[0, h, :, cols].astype(f32) * (dp - delta[:, cols])).astype(bf16)
            ds_s[h, :, cols] = ds
            for kb in range(NSEG):
                acc_ref[h, kb - qb + 3] += ds[kb * SEG : (kb + 1) * SEG, :].astype(f32)
        dvs.append(dot(p_ref[0, h], dout))
        dks.append(dot(ds_s[h], query))
        dqs.append(dot(keys_t[h * HD : (h + 1) * HD, :], ds_s[h]))
    low = lane < HD
    scale = HD**-0.5
    dq = (jnp.concatenate(dqs, axis=0).T * scale).astype(bf16)
    dk = (jnp.where(low, dks[0], dks[1]) * scale).astype(bf16)
    dv = jnp.where(low, dvs[0], dvs[1]).astype(bf16)
    dq_ref[...] = dq
    dk_ref[...] = dk
    dv_ref[...] = dv
    db_ref[0:1, :] += jnp.sum(dq.astype(f32), axis=0, keepdims=True)
    db_ref[1:2, :] += jnp.sum(dv.astype(f32), axis=0, keepdims=True)

    @pl.when(b == MICRO - 1)
    def _():
        for h in range(2):
            for d in range(7):
                wide = jnp.concatenate([acc_ref[h, d], jnp.zeros((SEG, SEG), f32)], axis=1)
                rows = SEG
                while rows > 1:
                    rows //= 2
                    wide = pltpu.roll(wide[:rows], rows, 1) + wide[rows:]
                dt_ref[h, d : d + 1, :] = wide
            dt_ref[h, 7:8, :] = jnp.zeros((1, 2 * SEG), f32)


def attend_back(qkv, p, dout, out):
    col = lambda g, b: (b, g)
    part = pl.BlockSpec((L, 2 * HD), col)
    return pl.pallas_call(
        attend_back_body,
        grid=(3, MICRO),
        in_specs=[
            part,
            pl.BlockSpec((L, 2 * HD), lambda g, b: (b, 3 + g)),
            pl.BlockSpec((L, 2 * HD), lambda g, b: (b, 6 + g)),
            pl.BlockSpec((1, 2, L, L), lambda g, b: (b, g, 0, 0)),
            part,
            part,
        ],
        out_specs=[part, part, part, pl.BlockSpec((2, 8, 2 * SEG), lambda g, b: (g, 0, 0)),
                   pl.BlockSpec((8, 2 * HD), lambda g, b: (0, g))],
        out_shape=[jax.ShapeDtypeStruct((T, HALF), bf16)] * 3
        + [jax.ShapeDtypeStruct((6, 8, 2 * SEG), f32), jax.ShapeDtypeStruct((8, HALF), f32)],
        scratch_shapes=[pltpu.VMEM((2, 7, SEG, SEG), f32), pltpu.VMEM((2, L, L), bf16)],
        compiler_params=params("arbitrary", "arbitrary"),
        cost_estimate=pl.CostEstimate(flops=24_000_000_000, bytes_accessed=12_000_000, transcendentals=0),
        name="attend_back",
    )(qkv, qkv, qkv, p, dout, out)


def qkv_weight_body(a_ref, dq_ref, dk_ref, dv_ref, out_ref):
    a = a_ref[...]
    out_ref[:, 0:HALF] = dot(a, dq_ref[...], 0, 0).astype(bf16)
    out_ref[:, HALF : 2 * HALF] = dot(a, dk_ref[...], 0, 0).astype(bf16)
    out_ref[:, 2 * HALF : 3 * HALF] = dot(a, dv_ref[...], 0, 0).astype(bf16)


def qkv_weight(a, dq, dk, dv):
    return pl.pallas_call(
        qkv_weight_body,
        out_shape=jax.ShapeDtypeStruct((D, 3 * HALF), bf16),
        compiler_params=params(),
        cost_estimate=pl.CostEstimate(flops=2 * T * D * 3 * HALF, bytes_accessed=6_000_000, transcendentals=0),
        name="qkv_weight",
    )(a, dq, dk, dv)


def back_entry_body(dq1, dk1, dv1, dq2, dk2, dv2, w1_ref, w2_ref, x_ref, dh_ref, mod_ref, dx_ref, dmod_ref):
    da = dot(dq1[...], w1_ref[:, 0:HALF], 1, 1)
    da += dot(dk1[...], w1_ref[:, HALF : 2 * HALF], 1, 1)
    da += dot(dv1[...], w1_ref[:, 2 * HALF : 3 * HALF], 1, 1)
    da += dot(dq2[...], w2_ref[:, 0:HALF], 1, 1)
    da += dot(dk2[...], w2_ref[:, HALF : 2 * HALF], 1, 1)
    da += dot(dv2[...], w2_ref[:, 2 * HALF : 3 * HALF], 1, 1)
    for s in range(NSEG):
        rows = pl.ds(s * SEG, SEG)
        piece = da[s * SEG : (s + 1) * SEG, :]
        norm, inverse = norm_of(x_ref[rows, :].astype(f32))
        dmod_ref[s, 0:1, :] = jnp.sum(piece, axis=0, keepdims=True)
        dmod_ref[s, 1:2, :] = jnp.sum(piece * norm, axis=0, keepdims=True)
        dx_ref[rows, :] = (
            dh_ref[rows, :] + norm_back(piece * (1.0 + mod_ref[s, 1:2, :]), norm, inverse)
        ).astype(bf16)


def back_entry(parts, w1, w2, x, dh, mods):
    row = lambda i: (i, 0)
    zero = lambda i: (0, 0)
    full = pl.BlockSpec((L, D), row)
    part = pl.BlockSpec((L, HALF), row)
    return pl.pallas_call(
        back_entry_body,
        grid=(MICRO,),
        in_specs=[part] * 6 + [pl.BlockSpec((D, 3 * HALF), zero)] * 2 + [full, full, pl.BlockSpec((NSEG, 6, D), lambda i: (i, 0, 0))],
        out_specs=[full, pl.BlockSpec((NSEG, 2, D), lambda i: (i, 0, 0))],
        out_shape=[jax.ShapeDtypeStruct((T, D), bf16), jax.ShapeDtypeStruct((MICRO * NSEG, 2, D), f32)],
        compiler_params=params("arbitrary"),
        cost_estimate=pl.CostEstimate(flops=4 * T * D * 3 * HALF, bytes_accessed=16_000_000, transcendentals=0),
        name="back_entry",
    )(*parts, w1, w2, x, dh, mods)


def place_body(order, idx_ref, own_ref, near_ref, far_ref, out_ref, sems):
    count = near_ref.shape[1] + 1
    rows, piece = own_ref.shape[0], near_ref.shape[2]
    me, spot = idx_ref[0], idx_ref[1]
    copies = [pltpu.make_async_copy(own_ref, out_ref.at[pl.ds(pl.multiple_of(me * rows, rows), rows), :], sems.at[0])]
    first, second = order
    for k in range(1, count):
        base = lax.rem(me + count - k, count) * rows
        for n, (ref, slot, other) in enumerate(
            ((near_ref, 0, 0), (near_ref, 1, first), (far_ref, 0, second), (far_ref, 1, first + second))
        ):
            start = pl.multiple_of(base + lax.bitwise_xor(spot, other) * piece, 16)
            copies.append(
                pltpu.make_async_copy(
                    ref.at[slot, k - 1], out_ref.at[pl.ds(start, piece), :], sems.at[1 + 4 * (k - 1) + n]
                )
            )
    for copy in copies:
        copy.start()
    for copy in copies:
        copy.wait()


def place(idx, own, near, far, order):
    count = near.shape[1] + 1
    rows, width = own.shape
    anywhere = pl.BlockSpec(memory_space=pl.ANY)
    return pl.pallas_call(
        partial(place_body, order),
        in_specs=[pl.BlockSpec(memory_space=pltpu.SMEM), anywhere, anywhere, anywhere],
        out_specs=anywhere,
        out_shape=jax.ShapeDtypeStruct((count * rows, width), own.dtype),
        scratch_shapes=[pltpu.SemaphoreType.DMA((1 + 4 * (count - 1),))],
        compiler_params=pltpu.CompilerParams(vmem_limit_bytes=8 * 1024 * 1024),
        cost_estimate=pl.CostEstimate(flops=0, bytes_accessed=4 * count * rows * width, transcendentals=0),
        name="place",
    )(idx, own, near, far)


def finish_ff_body(idx_ref, mine_ref, peer_ref, fc1_ref, fc2_ref):
    spot, core = idx_ref[1], idx_ref[2]
    for source, half in ((mine_ref, core), (peer_ref, 1 - core)):
        for j in range(4):
            place_at = lax.bitwise_xor(spot, j)
            low, high = lax.rem(place_at, 2), lax.div(place_at, 2)
            row = pl.multiple_of((2 * low + high) * 48, 16)
            for z in range(4):
                source_rows = pl.ds(48 * (z // 2), 48)
                block = source[j, source_rows, (z % 2) * HALF : (z % 2 + 1) * HALF]
                column = pl.multiple_of((2 * z + half) * HALF, 128)
                fc1_ref[pl.ds(row, 48), pl.ds(column, HALF)] = block.astype(f32)
            row = pl.multiple_of(half * HALF + (2 * high + low) * 96, 16)
            fc2_ref[pl.ds(row, 96), :] = source[j, 96:192, :].astype(f32)


def finish_ff(idx, mine, peer):
    vmem = pl.BlockSpec(memory_space=pltpu.VMEM)
    return pl.pallas_call(
        finish_ff_body,
        in_specs=[pl.BlockSpec(memory_space=pltpu.SMEM), vmem, vmem],
        out_specs=[vmem, vmem],
        out_shape=[jax.ShapeDtypeStruct((D // 4, FF), f32), jax.ShapeDtypeStruct((FF // 4, D), f32)],
        compiler_params=params(),
        cost_estimate=pl.CostEstimate(flops=0, bytes_accessed=8_000_000, transcendentals=0),
        name="finish_ff",
    )(idx, mine, peer)


def finish_attn_body(idx_ref, mine_ref, peer_ref, qkv_ref, proj_ref):
    spot, core = idx_ref[1], idx_ref[2]
    for source, half in ((mine_ref, core), (peer_ref, 1 - core)):
        column = half * HALF
        for j in range(4):
            place_at = lax.bitwise_xor(spot, j)
            low, high = lax.rem(place_at, 2), lax.div(place_at, 2)
            row0 = pl.multiple_of((2 * low + high) * 48, 16)
            row1 = pl.multiple_of((2 * high + low) * 48, 16)
            for t in range(4):
                block = source[j, 48 * (t // 2) : 48 * (t // 2 + 1), (t % 2) * HALF : (t % 2 + 1) * HALF].astype(f32)
                row = row0 if t < 2 else row1
                if t < 3:
                    qkv_ref[pl.ds(row, 48), pl.ds(pl.multiple_of(t * D + column, 128), HALF)] = block
                else:
                    proj_ref[pl.ds(row, 48), pl.ds(pl.multiple_of(column, 128), HALF)] = block


def finish_attn(idx, mine, peer):
    vmem = pl.BlockSpec(memory_space=pltpu.VMEM)
    return pl.pallas_call(
        finish_attn_body,
        in_specs=[pl.BlockSpec(memory_space=pltpu.SMEM), vmem, vmem],
        out_specs=[vmem, vmem],
        out_shape=[jax.ShapeDtypeStruct((D // 4, 3 * D), f32), jax.ShapeDtypeStruct((D // 4, D), f32)],
        compiler_params=params(),
        cost_estimate=pl.CostEstimate(flops=0, bytes_accessed=5_000_000, transcendentals=0),
        name="finish_attn",
    )(idx, mine, peer)


def swap(array, bit):
    count = lax.axis_size("dp")
    return lax.ppermute(array, "dp", [(i, i ^ bit) for i in range(count)])


def shift(array, step):
    count = lax.axis_size("mod")
    return lax.ppermute(array, "mod", [(i, (i + step) % count) for i in range(count)])


def take(array, index, size, axis=0):
    return lax.dynamic_slice_in_dim(array, index * size, size, axis)


def gather_half(own, spot, order):
    piece = take(own, spot, own.shape[0] // 4)
    near = jnp.stack([shift(piece, k) for k in range(1, lax.axis_size("mod"))])
    near = jnp.stack([near, swap(near, 2 * order[0])])
    far = swap(near, 2 * order[1])
    return near, far


def halve(grad, spot, bit):
    size = grad.shape[1] // 2
    side = (spot // bit) % 2
    arrived = swap(take(grad, 1 - side, size, 1), 2 * bit)
    return (take(grad, side, size, 1).astype(f32) + arrived.astype(f32)).astype(bf16)


def spread_chips(grad):
    bit = 8
    while bit < lax.axis_size("dp"):
        grad = (grad.astype(f32) + swap(grad, bit).astype(f32)).astype(bf16)
        bit *= 2
    return grad


def scatter_mod(grad, me):
    count = lax.axis_size("mod")
    total = lax.dynamic_index_in_dim(grad, me, 0, keepdims=False).astype(f32)
    for k in range(1, count):
        piece = lax.dynamic_index_in_dim(grad, (me + k) % count, 0, keepdims=False)
        total = total + shift(piece, k).astype(f32)
    return total.astype(bf16)


def gather_chips(piece):
    mine = jnp.stack([piece, swap(piece, 2), swap(piece, 4), swap(piece, 6)])
    return mine, swap(mine, 1)


def local(
    block_input,
    grad_out,
    long_flag,
    valid_mask,
    labels,
    tsteps,
    time_table,
    class_table,
    w_ada,
    b_ada,
    w_qkv,
    qv_bias,
    w_proj,
    proj_bias,
    w_fc1,
    fc1_bias,
    w_fc2,
    fc2_bias,
    rel_table,
):
    mods_n = lax.axis_size("mod")
    me = lax.axis_index("mod")
    place_dp = lax.axis_index("dp")
    core = place_dp % 2
    spot = (place_dp // 2) % 4
    idx = jnp.stack([me, spot, core]).astype(jnp.int32)
    first = 1 - core
    slots_n = MICRO * NSEG

    step_flat = tsteps.reshape(slots_n)
    label_flat = labels.reshape(slots_n)
    cond = time_table[step_flat].astype(f32) + class_table[label_flat].astype(f32)
    sigma = jax.nn.sigmoid(cond)
    act = (cond * sigma).astype(bf16)
    slope = sigma * (1.0 + cond * (1.0 - sigma))
    digits = jnp.stack([step_flat // 32, step_flat % 32, label_flat // 32, label_flat % 32], axis=1).astype(bf16)
    digits = jnp.pad(digits, ((0, 0), (0, 124)))
    rel_shape = rel_table.shape
    small = jnp.concatenate(
        [qv_bias, proj_bias, fc1_bias, fc2_bias, jnp.pad(rel_table, ((0, 0), (0, 1))).reshape(-1)]
    ).reshape(slots_n, -1)
    small_n = small.shape[1]
    packet = jnp.concatenate([act, digits, small], axis=1)
    group = jnp.stack([packet] + [shift(packet, k) for k in range(1, mods_n)])
    group_act = group[:, :, :D].reshape(mods_n * slots_n, D)
    columns = jnp.dot(group_act, w_ada, preferred_element_type=f32) + b_ada.astype(f32)
    columns = columns.reshape(mods_n, slots_n, -1)
    back = [columns[0]] + [shift(columns[k], mods_n - k) for k in range(1, mods_n)]
    turn = (mods_n - me) % mods_n
    modulation = lax.dynamic_slice_in_dim(jnp.stack(back + back), turn, mods_n, 0)
    modulation = modulation.transpose(1, 0, 2).reshape(MICRO, NSEG, 6, D)
    long_one = long_flag.reshape(MICRO)
    is_long = long_one[:, None, None, None] > 0
    seg_mod = jnp.where(is_long, modulation[:, :1], modulation)
    valid_seg = valid_mask.reshape(MICRO, NSEG, SEG)[:, :, 0]
    valid = valid_seg.astype(f32)[:, :, None, None]
    is_gate = (jnp.arange(6) % 3 == 2)[None, None, :, None]
    mods = jnp.where(is_gate, seg_mod * valid, seg_mod).reshape(slots_n, 6, D)

    rows_small = jnp.stack([group[k, :, D + 128 :] for k in range(mods_n)])
    rows_small = rows_small[::-1]
    rows_small = lax.dynamic_slice_in_dim(jnp.concatenate([rows_small, rows_small]), (mods_n - 1 - me) % mods_n, mods_n, 0)
    rows_small = rows_small.reshape(mods_n, -1).astype(f32)
    sizes = [qv_bias.shape[0], proj_bias.shape[0], fc1_bias.shape[0], fc2_bias.shape[0]]
    cuts = [0]
    for n in sizes:
        cuts.append(cuts[-1] + n)
    full_qv = rows_small[:, cuts[0] : cuts[1]].reshape(-1)
    full_proj_b = rows_small[:, cuts[1] : cuts[2]].reshape(1, -1)
    full_fc1_b = rows_small[:, cuts[2] : cuts[3]].reshape(mods_n, 2, HALF)
    full_fc2_b = rows_small[:, cuts[3] : cuts[4]].reshape(1, -1)
    full_rel = rows_small[:, cuts[4] :].reshape(H, 2 * L)
    windows = jnp.stack([full_rel[:, SEG * n : SEG * n + 2 * SEG] for n in range(7)], axis=1)
    windows = jnp.pad(windows[:, :, 254::-1], ((0, 0), (0, 1), (0, 1)))
    bias_thirds = jnp.concatenate([full_qv[:D], jnp.zeros((D,), f32), full_qv[D:]]).reshape(3, 2, HALF)

    def half_bias(which):
        return lax.dynamic_index_in_dim(bias_thirds, which, 1, keepdims=False).reshape(1, 3 * HALF)

    qkv_own = w_qkv.reshape(D // mods_n, 3, 2, HALF)
    proj_own = w_proj.reshape(D // mods_n, 2, HALF)
    fc1_own = w_fc1.reshape(D // mods_n, mods_n, 2, HALF)

    def halves(array, axis, shape):
        return tuple(
            lax.dynamic_index_in_dim(array, which, axis, keepdims=False).reshape(shape) for which in (first, core)
        )

    fetch = {}
    for name, (own, order) in dict(
        qkv=(halves(qkv_own, 2, (D // mods_n, 3 * HALF)), (1, 2)),
        proj=(halves(proj_own, 1, (D // mods_n, HALF)), (2, 1)),
        fc1=(halves(fc1_own, 2, (D // mods_n, FH)), (2, 1)),
        fc2=(halves(w_fc2.reshape(2, HALF, D), 0, (HALF, D)), (1, 2)),
        ada=(halves(w_ada.reshape(2, HALF, -1), 0, (HALF, w_ada.shape[1])), (2, 1)),
    ).items():
        near, far = gather_half(own[0], spot, order)
        fetch[name] = (
            place(idx, own[0], near, far, order),
            place(idx, own[1], swap(near, 1), swap(far, 1), order),
        )

    x = block_input.reshape(T, D)
    dy = grad_out.reshape(T, D)
    a, qkv1 = qkv_first(x, mods, fetch["qkv"][0], half_bias(first))
    qkv2 = qkv_second(a, fetch["qkv"][1], half_bias(core))
    o1, p1 = attend(qkv1, take(windows, first, H // 2), long_one, valid_seg)
    o2, p2 = attend(qkv2, take(windows, core, H // 2), long_one, valid_seg)
    half = first.reshape(1).astype(jnp.int32)
    swapped = core > 0
    proj_pair = fetch["proj"]
    proj_full = jnp.where(
        swapped,
        jnp.concatenate(proj_pair, axis=1),
        jnp.concatenate(proj_pair[::-1], axis=1),
    )
    hidden, m_in, attn, d_mlp, db_fc2 = middle(half, o1, o2, proj_full, full_proj_b, x, dy, mods)
    fc1_b = [lax.dynamic_index_in_dim(full_fc1_b, which, 1, keepdims=False).reshape(1, FH) for which in (first, core)]
    acc_o, acc_d, dw1_send, dw2_send, db1_first = mlp(m_in, d_mlp, fetch["fc1"][0], fetch["fc2"][0], fc1_b[0])
    ff, dm, dw1_keep, dw2_keep, db1_second = mlp(
        m_in, d_mlp, fetch["fc1"][1], fetch["fc2"][1], fc1_b[1], (acc_o, acc_d)
    )

    def pair_sum(keep, send):
        return (keep.astype(f32) + swap(send, 1).astype(f32)).astype(bf16)

    c1 = pair_sum(dw1_keep, dw1_send).reshape(mods_n, D // mods_n, FH)
    c2 = pair_sum(dw2_keep, dw2_send).reshape(mods_n, HALF, D)
    c1 = halve(c1, spot, 1)
    c2 = halve(c2, spot, 2)
    c1 = spread_chips(halve(c1, spot, 2))
    c2 = spread_chips(halve(c2, spot, 1))
    ff_part = scatter_mod(jnp.concatenate([c1[:, :, :D], c1[:, :, D:], c2], axis=1), me)
    grad_fc1, grad_fc2 = finish_ff(idx, *gather_chips(ff_part))

    y, d_h, do1, do2, dwp_send, dwp_keep, dmod_mid, db_proj = back_middle(
        half, hidden, dy, ff, full_fc2_b, dm, attn, mods, o1, o2, proj_full
    )
    dq1, dk1, dv1, dt1, dbq1 = attend_back(qkv1, p1, do1, o1)
    dwq_send = qkv_weight(a, dq1, dk1, dv1)
    dq2, dk2, dv2, dt2, dbq2 = attend_back(qkv2, p2, do2, o2)
    dwq_keep = qkv_weight(a, dq2, dk2, dv2)
    c3 = jnp.concatenate([pair_sum(dwq_keep, dwq_send), pair_sum(dwp_keep, dwp_send)], axis=1)
    c3 = c3.reshape(mods_n, D // mods_n, FH)
    left = spread_chips(halve(halve(c3[:, :, :D], spot, 1), spot, 2))
    right = spread_chips(halve(halve(c3[:, :, D:], spot, 2), spot, 1))
    attn_part = scatter_mod(jnp.concatenate([left, right], axis=1), me)
    grad_qkv, grad_proj = finish_attn(idx, *gather_chips(attn_part))

    dx, dmod_entry = back_entry(
        (dq1, dk1, dv1, dq2, dk2, dv2), fetch["qkv"][0], fetch["qkv"][1], x, d_h, mods
    )

    d_seg = jnp.concatenate([dmod_entry, dmod_mid[:, 2:, :]], axis=1).reshape(MICRO, NSEG, 6, D)
    d_seg = jnp.where(is_gate, d_seg * valid, d_seg)
    whole = jnp.sum(d_seg, axis=1, keepdims=True)
    lead = (jnp.arange(NSEG) == 0)[None, :, None, None]
    d_mod = jnp.where(is_long, jnp.where(lead, whole, 0.0), d_seg).reshape(slots_n, mods_n, -1).astype(bf16)
    ada_pair = fetch["ada"]
    width = w_ada.shape[1]

    def ada_half(which):
        weight = ada_pair[which].reshape(mods_n, HALF, width)
        return jnp.einsum("smc,mrc->sr", d_mod, weight, preferred_element_type=f32)

    one, two = ada_half(0), ada_half(1)
    d_act = jnp.where(swapped, jnp.concatenate([one, two], axis=1), jnp.concatenate([two, one], axis=1))
    d_cond = (d_act * slope).astype(bf16)

    def both(one_half, two_half, axis):
        pair = jnp.stack([one_half, two_half], axis=axis)
        return jnp.where(swapped, pair, jnp.flip(pair, axis))

    g_qv = both(
        jnp.stack([dbq1[0], dbq1[1]]), jnp.stack([dbq2[0], dbq2[1]]), 1
    ).reshape(mods_n, -1)
    g_fc1 = both(db1_first[0].reshape(mods_n, HALF), db1_second[0].reshape(mods_n, HALF), 1).reshape(mods_n, -1)
    dt = both(dt1, dt2, 0).reshape(H, 8, 2 * SEG)[:, :7, 254::-1]
    g_rel = sum(
        jnp.pad(dt[:, n], ((0, 0), (SEG * n, 2 * L - 255 - SEG * n))) for n in range(7)
    )
    g_small = jnp.concatenate(
        [g_qv, db_proj[0].reshape(mods_n, -1), g_fc1, db_fc2[0].reshape(mods_n, -1), g_rel.reshape(mods_n, -1)],
        axis=1,
    ).astype(bf16).reshape(mods_n, slots_n, small_n)

    def outgoing(k):
        target = (me + k) % mods_n
        return jnp.concatenate(
            [
                lax.dynamic_index_in_dim(d_mod, target, 1, keepdims=False),
                d_cond,
                lax.dynamic_index_in_dim(g_small, target, 0, keepdims=False),
            ],
            axis=1,
        )

    arrived = jnp.stack([outgoing(0)] + [shift(outgoing(k), k) for k in range(1, mods_n)])
    small_sum = jnp.sum(arrived[:, :, width + D :].astype(f32), axis=0).astype(bf16)
    body = jnp.concatenate([arrived[:, :, : width + D], group[:, :, : D + 128]], axis=2).reshape(mods_n * slots_n, -1)
    small_sum = jnp.pad(small_sum, ((0, 0), (0, body.shape[1] - small_n)))
    everyone = lax.all_gather(jnp.concatenate([body, small_sum]), "dp", axis=0, tiled=False)
    small_all = jnp.sum(everyone[:, mods_n * slots_n :, :small_n].astype(f32), axis=0).reshape(-1)
    everyone = everyone[:, : mods_n * slots_n].reshape(-1, body.shape[1])
    d_mod_all = everyone[:, :width]
    d_cond_all = everyone[:, width : width + D]
    act_all = everyone[:, width + D : width + 2 * D]
    digits_all = everyone[:, width + 2 * D : width + 2 * D + 4].astype(jnp.int32)
    grad_ada = lax.dot_general(act_all, d_mod_all, (((0,), (0,)), ((), ())), preferred_element_type=f32)
    grad_ada_b = jnp.sum(d_mod_all.astype(f32), axis=0)

    def table_grad(high, low, rows):
        share = rows // mods_n
        index = digits_all[:, high] * 32 + digits_all[:, low]
        hot = (index[None, :] == me * share + jnp.arange(share)[:, None]).astype(bf16)
        return jnp.dot(hot, d_cond_all, preferred_element_type=f32)

    grad_time = table_grad(0, 1, time_table.shape[0])
    grad_class = table_grad(2, 3, class_table.shape[0])
    return (
        y.reshape(block_input.shape),
        dx.reshape(block_input.shape),
        grad_time,
        grad_class,
        grad_ada,
        grad_ada_b,
        grad_qkv,
        small_all[cuts[0] : cuts[1]],
        grad_proj,
        small_all[cuts[1] : cuts[2]],
        grad_fc1,
        small_all[cuts[2] : cuts[3]],
        grad_fc2,
        small_all[cuts[3] : cuts[4]],
        small_all[cuts[4] :].reshape(rel_shape[0], 2 * L)[:, : rel_shape[1]],
    )


def solution(mesh):
    in_specs = (
        P(None, ("dp", "mod"), None),
        P(None, ("dp", "mod"), None),
        P(None, ("dp", "mod")),
        P(None, ("dp", "mod")),
        P(None, ("dp", "mod")),
        P(None, ("dp", "mod")),
        P(),
        P(),
        P(None, "mod"),
        P("mod"),
        P("mod", None),
        P("mod"),
        P("mod", None),
        P("mod"),
        P("mod", None),
        P("mod"),
        P("mod", None),
        P("mod"),
        P("mod", None),
    )
    out_specs = (
        P(None, ("dp", "mod"), None),
        P(None, ("dp", "mod"), None),
        P("mod", None),
        P("mod", None),
        P(None, "mod"),
        P("mod"),
        P("mod", None),
        P("mod"),
        P("mod", None),
        P("mod"),
        P("mod", None),
        P("mod"),
        P("mod", None),
        P("mod"),
        P("mod", None),
    )
    return jax.shard_map(local, mesh=mesh, in_specs=in_specs, out_specs=out_specs, check_vma=False)
```

```python
from functools import partial
import jax
import jax.numpy as jnp
from jax import lax
from jax.experimental import pallas as pl
from jax.experimental.pallas import tpu as pltpu
from jax.sharding import PartitionSpec as P

f32 = jnp.float32
bf16 = jnp.bfloat16
D = 768
H = 12
HD = 64
FF = 3072
L = 512
SEG = 128
NSEG = 4
MICRO = 2
T = MICRO * L
HALF = 384
FH = 1536
VMEM_LIMIT = 56 * 1024 * 1024


LONG = pl.CostEstimate(flops=30_000_000_000, bytes_accessed=1_000_000, transcendentals=0)
SHORT = pl.CostEstimate(flops=1, bytes_accessed=1, transcendentals=0)


def params(*sem):
    return pltpu.CompilerParams(vmem_limit_bytes=VMEM_LIMIT, dimension_semantics=sem)


def dot(a, b, ca=1, cb=0):
    return lax.dot_general(a, b, (((ca,), (cb,)), ((), ())), preferred_element_type=f32)


def norm_of(values):
    centred = values - jnp.mean(values, axis=1, keepdims=True)
    inverse = lax.rsqrt(jnp.mean(centred * centred, axis=1, keepdims=True) + 1e-6)
    return centred * inverse, inverse


def norm_back(grad, normed, inverse):
    return inverse * (
        grad
        - jnp.mean(grad, axis=1, keepdims=True)
        - normed * jnp.mean(grad * normed, axis=1, keepdims=True)
    )


UR = 48
ANY = pl.BlockSpec(memory_space=pl.ANY)
SMEM = pl.BlockSpec(memory_space=pltpu.SMEM)
VMEM = pl.BlockSpec(memory_space=pltpu.VMEM)


def whole(shape):
    return pl.BlockSpec(shape, lambda *_: (0,) * len(shape))


def bring(copies, sems):
    made = [pltpu.make_async_copy(source, target, sems.at[n]) for n, (source, target) in enumerate(copies)]
    return made


def go(made):
    for copy in made:
        copy.start()


def ready(made):
    for copy in made:
        copy.wait()


def quarters(idx_ref, sources):
    me, spot = idx_ref[0], idx_ref[1]
    for ref, lead, other in sources:
        for k in range(1, 4):
            yield (
                ref.at[k - 1] if lead is None else ref.at[lead, k - 1],
                lax.rem(me + 4 - k, 4),
                lax.bitwise_xor(spot, other),
            )


def pick_entry_body(idx_ref, w_ref, proj_ref, own_ref, piece_ref):
    spot, core = idx_ref[1], idx_ref[2]
    for n, half in enumerate((1 - core, core)):
        for u in range(3):
            column = pl.multiple_of((2 * u + half) * HALF, HALF)
            own_ref[n, u] = w_ref[:, pl.ds(column, HALF)].reshape(4, UR, HALF)
        own_ref[n, 3] = proj_ref[:, pl.ds(pl.multiple_of(half * HALF, HALF), HALF)].reshape(4, UR, HALF)
    for u in range(4):
        piece_ref[u] = own_ref[0, u, spot]


def pick_entry(idx, w, proj):
    return pl.pallas_call(
        pick_entry_body,
        in_specs=[SMEM, VMEM, VMEM],
        out_specs=[VMEM, VMEM],
        out_shape=[jax.ShapeDtypeStruct((2, 4, 4, UR, HALF), bf16), jax.ShapeDtypeStruct((4, UR, HALF), bf16)],
        compiler_params=params(),
        cost_estimate=SHORT,
        name="pick_entry",
    )(idx, w, proj)


def pick_ff_body(idx_ref, fc1_ref, fc2_ref, own1_ref, own2_ref, piece_ref):
    spot, core = idx_ref[1], idx_ref[2]
    for n, half in enumerate((1 - core, core)):
        for z in range(4):
            column = pl.multiple_of((2 * z + half) * HALF, HALF)
            own1_ref[n, z] = fc1_ref[:, pl.ds(column, HALF)].reshape(4, UR, HALF)
        for j in range(2):
            for i in range(2):
                row = pl.multiple_of(half * HALF + i * 192, 192)
                own2_ref[n, 2 * j + i] = fc2_ref[pl.ds(row, 192), j * HALF : (j + 1) * HALF].reshape(4, UR, HALF)
    for n, q in enumerate((spot, lax.bitwise_xor(spot, 3))):
        for u in range(4):
            piece_ref[n, u] = own1_ref[0, u, q]
            piece_ref[n, 4 + u] = own2_ref[0, u, q]


def pick_ff(idx, fc1, fc2):
    return pl.pallas_call(
        pick_ff_body,
        in_specs=[SMEM, VMEM, VMEM],
        out_specs=[VMEM] * 3,
        out_shape=[
            jax.ShapeDtypeStruct((2, 4, 4, UR, HALF), bf16),
            jax.ShapeDtypeStruct((2, 4, 4, UR, HALF), bf16),
            jax.ShapeDtypeStruct((2, 8, UR, HALF), bf16),
        ],
        compiler_params=params(),
        cost_estimate=SHORT,
        name="pick_ff",
    )(idx, fc1, fc2)


def pick_ada_body(idx_ref, w_ref, own_ref, piece_ref):
    spot, core = idx_ref[1], idx_ref[2]
    for n, half in enumerate((1 - core, core)):
        for c in range(3):
            for i in range(2):
                row = pl.multiple_of(half * HALF + i * 192, 192)
                own_ref[n, 2 * c + i] = w_ref[pl.ds(row, 192), c * HALF : (c + 1) * HALF].reshape(4, UR, HALF)
    for u in range(6):
        piece_ref[u] = own_ref[0, u, spot]


def pick_ada(idx, w):
    return pl.pallas_call(
        pick_ada_body,
        in_specs=[SMEM, VMEM],
        out_specs=[VMEM, VMEM],
        out_shape=[jax.ShapeDtypeStruct((2, 6, 4, UR, HALF), bf16), jax.ShapeDtypeStruct((6, UR, HALF), bf16)],
        compiler_params=params(),
        cost_estimate=SHORT,
        name="pick_ada",
    )(idx, w)


def entry_copies(idx_ref, own, half, sources, held):
    return [(own.at[half, pl.ds(0, 3)], held.at[:, idx_ref[0]])] + [
        (ref.at[pl.ds(0, 3)], held.at[:, z, q]) for ref, z, q in quarters(idx_ref, sources)
    ]


def stacked(ref):
    return [(ref, n, n) for n in range(4)]


def proj_copies(idx_ref, own, half, at, sources, held):
    return [(own.at[half, 3], held.at[at, idx_ref[0]])] + [
        (ref.at[3], held.at[at, z, q]) for ref, z, q in quarters(idx_ref, sources)
    ]


def fc1_copies(idx_ref, own, half, sources, held):
    return [(own.at[half], held.at[:, idx_ref[0]])] + [
        (ref.at[pl.ds(0, 4)], held.at[:, z, q]) for ref, z, q in quarters(idx_ref, sources)
    ]


def fc2_copies(idx_ref, own, half, sources, held):
    return [(own.at[half, pl.ds(2 * j, 2)], held.at[j, idx_ref[0]]) for j in range(2)] + [
        (ref.at[pl.ds(4 + 2 * j, 2)], held.at[j, z, :, q]) for ref, z, q in quarters(idx_ref, sources) for j in range(2)
    ]


def ada_copies(idx_ref, own, half, sources, held):
    return [(own.at[half, pl.ds(2 * c, 2)], held.at[idx_ref[0], c]) for c in range(3)] + [
        (ref.at[pl.ds(2 * c, 2)], held.at[z, c, :, q]) for ref, z, q in quarters(idx_ref, sources) for c in range(3)
    ]


def entry_weight(held):
    return jnp.concatenate([held[u].reshape(D, HALF) for u in range(3)], axis=1)


def proj_weight(held):
    return jnp.concatenate([held[n].reshape(D, HALF) for n in range(2)], axis=1)


ENTRY_HELD = (3, 4, 4, UR, HALF)


def qkv_first_body(idx_ref, x_ref, mod_ref, b_ref, own, fetched, a_ref, qkv_ref, held, sems):
    i = pl.program_id(0)
    copies = bring(entry_copies(idx_ref, own, 0, stacked(fetched), held), sems)

    @pl.when(i == 0)
    def _():
        go(copies)

    for s in range(NSEG):
        rows = pl.ds(s * SEG, SEG)
        at = pl.ds(i * NSEG + s, 1)
        norm, _ = norm_of(x_ref[rows, :].astype(f32))
        a_ref[rows, :] = (norm * (1.0 + mod_ref[1, at, :]) + mod_ref[0, at, :]).astype(bf16)

    @pl.when(i == 0)
    def _():
        ready(copies)

    qkv_ref[...] = (dot(a_ref[...], entry_weight(held)) + b_ref[...]).astype(bf16)


def qkv_first(idx, x, mods, b, own, near):
    return pl.pallas_call(
        qkv_first_body,
        grid=(MICRO,),
        in_specs=[
            SMEM,
            pl.BlockSpec((L, D), lambda i: (i, 0)),
            whole((6, MICRO * NSEG, D)),
            whole((1, 3 * HALF)),
            ANY, ANY,
        ],
        out_specs=[
            pl.BlockSpec((L, D), lambda i: (i, 0)),
            pl.BlockSpec((L, 3 * HALF), lambda i: (i, 0)),
        ],
        out_shape=[
            jax.ShapeDtypeStruct((T, D), bf16),
            jax.ShapeDtypeStruct((T, 3 * HALF), bf16),
        ],
        scratch_shapes=[pltpu.VMEM(ENTRY_HELD, bf16), pltpu.SemaphoreType.DMA((13,))],
        compiler_params=params("arbitrary"),
        cost_estimate=SHORT,
        name="qkv_first",
    )(idx, x, mods, b, own, near)


def qkv_second_body(idx_ref, a_ref, b_ref, own, fetched, qkv_ref, held, sems):
    copies = bring(entry_copies(idx_ref, own, 1, stacked(fetched), held), sems)

    @pl.when(pl.program_id(0) == 0)
    def _():
        go(copies)
        ready(copies)

    qkv_ref[...] = (dot(a_ref[...], entry_weight(held)) + b_ref[...]).astype(bf16)


def qkv_second(idx, a, b, own, near):
    return pl.pallas_call(
        qkv_second_body,
        grid=(MICRO,),
        in_specs=[
            SMEM,
            pl.BlockSpec((L, D), lambda i: (i, 0)),
            whole((1, 3 * HALF)),
            ANY, ANY,
        ],
        out_specs=pl.BlockSpec((L, 3 * HALF), lambda i: (i, 0)),
        out_shape=jax.ShapeDtypeStruct((T, 3 * HALF), bf16),
        scratch_shapes=[pltpu.VMEM(ENTRY_HELD, bf16), pltpu.SemaphoreType.DMA((13,))],
        compiler_params=params("arbitrary"),
        cost_estimate=SHORT,
        name="qkv_second",
    )(idx, a, b, own, near)


def lane_reverse(rows):
    at = lax.broadcasted_iota(jnp.int32, (2 * SEG, 2 * SEG), 0) + lax.broadcasted_iota(jnp.int32, (2 * SEG, 2 * SEG), 1)
    turn = (at == 2 * SEG - 2).astype(f32)
    return lax.dot_general(
        rows, turn, (((1,), (0,)), ((), ())), precision=lax.Precision.HIGHEST, preferred_element_type=f32
    )


def attend_body(long_ref, valid_ref, q_ref, k_ref, v_ref, t_ref, o_ref, p_ref, bias_ref):
    b = pl.program_id(1)

    @pl.when(b == 0)
    def _():
        windows = [t_ref[0, h : h + 1, d * SEG : (d + 2) * SEG] for h in range(2) for d in range(7)]
        windows = lane_reverse(jnp.concatenate(windows + windows[:2], axis=0))
        for h in range(2):
            for d in range(7):
                row = jnp.broadcast_to(windows[h * 7 + d : h * 7 + d + 1, :], (SEG, 2 * SEG))
                bias_ref[h, d] = pltpu.roll(row, SEG + 1, 1, stride=1, stride_axis=0)[:, :SEG]

    is_long = long_ref[b]
    lane = lax.broadcasted_iota(jnp.int32, (L, 2 * HD), 1)
    query = q_ref[...] * jnp.asarray(HD**-0.5, bf16)
    keys = k_ref[...]
    values_t = v_ref[...].T
    outs = []
    for h in range(2):
        mine = (lane < HD) if h == 0 else (lane >= HD)
        key_h = jnp.where(mine, keys, jnp.zeros_like(keys))
        for qb in range(NSEG):
            cols = pl.ds(qb * SEG, SEG)
            scores = dot(key_h, query[qb * SEG : (qb + 1) * SEG, :], 1, 1)
            parts = []
            for kb in range(NSEG):
                open_ = (valid_ref[b, kb] > 0) if kb == qb else ((valid_ref[b, kb] > 0) & (is_long > 0))
                shut = jnp.where(open_, 0.0, -1e30).astype(f32)
                parts.append(scores[kb * SEG : (kb + 1) * SEG, :] + (bias_ref[h, kb - qb + 3] + shut))
            scores = jnp.concatenate(parts, axis=0)
            top = jnp.max(scores, axis=0, keepdims=True)
            expo = jnp.exp(scores - top)
            total = jnp.sum(expo, axis=0, keepdims=True)
            p_ref[0, h, :, cols] = (expo * (1.0 / total)).astype(bf16)
        outs.append(dot(values_t[h * HD : (h + 1) * HD, :], p_ref[0, h]))
    o_ref[...] = jnp.concatenate(outs, axis=0).T.astype(bf16)


def attend(qkv, table, long_flag, valid_seg):
    pairs = 3
    return pl.pallas_call(
        attend_body,
        grid_spec=pltpu.PrefetchScalarGridSpec(
            num_scalar_prefetch=2,
            grid=(pairs, MICRO),
            in_specs=[
                pl.BlockSpec((L, 2 * HD), lambda g, b, *_: (b, g)),
                pl.BlockSpec((L, 2 * HD), lambda g, b, *_: (b, 3 + g)),
                pl.BlockSpec((L, 2 * HD), lambda g, b, *_: (b, 6 + g)),
                pl.BlockSpec((1, 2, 2 * L), lambda g, b, *_: (g, 0, 0)),
            ],
            out_specs=[
                pl.BlockSpec((L, 2 * HD), lambda g, b, *_: (b, g)),
                pl.BlockSpec((1, 2, L, L), lambda g, b, *_: (b, g, 0, 0)),
            ],
            scratch_shapes=[pltpu.VMEM((2, 7, SEG, SEG), f32)],
        ),
        out_shape=[
            jax.ShapeDtypeStruct((T, HALF), bf16),
            jax.ShapeDtypeStruct((MICRO, 6, L, L), bf16),
        ],
        compiler_params=params("arbitrary", "arbitrary"),
        cost_estimate=SHORT,
        name="attend",
    )(long_flag, valid_seg, qkv, qkv, qkv, table)


def middle_body(idx_ref, o1_ref, o2_ref, b_ref, x_ref, dy_ref, mod_ref, own, fetched, peer,
                h_ref, m_ref, attn_ref, dmlp_ref, db_ref, held, w_ref, sems):
    core = idx_ref[2]
    i = pl.program_id(0)

    @pl.when(i == 0)
    def _():
        copies = bring(
            proj_copies(idx_ref, own, 0, 1 - core, stacked(fetched), held)
            + proj_copies(idx_ref, own, 1, core, stacked(peer), held),
            sems,
        )
        go(copies)
        ready(copies)
        w_ref[...] = proj_weight(held)

    first = pl.multiple_of((1 - core) * HALF, HALF)
    second = pl.multiple_of(core * HALF, HALF)
    attn = dot(o1_ref[...], w_ref[pl.ds(first, HALF), :]) + dot(o2_ref[...], w_ref[pl.ds(second, HALF), :])
    attn = attn + b_ref[...]
    attn_ref[...] = attn.astype(bf16)
    total = jnp.zeros((1, D), f32)
    for s in range(NSEG):
        rows = pl.ds(s * SEG, SEG)
        at = pl.ds(i * NSEG + s, 1)
        hidden = x_ref[rows, :].astype(f32) + mod_ref[2, at, :] * attn[s * SEG : (s + 1) * SEG, :]
        h_ref[rows, :] = hidden
        norm, _ = norm_of(hidden)
        m_ref[rows, :] = (norm * (1.0 + mod_ref[4, at, :]) + mod_ref[3, at, :]).astype(bf16)
        dmlp = (dy_ref[rows, :].astype(f32) * mod_ref[5, at, :]).astype(bf16)
        dmlp_ref[rows, :] = dmlp
        total = total + jnp.sum(dmlp.astype(f32), axis=0, keepdims=True)

    @pl.when(pl.program_id(0) == 0)
    def _():
        db_ref[...] = jnp.zeros_like(db_ref)

    db_ref[0:1, :] += total


def middle(idx, o1, o2, b, x, dy, mods, own, one, two):
    row = lambda i: (i, 0)
    return pl.pallas_call(
        middle_body,
        grid=(MICRO,),
        in_specs=[
            SMEM,
            pl.BlockSpec((L, HALF), row),
            pl.BlockSpec((L, HALF), row),
            whole((1, D)),
            pl.BlockSpec((L, D), row),
            pl.BlockSpec((L, D), row),
            whole((6, MICRO * NSEG, D)),
        ] + [ANY] * 3,
        out_specs=[
            pl.BlockSpec((L, D), row),
            pl.BlockSpec((L, D), row),
            pl.BlockSpec((L, D), row),
            pl.BlockSpec((L, D), row),
            whole((8, D)),
        ],
        out_shape=[
            jax.ShapeDtypeStruct((T, D), f32),
            jax.ShapeDtypeStruct((T, D), bf16),
            jax.ShapeDtypeStruct((T, D), bf16),
            jax.ShapeDtypeStruct((T, D), bf16),
            jax.ShapeDtypeStruct((8, D), f32),
        ],
        scratch_shapes=[
            pltpu.VMEM((2, 4, 4, UR, HALF), bf16),
            pltpu.VMEM((D, D), bf16),
            pltpu.SemaphoreType.DMA((26,)),
        ],
        compiler_params=params("arbitrary"),
        cost_estimate=LONG,
        name="middle",
    )(idx, o1, o2, b, x, dy, mods, own, one, two)


FB = 768


def mlp_body(has_acc, idx_ref, m_ref, dmlp_ref, b_ref, own1, own2, fetched, *refs):
    if has_acc:
        acc_o, acc_d, out_o, out_d, dw1_ref, dw2_ref, db_ref, g_s, du_s, held1, held2, sems = refs
    else:
        out_o, out_d, dw1_ref, dw2_ref, db_ref, g_s, du_s, held1, held2, sems = refs
    f = pl.program_id(0)
    half_index = 1 if has_acc else 0

    @pl.when(f == 0)
    def _():
        copies = bring(
            fc1_copies(idx_ref, own1, half_index, stacked(fetched), held1)
            + fc2_copies(idx_ref, own2, half_index, stacked(fetched), held2),
            sems,
        )
        go(copies)
        ready(copies)

    w1 = jnp.concatenate([held1[2 * f + n].reshape(D, HALF) for n in range(2)], axis=1)
    w2 = jnp.concatenate([held2[j, pl.ds(2 * f, 2)].reshape(D, HALF) for j in range(2)], axis=1)
    bias = b_ref[0:1, :]
    chunk = 256
    total = jnp.zeros((1, FB), f32)
    c0 = (2.0 / jnp.pi) ** 0.5
    for r in range(T // chunk):
        rows = pl.ds(r * chunk, chunk)
        u = dot(m_ref[rows, :], w1) + bias
        dg = dot(dmlp_ref[rows, :], w2, 1, 1)
        u2 = u * u
        th = jnp.tanh(u * (c0 + (c0 * 0.044715) * u2))
        half = 0.5 + 0.5 * th
        g_s[rows, :] = (u * half).astype(bf16)
        slope = half + u * (0.5 - 0.5 * th * th) * (c0 + (3.0 * c0 * 0.044715) * u2)
        du = (dg * slope).astype(bf16)
        du_s[rows, :] = du
        total = total + jnp.sum(du.astype(f32), axis=0, keepdims=True)
    db_ref[0:1, :] = total

    @pl.when(f == 0)
    def _():
        if has_acc:
            out_o[...] = acc_o[...] + dot(g_s[...], w2)
            out_d[...] = acc_d[...] + dot(du_s[...], w1, 1, 1)
        else:
            out_o[...] = dot(g_s[...], w2)
            out_d[...] = dot(du_s[...], w1, 1, 1)

    @pl.when(f > 0)
    def _():
        out_o[...] += dot(g_s[...], w2)
        out_d[...] += dot(du_s[...], w1, 1, 1)

    dw2_ref[...] = dot(g_s[...], dmlp_ref[...], 0, 0).astype(bf16)
    dw1_ref[...] = dot(m_ref[...], du_s[...], 0, 0).astype(bf16)


def mlp(idx, m_in, dmlp, b1, own1, own2, fetched, acc=None):
    zero = lambda f: (0, 0)
    col = lambda f: (0, f)
    once = pl.Buffered(1)
    specs = [
        SMEM,
        pl.BlockSpec((T, D), zero, pipeline_mode=once),
        pl.BlockSpec((T, D), zero, pipeline_mode=once),
        pl.BlockSpec((1, FB), col),
    ] + [ANY] * 3
    args = [idx, m_in, dmlp, b1, own1, own2, fetched]
    if acc is not None:
        specs += [pl.BlockSpec((T, D), zero, pipeline_mode=once)] * 2
        args += list(acc)
    return pl.pallas_call(
        partial(mlp_body, acc is not None),
        grid=(FH // FB,),
        in_specs=specs,
        out_specs=[
            pl.BlockSpec((T, D), zero),
            pl.BlockSpec((T, D), zero),
            pl.BlockSpec((D, FB), col),
            pl.BlockSpec((FB, D), lambda f: (f, 0)),
            pl.BlockSpec((8, FB), col),
        ],
        out_shape=[
            jax.ShapeDtypeStruct((T, D), f32),
            jax.ShapeDtypeStruct((T, D), f32),
            jax.ShapeDtypeStruct((D, FH), bf16),
            jax.ShapeDtypeStruct((FH, D), bf16),
            jax.ShapeDtypeStruct((8, FH), f32),
        ],
        scratch_shapes=[
            pltpu.VMEM((T, FB), bf16),
            pltpu.VMEM((T, FB), bf16),
            pltpu.VMEM((4, 4, 4, UR, HALF), bf16),
            pltpu.VMEM((2, 4, 2, 4, UR, HALF), bf16),
            pltpu.SemaphoreType.DMA((39,)),
        ],
        compiler_params=params("arbitrary"),
        cost_estimate=LONG,
        name="mlp",
    )(*args)


def back_middle_body(idx_ref, h_ref, dy_ref, mlp_ref, b2_ref, dm_ref, attn_ref, mod_ref, o1_ref, o2_ref,
                     own, fetched, peer,
                     y_ref, dh_ref, do1_ref, do2_ref, dws_ref, dwk_ref, dmod_ref, db_ref,
                     dattn_s, dw_s, held, w_ref, sems):
    i = pl.program_id(0)
    core = idx_ref[2]
    first = pl.multiple_of((1 - core) * HALF, HALF)
    second = pl.multiple_of(core * HALF, HALF)
    copies = bring(
        proj_copies(idx_ref, own, 0, 1 - core, stacked(fetched), held)
        + proj_copies(idx_ref, own, 1, core, stacked(peer), held),
        sems,
    )

    @pl.when(i == 0)
    def _():
        go(copies)

    total = jnp.zeros((1, D), f32)
    for s in range(NSEG):
        rows = pl.ds(s * SEG, SEG)
        at = pl.ds(i * NSEG + s, 1)
        hidden = h_ref[rows, :]
        dy = dy_ref[rows, :].astype(f32)
        ff = mlp_ref[rows, :] + b2_ref[...]
        y_ref[rows, :] = (hidden + mod_ref[5, at, :] * ff).astype(bf16)
        dmod_ref[5, at, :] = jnp.sum(dy * ff, axis=0, keepdims=True)
        norm, inverse = norm_of(hidden)
        dm = dm_ref[rows, :]
        dmod_ref[3, at, :] = jnp.sum(dm, axis=0, keepdims=True)
        dmod_ref[4, at, :] = jnp.sum(dm * norm, axis=0, keepdims=True)
        dh = dy + norm_back(dm * (1.0 + mod_ref[4, at, :]), norm, inverse)
        dh_ref[rows, :] = dh
        dmod_ref[2, at, :] = jnp.sum(dh * attn_ref[rows, :].astype(f32), axis=0, keepdims=True)
        dattn = (dh * mod_ref[2, at, :]).astype(bf16)
        dattn_s[rows, :] = dattn
        total = total + jnp.sum(dattn.astype(f32), axis=0, keepdims=True)
    dattn = dattn_s[...]

    @pl.when(i == 0)
    def _():
        ready(copies)
        w_ref[...] = proj_weight(held)

    do1_ref[...] = dot(dattn, w_ref[pl.ds(first, HALF), :], 1, 1).astype(bf16)
    do2_ref[...] = dot(dattn, w_ref[pl.ds(second, HALF), :], 1, 1).astype(bf16)

    @pl.when(i == 0)
    def _():
        db_ref[...] = jnp.zeros_like(db_ref)
        dmod_ref[0:2] = jnp.zeros((2, MICRO * NSEG, D), f32)
        dw_s[...] = jnp.zeros_like(dw_s)

    db_ref[0:1, :] += total
    dw_s[pl.ds(first, HALF), :] += dot(o1_ref[...], dattn, 0, 0)
    dw_s[pl.ds(second, HALF), :] += dot(o2_ref[...], dattn, 0, 0)

    @pl.when(i == MICRO - 1)
    def _():
        dws_ref[...] = dw_s[:, pl.ds(first, HALF)].astype(bf16)
        dwk_ref[...] = dw_s[:, pl.ds(second, HALF)].astype(bf16)


def back_middle(idx, h, dy, ff, b2, dm, attn, mods, o1, o2, own, one, two):
    row = lambda i: (i, 0)
    full = pl.BlockSpec((L, D), row)
    part = pl.BlockSpec((L, HALF), row)
    modspec = whole((6, MICRO * NSEG, D))
    return pl.pallas_call(
        back_middle_body,
        grid=(MICRO,),
        in_specs=[SMEM, full, full, full, whole((1, D)), full, full, modspec, part, part] + [ANY] * 3,
        out_specs=[full, full, part, part, whole((D, HALF)), whole((D, HALF)), modspec, whole((8, D))],
        scratch_shapes=[
            pltpu.VMEM((L, D), bf16),
            pltpu.VMEM((D, D), f32),
            pltpu.VMEM((2, 4, 4, UR, HALF), bf16),
            pltpu.VMEM((D, D), bf16),
            pltpu.SemaphoreType.DMA((26,)),
        ],
        out_shape=[
            jax.ShapeDtypeStruct((T, D), bf16),
            jax.ShapeDtypeStruct((T, D), f32),
            jax.ShapeDtypeStruct((T, HALF), bf16),
            jax.ShapeDtypeStruct((T, HALF), bf16),
            jax.ShapeDtypeStruct((D, HALF), bf16),
            jax.ShapeDtypeStruct((D, HALF), bf16),
            jax.ShapeDtypeStruct((6, MICRO * NSEG, D), f32),
            jax.ShapeDtypeStruct((8, D), f32),
        ],
        compiler_params=params("arbitrary"),
        cost_estimate=LONG,
        name="back_middle",
    )(idx, h, dy, ff, b2, dm, attn, mods, o1, o2, own, one, two)


def attend_back_body(q_ref, k_ref, v_ref, p_ref, do_ref, o_ref, dq_ref, dk_ref, dv_ref, dt_ref, db_ref, acc_ref, ds_s):
    b = pl.program_id(1)

    @pl.when(b == 0)
    def _():
        acc_ref[...] = jnp.zeros_like(acc_ref)
        db_ref[...] = jnp.zeros_like(db_ref)

    lane = lax.broadcasted_iota(jnp.int32, (L, 2 * HD), 1)
    query = q_ref[...]
    keys_t = k_ref[...].T
    values = v_ref[...]
    dout = do_ref[...]
    prod = (dout.astype(f32) * o_ref[...].astype(f32)).T
    dqs, dks, dvs = [], [], []
    for h in range(2):
        mine = (lane < HD) if h == 0 else (lane >= HD)
        value_h = jnp.where(mine, values, jnp.zeros_like(values))
        delta = jnp.sum(prod[h * HD : (h + 1) * HD, :], axis=0, keepdims=True)
        for qb in range(NSEG):
            cols = slice(qb * SEG, (qb + 1) * SEG)
            dp = dot(value_h, dout[cols, :], 1, 1)
            ds = (p_ref[0, h, :, cols].astype(f32) * (dp - delta[:, cols])).astype(bf16)
            ds_s[h, :, cols] = ds
            for kb in range(NSEG):
                acc_ref[h, kb - qb + 3] += ds[kb * SEG : (kb + 1) * SEG, :].astype(f32)
        dvs.append(dot(p_ref[0, h], dout))
        dks.append(dot(ds_s[h], query))
        dqs.append(dot(keys_t[h * HD : (h + 1) * HD, :], ds_s[h]))
    low = lane < HD
    scale = HD**-0.5
    dq = (jnp.concatenate(dqs, axis=0).T * scale).astype(bf16)
    dk = (jnp.where(low, dks[0], dks[1]) * scale).astype(bf16)
    dv = jnp.where(low, dvs[0], dvs[1]).astype(bf16)
    dq_ref[...] = dq
    dk_ref[...] = dk
    dv_ref[...] = dv
    db_ref[0:1, :] += jnp.sum(dq.astype(f32), axis=0, keepdims=True)
    db_ref[1:2, :] += jnp.sum(dv.astype(f32), axis=0, keepdims=True)

    @pl.when(b == MICRO - 1)
    def _():
        sums = []
        for h in range(2):
            for d in range(7):
                wide = jnp.concatenate([acc_ref[h, d], jnp.zeros((SEG, SEG), f32)], axis=1)
                rows = SEG
                while rows > 1:
                    rows //= 2
                    wide = pltpu.roll(wide[:rows], rows, 1) + wide[rows:]
                sums.append(wide)
        sums = lane_reverse(jnp.concatenate(sums + sums[:2], axis=0))
        dt_ref[...] = jnp.zeros_like(dt_ref)
        for h in range(2):
            for d in range(7):
                dt_ref[0, h : h + 1, d * SEG : (d + 2) * SEG] += sums[h * 7 + d : h * 7 + d + 1, :]


def attend_back(qkv, p, dout, out, cost):
    col = lambda g, b: (b, g)
    part = pl.BlockSpec((L, 2 * HD), col)
    return pl.pallas_call(
        attend_back_body,
        grid=(3, MICRO),
        in_specs=[
            part,
            pl.BlockSpec((L, 2 * HD), lambda g, b: (b, 3 + g)),
            pl.BlockSpec((L, 2 * HD), lambda g, b: (b, 6 + g)),
            pl.BlockSpec((1, 2, L, L), lambda g, b: (b, g, 0, 0)),
            part,
            part,
        ],
        out_specs=[part, part, part, pl.BlockSpec((1, 8, 2 * L), lambda g, b: (g, 0, 0)),
                   pl.BlockSpec((8, 2 * HD), lambda g, b: (0, g))],
        out_shape=[jax.ShapeDtypeStruct((T, HALF), bf16)] * 3
        + [jax.ShapeDtypeStruct((3, 8, 2 * L), f32), jax.ShapeDtypeStruct((8, HALF), f32)],
        scratch_shapes=[pltpu.VMEM((2, 7, SEG, SEG), f32), pltpu.VMEM((2, L, L), bf16)],
        compiler_params=params("arbitrary", "arbitrary"),
        cost_estimate=cost,
        name="attend_back",
    )(qkv, qkv, qkv, p, dout, out)


def qkv_weight_body(a_ref, dq_ref, dk_ref, dv_ref, out_ref):
    a = a_ref[...]
    out_ref[:, 0:HALF] = dot(a, dq_ref[...], 0, 0).astype(bf16)
    out_ref[:, HALF : 2 * HALF] = dot(a, dk_ref[...], 0, 0).astype(bf16)
    out_ref[:, 2 * HALF : 3 * HALF] = dot(a, dv_ref[...], 0, 0).astype(bf16)


def qkv_weight(a, dq, dk, dv, cost):
    return pl.pallas_call(
        qkv_weight_body,
        out_shape=jax.ShapeDtypeStruct((D, 3 * HALF), bf16),
        compiler_params=params(),
        cost_estimate=cost,
        name="qkv_weight",
    )(a, dq, dk, dv)


def back_entry_body(idx_ref, dq1, dk1, dv1, dq2, dk2, dv2, x_ref, dh_ref, mod_ref, own, fetched, peer,
                    dx_ref, dmod_ref, held1, held2, sems):
    i = pl.program_id(0)

    @pl.when(i == 0)
    def _():
        copies = bring(
            entry_copies(idx_ref, own, 0, stacked(fetched), held1)
            + entry_copies(idx_ref, own, 1, stacked(peer), held2),
            sems,
        )
        go(copies)
        ready(copies)

    one = jnp.concatenate([dq1[...], dk1[...], dv1[...]], axis=1)
    two = jnp.concatenate([dq2[...], dk2[...], dv2[...]], axis=1)
    da = dot(one, entry_weight(held1), 1, 1) + dot(two, entry_weight(held2), 1, 1)
    for s in range(NSEG):
        rows = pl.ds(s * SEG, SEG)
        at = pl.ds(i * NSEG + s, 1)
        piece = da[s * SEG : (s + 1) * SEG, :]
        norm, inverse = norm_of(x_ref[rows, :].astype(f32))
        dmod_ref[0, at, :] = jnp.sum(piece, axis=0, keepdims=True)
        dmod_ref[1, at, :] = jnp.sum(piece * norm, axis=0, keepdims=True)
        dx_ref[rows, :] = (
            dh_ref[rows, :] + norm_back(piece * (1.0 + mod_ref[1, at, :]), norm, inverse)
        ).astype(bf16)


def back_entry(idx, parts, x, dh, mods, own, near, peer):
    row = lambda i: (i, 0)
    full = pl.BlockSpec((L, D), row)
    part = pl.BlockSpec((L, HALF), row)
    return pl.pallas_call(
        back_entry_body,
        grid=(MICRO,),
        in_specs=[SMEM] + [part] * 6 + [full, full, whole((6, MICRO * NSEG, D))] + [ANY] * 3,
        out_specs=[full, whole((2, MICRO * NSEG, D))],
        out_shape=[jax.ShapeDtypeStruct((T, D), bf16), jax.ShapeDtypeStruct((2, MICRO * NSEG, D), f32)],
        scratch_shapes=[
            pltpu.VMEM(ENTRY_HELD, bf16),
            pltpu.VMEM(ENTRY_HELD, bf16),
            pltpu.SemaphoreType.DMA((26,)),
        ],
        compiler_params=params("arbitrary"),
        cost_estimate=SHORT,
        name="back_entry",
    )(idx, *parts, x, dh, mods, own, near, peer)


def pack_small_body(idx_ref, q1, q2, proj_ref, u1, u2, fc2_ref, t1, t2, out_ref):
    core = idx_ref[2]
    for z in range(4):
        half = z // 2
        tail = []
        for t in range(3):
            n = (z % 2) * 3 + t
            row = jnp.where(core == half, t2[n // 2, n % 2 : n % 2 + 1, :], t1[n // 2, n % 2 : n % 2 + 1, :])
            out_ref[z, t : t + 1, :] = row[:, :D]
            tail.append(row[:, D:])
        out_ref[z, 3:4, :] = jnp.concatenate(tail, axis=1)
        for h in range(2):
            block = slice(z * HALF, (z + 1) * HALF)
            out_ref[z, 4:5, h * HALF : (h + 1) * HALF] = jnp.where(core == h, u2[0:1, block], u1[0:1, block])
        half, kind = z % 2, z // 2
        out_ref[z, 5:6, 0:HALF] = jnp.where(core == half, q2[kind : kind + 1, :], q1[kind : kind + 1, :])
        out_ref[z, 5:6, HALF:] = jnp.zeros((1, HALF), f32)
        out_ref[z, 6:7, :] = proj_ref[0:1, :]
        out_ref[z, 7:8, :] = fc2_ref[0:1, :]


def pack_small(idx, *arrays):
    return pl.pallas_call(
        pack_small_body,
        in_specs=[SMEM] + [VMEM] * 8,
        out_specs=VMEM,
        out_shape=jax.ShapeDtypeStruct((4, 8, D), f32),
        compiler_params=params(),
        cost_estimate=SHORT,
        name="pack_small",
    )(idx, *arrays)


def back_cond_body(idx_ref, long_ref, valid_ref, mid_ref, entry_ref, slope_ref, own, fetched, peer,
                   out_ref, held1, held2, sems):
    copies = bring(
        ada_copies(idx_ref, own, 0, stacked(fetched), held1)
        + ada_copies(idx_ref, own, 1, stacked(peer), held2),
        sems,
    )
    go(copies)
    core = idx_ref[2]
    slots = MICRO * NSEG
    row = lax.broadcasted_iota(jnp.int32, (slots, 1), 0)
    upper = row < NSEG
    is_long = jnp.where(upper, long_ref[0], long_ref[1]) > 0
    valid = jnp.zeros((slots, 1), f32)
    for n in range(slots):
        valid = jnp.where(row == n, valid_ref[n // NSEG, n % NSEG].astype(f32), valid)
    lead = (row == 0) | (row == NSEG)
    blocks = []
    for j in range(6):
        value = entry_ref[j] if j < 2 else mid_ref[j]
        if j % 3 == 2:
            value = value * valid
        total = jnp.where(
            upper,
            jnp.sum(value[:NSEG], axis=0, keepdims=True),
            jnp.sum(value[NSEG:], axis=0, keepdims=True),
        )
        value = jnp.where(is_long, jnp.where(lead, total, 0.0), value).astype(bf16)
        blocks += [value[:, :HALF], value[:, HALF:]]
    ready(copies)
    for held, half in ((held1, 1 - core), (held2, core)):
        grad = jnp.zeros((slots, HALF), f32)
        for z in range(4):
            for c in range(3):
                grad += dot(blocks[3 * z + c], held[z, c].reshape(HALF, HALF), 1, 1)
        at = pl.ds(pl.multiple_of(half * HALF, HALF), HALF)
        out_ref[0, :, pl.ds(pl.multiple_of(3 * HALF + half * HALF, HALF), HALF)] = grad * slope_ref[:, at]
    for z in range(4):
        if z:
            out_ref[z, :, 3 * HALF :] = out_ref[0, :, 3 * HALF :]
        for c in range(3):
            out_ref[z, :, c * HALF : (c + 1) * HALF] = blocks[3 * z + c].astype(f32)


def back_cond(idx, long_flag, valid_seg, mid, entry, slope, own, near, peer):
    return pl.pallas_call(
        back_cond_body,
        in_specs=[SMEM, SMEM, SMEM, VMEM, VMEM, VMEM] + [ANY] * 3,
        out_specs=VMEM,
        out_shape=jax.ShapeDtypeStruct((4, MICRO * NSEG, 5 * HALF), f32),
        scratch_shapes=[
            pltpu.VMEM((4, 3, 2, 4, UR, HALF), bf16),
            pltpu.VMEM((4, 3, 2, 4, UR, HALF), bf16),
            pltpu.SemaphoreType.DMA((78,)),
        ],
        compiler_params=params(),
        cost_estimate=SHORT,
        name="back_cond",
    )(idx, long_flag, valid_seg, mid, entry, slope, own, near, peer)


def finish_ff_body(idx_ref, mine_ref, peer_ref, fc1_ref, fc2_ref):
    spot, core = idx_ref[1], idx_ref[2]
    for source, half in ((mine_ref, core), (peer_ref, 1 - core)):
        for j in range(4):
            place_at = lax.bitwise_xor(spot, j)
            low, high = lax.rem(place_at, 2), lax.div(place_at, 2)
            row = pl.multiple_of((2 * low + high) * 48, 16)
            for z in range(4):
                source_rows = pl.ds(48 * (z // 2), 48)
                block = source[j, source_rows, (z % 2) * HALF : (z % 2 + 1) * HALF]
                column = pl.multiple_of((2 * z + half) * HALF, 128)
                fc1_ref[pl.ds(row, 48), pl.ds(column, HALF)] = block.astype(f32)
            row = pl.multiple_of(half * HALF + (2 * high + low) * 96, 16)
            fc2_ref[pl.ds(row, 96), :] = source[j, 96:192, :].astype(f32)


def finish_ff(idx, mine, peer):
    vmem = pl.BlockSpec(memory_space=pltpu.VMEM)
    return pl.pallas_call(
        finish_ff_body,
        in_specs=[pl.BlockSpec(memory_space=pltpu.SMEM), vmem, vmem],
        out_specs=[vmem, vmem],
        out_shape=[jax.ShapeDtypeStruct((D // 4, FF), f32), jax.ShapeDtypeStruct((FF // 4, D), f32)],
        compiler_params=params(),
        cost_estimate=SHORT,
        name="finish_ff",
    )(idx, mine, peer)


def finish_attn_body(idx_ref, mine_ref, peer_ref, qkv_ref, proj_ref):
    spot, core = idx_ref[1], idx_ref[2]
    for source, half in ((mine_ref, core), (peer_ref, 1 - core)):
        column = half * HALF
        for j in range(4):
            place_at = lax.bitwise_xor(spot, j)
            low, high = lax.rem(place_at, 2), lax.div(place_at, 2)
            row0 = pl.multiple_of((2 * low + high) * 48, 16)
            row1 = pl.multiple_of((2 * high + low) * 48, 16)
            for t in range(4):
                block = source[j, 48 * (t // 2) : 48 * (t // 2 + 1), (t % 2) * HALF : (t % 2 + 1) * HALF].astype(f32)
                row = row0 if t < 2 else row1
                if t < 3:
                    qkv_ref[pl.ds(row, 48), pl.ds(pl.multiple_of(t * D + column, 128), HALF)] = block
                else:
                    proj_ref[pl.ds(row, 48), pl.ds(pl.multiple_of(column, 128), HALF)] = block


def finish_attn(idx, mine, peer):
    vmem = pl.BlockSpec(memory_space=pltpu.VMEM)
    return pl.pallas_call(
        finish_attn_body,
        in_specs=[pl.BlockSpec(memory_space=pltpu.SMEM), vmem, vmem],
        out_specs=[vmem, vmem],
        out_shape=[jax.ShapeDtypeStruct((D // 4, 3 * D), f32), jax.ShapeDtypeStruct((D // 4, D), f32)],
        compiler_params=params(),
        cost_estimate=SHORT,
        name="finish_attn",
    )(idx, mine, peer)


def swap(array, bit):
    count = lax.axis_size("dp")
    return lax.ppermute(array, "dp", [(i, i ^ bit) for i in range(count)])


def shift(array, step):
    count = lax.axis_size("mod")
    return lax.ppermute(array, "mod", [(i, (i + step) % count) for i in range(count)])


def take(array, index, size, axis=0):
    return lax.dynamic_slice_in_dim(array, index * size, size, axis)


def after(value, *earlier):
    return lax.optimization_barrier((value, *earlier))[0]


def fence(*values):
    return lax.optimization_barrier(values)


def around(piece):
    return [shift(piece, k) for k in range(1, 4)]


def three(near):
    return [near, swap(near, 2), swap(near, 4), swap(near, 6)]


def add(*terms):
    total = terms[0].astype(f32)
    for term in terms[1:]:
        total = total + term.astype(f32)
    return total.astype(bf16)


def spread_chips(grad):
    bit = 8
    while bit < lax.axis_size("dp"):
        grad = add(grad, swap(grad, bit))
        bit *= 2
    return grad


def pick_mod(grad, index):
    return lax.dynamic_index_in_dim(grad, index, 0, keepdims=False)


def local(
    block_input,
    grad_out,
    long_flag,
    valid_mask,
    labels,
    tsteps,
    time_table,
    class_table,
    w_ada,
    b_ada,
    w_qkv,
    qv_bias,
    w_proj,
    proj_bias,
    w_fc1,
    fc1_bias,
    w_fc2,
    fc2_bias,
    rel_table,
):
    mods_n = lax.axis_size("mod")
    me = lax.axis_index("mod")
    core = lax.axis_index("dp") % 2
    spot = (lax.axis_index("dp") // 2) % 4
    idx = jnp.stack([me, spot, core]).astype(jnp.int32)
    first = 1 - core
    slots_n = MICRO * NSEG

    own_a, piece_a = pick_entry(idx, w_qkv, w_proj)
    step_flat = tsteps.reshape(slots_n)
    label_flat = labels.reshape(slots_n)
    cond = time_table[step_flat].astype(f32) + class_table[label_flat].astype(f32)
    sigma = jax.nn.sigmoid(cond)
    act = (cond * sigma).astype(bf16)
    slope = sigma * (1.0 + cond * (1.0 - sigma))
    digits = jnp.stack([step_flat // 32, step_flat % 32, label_flat // 32, label_flat % 32], axis=1).astype(bf16)
    digits = jnp.pad(digits, ((0, 0), (0, 124)))
    rel_shape = rel_table.shape
    small = jnp.concatenate(
        [qv_bias, proj_bias, fc1_bias, fc2_bias, jnp.pad(rel_table, ((0, 0), (0, 1))).reshape(-1)]
    ).reshape(slots_n, -1)
    packet = jnp.concatenate([act, digits, small], axis=1)
    group = jnp.stack([packet] + [shift(packet, k) for k in range(1, mods_n)])
    near_a = jnp.stack(around(piece_a))
    group_act = group[:, :, :D].reshape(mods_n * slots_n, D)
    columns = jnp.dot(group_act, w_ada, preferred_element_type=f32) + b_ada.astype(f32)
    columns = columns.reshape(mods_n, slots_n, -1)
    own_1, own_2, piece_b = pick_ff(idx, w_fc1, w_fc2)
    near_a, columns, piece_b, group = fence(near_a, columns, piece_b, group)
    set_a = three(near_a)
    got_b = around(piece_b)
    back = [columns[0]] + [shift(columns[k], mods_n - k) for k in range(1, mods_n)]
    act_all = lax.all_gather(
        group[:, :, : D + 128].reshape(mods_n * slots_n, D + 128), "dp", axis=0, tiled=True
    )
    act_all, *rest = fence(act_all, *set_a, *back)
    set_a, back = jnp.stack(rest[:4]), rest[4:]
    turn = (mods_n - me) % mods_n
    modulation = lax.dynamic_slice_in_dim(jnp.stack(back + back), turn, mods_n, 0)
    modulation = modulation.transpose(1, 0, 2).reshape(MICRO, NSEG, 6, D)
    long_one = long_flag.reshape(MICRO)
    is_long = long_one[:, None, None, None] > 0
    seg_mod = jnp.where(is_long, modulation[:, :1], modulation)
    valid_seg = valid_mask.reshape(MICRO, NSEG, SEG)[:, :, 0]
    valid = valid_seg.astype(f32)[:, :, None, None]
    is_gate = (jnp.arange(6) % 3 == 2)[None, None, :, None]
    mods = jnp.where(is_gate, seg_mod * valid, seg_mod).reshape(slots_n, 6, D).transpose(1, 0, 2)

    rows_small = group[:, :, D + 128 :][::-1]
    rows_small = lax.dynamic_slice_in_dim(jnp.concatenate([rows_small, rows_small]), (mods_n - 1 - me) % mods_n, mods_n, 0)
    rows_small = rows_small.reshape(mods_n, -1).astype(f32)
    cuts = [0]
    for bias in (qv_bias, proj_bias, fc1_bias, fc2_bias):
        cuts.append(cuts[-1] + bias.shape[0])
    full_qv = rows_small[:, cuts[0] : cuts[1]].reshape(-1)
    full_proj_b = rows_small[:, cuts[1] : cuts[2]].reshape(1, -1)
    full_fc1_b = rows_small[:, cuts[2] : cuts[3]].reshape(mods_n, 2, HALF)
    full_fc2_b = rows_small[:, cuts[3] : cuts[4]].reshape(1, -1)
    full_rel = rows_small[:, cuts[4] :].reshape(2, H // 4, 2, 2 * L)
    bias_thirds = jnp.concatenate([full_qv[:D], jnp.zeros((D,), f32), full_qv[D:]]).reshape(3, 2, HALF)

    def by_half(array, axis):
        one, two = (lax.index_in_dim(array, n, axis, keepdims=False) for n in (0, 1))
        return jnp.where(core > 0, one, two), jnp.where(core > 0, two, one)

    qkv_b = [b.reshape(1, 3 * HALF) for b in by_half(bias_thirds, 1)]
    fc1_b = [b.reshape(1, FH) for b in by_half(full_fc1_b, 1)]
    rel = by_half(full_rel, 0)

    x = block_input.reshape(T, D)
    dy = grad_out.reshape(T, D)
    peer_a = swap(set_a, 1)
    a, qkv1 = qkv_first(idx, x, mods, qkv_b[0], own_a, set_a)
    o1, p1 = attend(qkv1, rel[0], long_one, valid_seg)
    a, o1, peer_a = fence(a, o1, peer_a)
    qkv2 = qkv_second(idx, a, qkv_b[1], own_a, peer_a)
    o2, p2 = attend(qkv2, rel[1], long_one, valid_seg)
    o2, *got_b = fence(o2, *got_b)
    near_b = jnp.stack([g[0] for g in got_b])
    diag_b = jnp.stack([g[1] for g in got_b])
    side_b = [swap(near_b, 2), swap(near_b, 4)]
    hidden, m_in, attn, d_mlp, db_fc2 = middle(idx, o1, o2, full_proj_b, x, dy, mods, own_a, set_a, peer_a)
    m_in, near_b, diag_b, *side_b = fence(m_in, near_b, diag_b, *side_b)
    set_b = jnp.stack([near_b, *side_b, diag_b])
    peer_b = swap(set_b, 1)
    own_c, piece_c = pick_ada(idx, w_ada)
    piece_c, m_in = fence(piece_c, m_in)
    got_c = around(piece_c)
    acc_o, acc_d, dw1_send, dw2_send, db1_first = mlp(idx, m_in, d_mlp, fc1_b[0], own_1, own_2, set_b)
    acc_o, peer_b, *got_c = fence(acc_o, peer_b, *got_c)
    near_c = jnp.stack(got_c)
    set_c = three(near_c)
    from_core = [swap(dw1_send, 1), swap(dw2_send, 1)]
    ff, dm, dw1_keep, dw2_keep, db1_second = mlp(
        idx, m_in, d_mlp, fc1_b[1], own_1, own_2, peer_b, (acc_o, acc_d)
    )
    ff, dw1_keep, dw2_keep, *rest = fence(ff, dw1_keep, dw2_keep, *from_core, *set_c)
    from_core, set_c = rest[:2], jnp.stack(rest[2:])

    side_x, side_y = spot % 2, spot // 2

    def cut(terms, side):
        size = terms[0].shape[1] // 2
        return [take(term, side, size, 1) for term in terms]

    terms_1 = [g.reshape(mods_n, D // mods_n, FH) for g in (dw1_keep, from_core[0])]
    terms_2 = [g.reshape(mods_n, HALF, D) for g in (dw2_keep, from_core[1])]
    in_1 = swap(add(*cut(terms_1, 1 - side_x)), 2)
    in_2 = swap(add(*cut(terms_2, 1 - side_y)), 4)
    y, d_h, do1, do2, dwp_send, dwp_keep, dmod_mid, db_proj = back_middle(
        idx, hidden, dy, ff, full_fc2_b, dm, attn, mods, o1, o2, own_a, set_a, peer_a
    )
    dq1, dk1, dv1, dt1, dbq1 = attend_back(qkv1, p1, do1, o1, SHORT)
    dwq_send = qkv_weight(a, dq1, dk1, dv1, SHORT)
    in_1, in_2, dwq_send, do2, set_c = fence(in_1, in_2, dwq_send, do2, set_c)
    terms_1 = cut(terms_1, side_x) + [in_1]
    terms_2 = cut(terms_2, side_y) + [in_2]
    far_in_1 = swap(add(*cut(terms_1, 1 - side_y)), 4)
    far_in_2 = swap(add(*cut(terms_2, 1 - side_x)), 2)
    peer_c = swap(set_c, 1)
    dwq_in = swap(dwq_send, 1)
    dwp_in = swap(dwp_send, 1)
    dq2, dk2, dv2, dt2, dbq2 = attend_back(qkv2, p2, do2, o2, LONG)
    dq2, dk2, dv2, dt2, dbq2, far_in_1, far_in_2, peer_c, dwq_in, dwp_in = fence(
        dq2, dk2, dv2, dt2, dbq2, far_in_1, far_in_2, peer_c, dwq_in, dwp_in
    )
    kept_1 = spread_chips(add(*cut(terms_1, side_y), far_in_1))
    kept_2 = spread_chips(add(*cut(terms_2, side_x), far_in_2))
    ff_parts = jnp.concatenate([kept_1[:, :, :D], kept_1[:, :, D:], kept_2], axis=1)

    def scatter_send(grad):
        return [shift(pick_mod(grad, (me + k) % mods_n), k) for k in range(1, mods_n)]

    ff_in = scatter_send(ff_parts)
    dwq_keep = qkv_weight(a, dq2, dk2, dv2, LONG)
    packed = pack_small(idx, dbq1, dbq2, db_proj, db1_first, db1_second, db_fc2, dt1, dt2).astype(bf16)
    packed = add(packed, swap(packed, 1))

    dwq = [dwq_keep, dwq_in]
    dwp = [g.reshape(mods_n, D // mods_n, HALF) for g in (dwp_keep, dwp_in)]
    left = [g[:, :D].reshape(mods_n, D // mods_n, D) for g in dwq]
    right = [g[:, D:].reshape(mods_n, D // mods_n, HALF) for g in dwq]

    def right_add(side):
        return jnp.concatenate([add(*cut(right, side)), add(*cut(dwp, side))], axis=2)

    in_l = swap(jnp.concatenate([add(*cut(left, 1 - side_x)), packed], axis=1), 2)
    in_r = swap(right_add(1 - side_y), 4)
    dx, dmod_entry = back_entry(
        idx, (dq1, dk1, dv1, dq2, dk2, dv2), x, after(d_h, dwq_keep), mods, own_a, set_a, peer_a
    )
    d_cond = back_cond(idx, long_one, valid_seg, dmod_mid, dmod_entry, slope, own_c, set_c, peer_c).astype(bf16)
    in_l, in_r, d_cond, dx, *ff_in = fence(in_l, in_r, d_cond, dx, *ff_in)
    rows = left[0].shape[1] // 2
    left = cut(left, side_x) + [in_l[:, :rows]]
    packed = add(packed, in_l[:, rows:])
    right_mid = [right_add(side_y), in_r]
    far_l = swap(jnp.concatenate([add(*cut(left, 1 - side_y)), packed], axis=1), 4)
    far_r = swap(add(*cut(right_mid, 1 - side_x)), 2)
    cond_in = scatter_send(d_cond)
    far_l, far_r, *cond_in = fence(far_l, far_r, *cond_in)
    packed = add(packed, far_l[:, rows // 2 :])
    attn_parts = spread_chips(
        jnp.concatenate(
            [add(*cut(left, side_y), far_l[:, : rows // 2]), add(*cut(right_mid, side_x), far_r), packed], axis=1
        )
    )
    attn_in = scatter_send(attn_parts)
    everyone = lax.all_gather(jnp.concatenate([pick_mod(d_cond, me), *cond_in]), "dp", axis=0, tiled=True)
    ff_part = add(pick_mod(ff_parts, me), *ff_in)
    attn_in[0], everyone = fence(attn_in[0], everyone)
    attn_part = add(pick_mod(attn_parts, me), *attn_in)

    def gather_chips(piece):
        mine = jnp.stack(three(piece))
        return mine, swap(mine, 1)

    grad_fc1, grad_fc2 = finish_ff(idx, *gather_chips(ff_part))
    grad_qkv, grad_proj = finish_attn(idx, *gather_chips(attn_part[:D // 8]))
    small_all = attn_part[D // 8 :].astype(f32)

    width = w_ada.shape[1]
    d_mod_all = everyone[:, :width]
    d_cond_all = everyone[:, width:]
    digits_all = act_all[:, D : D + 4].astype(jnp.int32)
    grad_ada = lax.dot_general(act_all[:, :D], d_mod_all, (((0,), (0,)), ((), ())), preferred_element_type=f32)
    grad_ada_b = jnp.sum(d_mod_all.astype(f32), axis=0)

    def table_grad(high, low, rows):
        share = rows // mods_n
        index = digits_all[:, high] * 32 + digits_all[:, low]
        hot = (index[None, :] == me * share + jnp.arange(share)[:, None]).astype(bf16)
        return jnp.dot(hot, d_cond_all, preferred_element_type=f32)

    grad_rel = jnp.concatenate([small_all[:3], small_all[3].reshape(3, 2 * L - D)], axis=1)
    return (
        y.reshape(block_input.shape),
        dx.reshape(block_input.shape),
        table_grad(0, 1, time_table.shape[0]),
        table_grad(2, 3, class_table.shape[0]),
        grad_ada,
        grad_ada_b,
        grad_qkv,
        small_all[5, : qv_bias.shape[0]],
        grad_proj,
        take(small_all[6], me, proj_bias.shape[0]),
        grad_fc1,
        small_all[4],
        grad_fc2,
        take(small_all[7], me, fc2_bias.shape[0]),
        grad_rel[:, : rel_shape[1]],
    )


def solution(mesh):
    in_specs = (
        P(None, ("dp", "mod"), None),
        P(None, ("dp", "mod"), None),
        P(None, ("dp", "mod")),
        P(None, ("dp", "mod")),
        P(None, ("dp", "mod")),
        P(None, ("dp", "mod")),
        P(),
        P(),
        P(None, "mod"),
        P("mod"),
        P("mod", None),
        P("mod"),
        P("mod", None),
        P("mod"),
        P("mod", None),
        P("mod"),
        P("mod", None),
        P("mod"),
        P("mod", None),
    )
    out_specs = (
        P(None, ("dp", "mod"), None),
        P(None, ("dp", "mod"), None),
        P("mod", None),
        P("mod", None),
        P(None, "mod"),
        P("mod"),
        P("mod", None),
        P("mod"),
        P("mod", None),
        P("mod"),
        P("mod", None),
        P("mod"),
        P("mod", None),
        P("mod"),
        P("mod", None),
    )
    return jax.shard_map(local, mesh=mesh, in_specs=in_specs, out_specs=out_specs, check_vma=False)
```

```python
from functools import partial
import jax
import jax.numpy as jnp
from jax import lax
from jax.experimental import pallas as pl
from jax.experimental.pallas import tpu as pltpu
from jax.sharding import PartitionSpec as P

f32 = jnp.float32
bf16 = jnp.bfloat16
D = 768
H = 12
HD = 64
FF = 3072
L = 512
SEG = 128
NSEG = 4
MICRO = 2
T = MICRO * L
HALF = 384
FH = 1536
VMEM_LIMIT = 56 * 1024 * 1024


LONG = pl.CostEstimate(flops=30_000_000_000, bytes_accessed=1_000_000, transcendentals=0)
SHORT = pl.CostEstimate(flops=1, bytes_accessed=1, transcendentals=0)


def params(*sem):
    return pltpu.CompilerParams(vmem_limit_bytes=VMEM_LIMIT, dimension_semantics=sem)


def dot(a, b, ca=1, cb=0):
    return lax.dot_general(a, b, (((ca,), (cb,)), ((), ())), preferred_element_type=f32)


def norm_of(values):
    centred = values - jnp.mean(values, axis=1, keepdims=True)
    inverse = lax.rsqrt(jnp.mean(centred * centred, axis=1, keepdims=True) + 1e-6)
    return centred * inverse, inverse


def norm_back(grad, normed, inverse):
    return inverse * (
        grad
        - jnp.mean(grad, axis=1, keepdims=True)
        - normed * jnp.mean(grad * normed, axis=1, keepdims=True)
    )


UR = 48
ANY = pl.BlockSpec(memory_space=pl.ANY)
SMEM = pl.BlockSpec(memory_space=pltpu.SMEM)
VMEM = pl.BlockSpec(memory_space=pltpu.VMEM)


def whole(shape):
    return pl.BlockSpec(shape, lambda *_: (0,) * len(shape))


def bring(copies, sems):
    made = [pltpu.make_async_copy(source, target, sems.at[n]) for n, (source, target) in enumerate(copies)]
    return made


def go(made):
    for copy in made:
        copy.start()


def ready(made):
    for copy in made:
        copy.wait()


def quarters(idx_ref, sources):
    me, spot = idx_ref[0], idx_ref[1]
    for ref, lead, other in sources:
        for k in range(1, 4):
            yield (
                ref.at[k - 1] if lead is None else ref.at[lead, k - 1],
                lax.rem(me + 4 - k, 4),
                lax.bitwise_xor(spot, other),
            )


def pick_entry_body(idx_ref, step_ref, label_ref, w_ref, proj_ref, cond_ref, bias_ref, rel_ref, own_ref, out_ref):
    me, spot, core = idx_ref[0], idx_ref[1], idx_ref[2]
    for n, half in enumerate((1 - core, core)):
        for u in range(3):
            column = pl.multiple_of((2 * u + half) * HALF, HALF)
            own_ref[n, u] = w_ref[:, pl.ds(column, HALF)].reshape(4, UR, HALF)
        own_ref[n, 3] = proj_ref[:, pl.ds(pl.multiple_of(half * HALF, HALF), HALF)].reshape(4, UR, HALF)
    for n, q in enumerate((spot, lax.bitwise_xor(spot, 3))):
        for u in range(4):
            out_ref[4 * n + u] = own_ref[0, u, q]
    slots = MICRO * NSEG
    cond = cond_ref[...]
    act = cond / (1.0 + jnp.exp(-cond))
    row = lax.broadcasted_iota(jnp.int32, (slots, HALF), 0)
    lane = lax.broadcasted_iota(jnp.int32, (slots, HALF), 1)
    digits = jnp.zeros((slots, HALF), jnp.int32)
    for n in range(slots):
        step, label = step_ref[n // NSEG, n % NSEG], label_ref[n // NSEG, n % NSEG]
        values = (step // 32, step % 32, label // 32, label % 32)
        for m, value in enumerate(values):
            digits = jnp.where((row == n) & (lane == m), value, digits)
    rel = rel_ref[...].astype(f32)
    rel = jnp.concatenate([rel, jnp.zeros((3, 1), f32)], axis=1)
    bias = bias_ref[...].astype(f32)
    pair = jnp.broadcast_to(bias[3:4], (8, HALF))
    lane = lax.broadcasted_iota(jnp.int32, (8, HALF), 1)
    blank = jnp.zeros((8, HALF), f32)
    proj_b = jnp.concatenate([jnp.where(lane < 192, pair, 0.0), blank], axis=1)
    fc2_b = jnp.concatenate([jnp.where(lane < 192, 0.0, pair), blank], axis=1)
    proj_b = pltpu.roll(proj_b, me * 192, 1)
    fc2_b = pltpu.roll(fc2_b, lax.rem(me + 3, 4) * 192, 1)
    out_ref[8] = jnp.concatenate(
        [
            act[:, :HALF],
            act[:, HALF:],
            digits.astype(f32),
            rel[:, :HALF],
            rel[:, HALF : 2 * HALF],
            jnp.concatenate([rel[:, 2 * HALF :], jnp.zeros((3, 128), f32)], axis=1),
            bias[0:3],
            proj_b[0:1, :HALF],
            proj_b[0:1, HALF:],
            fc2_b[0:1, :HALF],
            fc2_b[0:1, HALF:],
            jnp.zeros((8, HALF), f32),
        ],
        axis=0,
    ).astype(bf16)


def pick_entry(idx, steps, labels, w, proj, cond, bias, rel):
    return pl.pallas_call(
        pick_entry_body,
        in_specs=[SMEM, SMEM, SMEM, VMEM, VMEM, VMEM, VMEM, VMEM],
        out_specs=[VMEM, VMEM],
        out_shape=[jax.ShapeDtypeStruct((2, 4, 4, UR, HALF), bf16), jax.ShapeDtypeStruct((9, UR, HALF), bf16)],
        compiler_params=params(),
        cost_estimate=SHORT,
        name="pick_entry",
    )(idx, steps, labels, w, proj, cond, bias, rel)


def pick_ff_body(idx_ref, fc1_ref, fc2_ref, own1_ref, own2_ref, piece_ref):
    spot, core = idx_ref[1], idx_ref[2]
    for n, half in enumerate((1 - core, core)):
        for z in range(4):
            column = pl.multiple_of((2 * z + half) * HALF, HALF)
            own1_ref[n, z] = fc1_ref[:, pl.ds(column, HALF)].reshape(4, UR, HALF)
        for j in range(2):
            for i in range(2):
                row = pl.multiple_of(half * HALF + i * 192, 192)
                own2_ref[n, 2 * j + i] = fc2_ref[pl.ds(row, 192), j * HALF : (j + 1) * HALF].reshape(4, UR, HALF)
    for n, q in enumerate((spot, lax.bitwise_xor(spot, 3))):
        for u in range(4):
            piece_ref[n, u] = own1_ref[0, u, q]
            piece_ref[n, 4 + u] = own2_ref[0, u, q]


def pick_ff(idx, fc1, fc2):
    return pl.pallas_call(
        pick_ff_body,
        in_specs=[SMEM, VMEM, VMEM],
        out_specs=[VMEM] * 3,
        out_shape=[
            jax.ShapeDtypeStruct((2, 4, 4, UR, HALF), bf16),
            jax.ShapeDtypeStruct((2, 4, 4, UR, HALF), bf16),
            jax.ShapeDtypeStruct((2, 8, UR, HALF), bf16),
        ],
        compiler_params=params(),
        cost_estimate=SHORT,
        name="pick_ff",
    )(idx, fc1, fc2)


def pick_ada_body(idx_ref, w_ref, own_ref, piece_ref):
    spot, core = idx_ref[1], idx_ref[2]
    for n, half in enumerate((1 - core, core)):
        for c in range(3):
            for i in range(2):
                row = pl.multiple_of(half * HALF + i * 192, 192)
                own_ref[n, 2 * c + i] = w_ref[pl.ds(row, 192), c * HALF : (c + 1) * HALF].reshape(4, UR, HALF)
    for u in range(6):
        piece_ref[u] = own_ref[0, u, spot]


def pick_ada(idx, w):
    return pl.pallas_call(
        pick_ada_body,
        in_specs=[SMEM, VMEM],
        out_specs=[VMEM, VMEM],
        out_shape=[jax.ShapeDtypeStruct((2, 6, 4, UR, HALF), bf16), jax.ShapeDtypeStruct((6, UR, HALF), bf16)],
        compiler_params=params(),
        cost_estimate=SHORT,
        name="pick_ada",
    )(idx, w)


def entry_copies(idx_ref, own, half, sources, held):
    return [(own.at[half, pl.ds(0, 3)], held.at[:, idx_ref[0]])] + [
        (ref.at[pl.ds(0, 3)], held.at[:, z, q]) for ref, z, q in quarters(idx_ref, sources)
    ]


def stacked(ref):
    return [(ref, n, n) for n in range(4)]


def proj_copies(idx_ref, own, half, at, sources, held):
    return [(own.at[half, 3], held.at[at, idx_ref[0]])] + [
        (ref.at[3], held.at[at, z, q]) for ref, z, q in quarters(idx_ref, sources)
    ]


def fc1_copies(idx_ref, own, half, sources, held):
    return [(own.at[half], held.at[:, idx_ref[0]])] + [
        (ref.at[pl.ds(0, 4)], held.at[:, z, q]) for ref, z, q in quarters(idx_ref, sources)
    ]


def fc2_copies(idx_ref, own, half, sources, held):
    return [(own.at[half, pl.ds(2 * j, 2)], held.at[j, idx_ref[0]]) for j in range(2)] + [
        (ref.at[pl.ds(4 + 2 * j, 2)], held.at[j, z, :, q]) for ref, z, q in quarters(idx_ref, sources) for j in range(2)
    ]


def ada_copies(idx_ref, own, half, sources, held):
    return [(own.at[half], held.at[:, idx_ref[0]])] + [
        (ref, held.at[:, z, q]) for ref, z, q in quarters(idx_ref, sources)
    ]


def entry_weight(held):
    return jnp.concatenate([held[u].reshape(D, HALF) for u in range(3)], axis=1)


def proj_weight(held):
    return jnp.concatenate([held[n].reshape(D, HALF) for n in range(2)], axis=1)


ENTRY_HELD = (3, 4, 4, UR, HALF)


def columns_body(w_ref, b_ref, p0, p1, p2, p3, c0, c1, c2, c3, held, sems):
    copies = bring([(p.at[8], held.at[k]) for k, p in enumerate((p0, p1, p2, p3))], sems)
    go(copies)
    ready(copies)
    slots = MICRO * NSEG
    units = [held[k].astype(f32) for k in range(4)]
    act = jnp.concatenate(
        [jnp.concatenate([u[:slots], u[slots : 2 * slots]], axis=1) for u in units], axis=0
    ).astype(bf16)
    out = dot(act, w_ref[...]) + b_ref[...].astype(f32)
    for k, c in enumerate((c0, c1, c2, c3)):
        c[...] = out[k * slots : (k + 1) * slots]


def mod_columns(w, b, payloads):
    return pl.pallas_call(
        columns_body,
        in_specs=[VMEM, VMEM] + [ANY] * 4,
        out_specs=[VMEM] * 4,
        out_shape=[jax.ShapeDtypeStruct((MICRO * NSEG, 3 * HALF), f32)] * 4,
        scratch_shapes=[pltpu.VMEM((4, UR, HALF), bf16), pltpu.SemaphoreType.DMA((4,))],
        compiler_params=params(),
        cost_estimate=SHORT,
        name="mod_columns",
    )(w, b, *payloads)


def prepare_body(idx_ref, long_ref, valid_ref, c0, c1, c2, c3, p0, p1, p2, p3,
                 mod_ref, qb1, qb2, pb_ref, ub1, ub2, fb_ref, r1, r2, cols, held, rows, sems):
    me, core = idx_ref[0], idx_ref[2]
    copies = bring([(p.at[8], held.at[lax.rem(me + 4 - k, 4)]) for k, p in enumerate((p0, p1, p2, p3))], sems)
    go(copies)
    for k, c in enumerate((c0, c1, c2, c3)):
        cols[lax.rem(me + k, 4)] = c[...]
    ready(copies)
    rows[...] = held[...].astype(f32)
    slots = MICRO * NSEG
    row = lax.broadcasted_iota(jnp.int32, (slots, 1), 0)
    upper = row < NSEG
    is_long = jnp.where(upper, long_ref[0], long_ref[1]) > 0
    valid = jnp.zeros((slots, 1), f32)
    for n in range(slots):
        valid = jnp.where(row == n, valid_ref[n // NSEG, n % NSEG].astype(f32), valid)
    for g in range(12):
        value = cols[g // 3, :, (g % 3) * HALF : (g % 3 + 1) * HALF]
        value = jnp.where(is_long, jnp.where(upper, value[0:1], value[NSEG : NSEG + 1]), value)
        if (g // 2) % 3 == 2:
            value = value * valid
        mod_ref[g // 2, :, (g % 2) * HALF : (g % 2 + 1) * HALF] = value
    for half, qb, ub, r in ((1 - core, qb1, ub1, r1), (core, qb2, ub2, r2)):
        qb[:, :HALF] = rows[half, 33:34, :]
        qb[:, HALF : 2 * HALF] = jnp.zeros((1, HALF), f32)
        qb[:, 2 * HALF :] = rows[2 + half, 33:34, :]
        for z in range(4):
            ub[:, z * HALF : (z + 1) * HALF] = jnp.where(half > 0, rows[z, 35:36, :], rows[z, 34:35, :])
        for n in range(6):
            z, t, to = 2 * half + n // 3, n % 3, slice(n % 2, n % 2 + 1)
            r[n // 2, to, :HALF] = rows[z, 24 + t : 25 + t, :]
            r[n // 2, to, HALF : 2 * HALF] = rows[z, 27 + t : 28 + t, :]
            r[n // 2, to, 2 * HALF :] = rows[z, 30 + t : 31 + t, :256]
    for ref, at in ((pb_ref, 36), (fb_ref, 38)):
        for n in range(2):
            ref[:, n * HALF : (n + 1) * HALF] = (
                rows[0, at + n : at + n + 1, :]
                + rows[1, at + n : at + n + 1, :]
                + rows[2, at + n : at + n + 1, :]
                + rows[3, at + n : at + n + 1, :]
            )


def prepare(idx, long_flag, valid_seg, columns, payloads):
    shapes = [(6, MICRO * NSEG, D), (1, 3 * HALF), (1, 3 * HALF), (1, D), (1, FH), (1, FH), (1, D),
              (3, 2, 2 * L), (3, 2, 2 * L)]
    return pl.pallas_call(
        prepare_body,
        in_specs=[SMEM] * 3 + [VMEM] * 4 + [ANY] * 4,
        out_specs=[VMEM] * 9,
        out_shape=[jax.ShapeDtypeStruct(shape, f32) for shape in shapes],
        scratch_shapes=[
            pltpu.VMEM((4, MICRO * NSEG, 3 * HALF), f32),
            pltpu.VMEM((4, UR, HALF), bf16),
            pltpu.VMEM((4, UR, HALF), f32),
            pltpu.SemaphoreType.DMA((4,)),
        ],
        compiler_params=params(),
        cost_estimate=SHORT,
        name="prepare",
    )(idx, long_flag, valid_seg, *columns, *payloads)


def qkv_first_body(idx_ref, x_ref, mod_ref, b_ref, own, fetched, a_ref, qkv_ref, held, sems):
    i = pl.program_id(0)
    copies = bring(entry_copies(idx_ref, own, 0, stacked(fetched), held), sems)

    @pl.when(i == 0)
    def _():
        go(copies)

    for s in range(NSEG):
        rows = pl.ds(s * SEG, SEG)
        at = pl.ds(i * NSEG + s, 1)
        norm, _ = norm_of(x_ref[rows, :].astype(f32))
        a_ref[rows, :] = (norm * (1.0 + mod_ref[1, at, :]) + mod_ref[0, at, :]).astype(bf16)

    @pl.when(i == 0)
    def _():
        ready(copies)

    qkv_ref[...] = (dot(a_ref[...], entry_weight(held)) + b_ref[...]).astype(bf16)


def qkv_first(idx, x, mods, b, own, near):
    return pl.pallas_call(
        qkv_first_body,
        grid=(MICRO,),
        in_specs=[
            SMEM,
            pl.BlockSpec((L, D), lambda i: (i, 0)),
            whole((6, MICRO * NSEG, D)),
            whole((1, 3 * HALF)),
            ANY, ANY,
        ],
        out_specs=[
            pl.BlockSpec((L, D), lambda i: (i, 0)),
            pl.BlockSpec((L, 3 * HALF), lambda i: (i, 0)),
        ],
        out_shape=[
            jax.ShapeDtypeStruct((T, D), bf16),
            jax.ShapeDtypeStruct((T, 3 * HALF), bf16),
        ],
        scratch_shapes=[pltpu.VMEM(ENTRY_HELD, bf16), pltpu.SemaphoreType.DMA((13,))],
        compiler_params=params("arbitrary"),
        cost_estimate=SHORT,
        name="qkv_first",
    )(idx, x, mods, b, own, near)


def qkv_second_body(idx_ref, a_ref, b_ref, own, fetched, qkv_ref, held, sems):
    copies = bring(entry_copies(idx_ref, own, 1, stacked(fetched), held), sems)

    @pl.when(pl.program_id(0) == 0)
    def _():
        go(copies)
        ready(copies)

    qkv_ref[...] = (dot(a_ref[...], entry_weight(held)) + b_ref[...]).astype(bf16)


def qkv_second(idx, a, b, own, near):
    return pl.pallas_call(
        qkv_second_body,
        grid=(MICRO,),
        in_specs=[
            SMEM,
            pl.BlockSpec((L, D), lambda i: (i, 0)),
            whole((1, 3 * HALF)),
            ANY, ANY,
        ],
        out_specs=pl.BlockSpec((L, 3 * HALF), lambda i: (i, 0)),
        out_shape=jax.ShapeDtypeStruct((T, 3 * HALF), bf16),
        scratch_shapes=[pltpu.VMEM(ENTRY_HELD, bf16), pltpu.SemaphoreType.DMA((13,))],
        compiler_params=params("arbitrary"),
        cost_estimate=SHORT,
        name="qkv_second",
    )(idx, a, b, own, near)


def lane_reverse(rows):
    at = lax.broadcasted_iota(jnp.int32, (2 * SEG, 2 * SEG), 0) + lax.broadcasted_iota(jnp.int32, (2 * SEG, 2 * SEG), 1)
    turn = (at == 2 * SEG - 2).astype(f32)
    return lax.dot_general(
        rows, turn, (((1,), (0,)), ((), ())), precision=lax.Precision.HIGHEST, preferred_element_type=f32
    )


def attend_body(long_ref, valid_ref, q_ref, k_ref, v_ref, t_ref, o_ref, p_ref, bias_ref):
    b = pl.program_id(1)

    @pl.when(b == 0)
    def _():
        windows = [t_ref[0, h : h + 1, d * SEG : (d + 2) * SEG] for h in range(2) for d in range(7)]
        windows = lane_reverse(jnp.concatenate(windows + windows[:2], axis=0))
        for h in range(2):
            for d in range(7):
                row = jnp.broadcast_to(windows[h * 7 + d : h * 7 + d + 1, :], (SEG, 2 * SEG))
                bias_ref[h, d] = pltpu.roll(row, SEG + 1, 1, stride=1, stride_axis=0)[:, :SEG]

    is_long = long_ref[b]
    lane = lax.broadcasted_iota(jnp.int32, (L, 2 * HD), 1)
    query = q_ref[...] * jnp.asarray(HD**-0.5, bf16)
    keys = k_ref[...]
    values_t = v_ref[...].T
    outs = []
    for h in range(2):
        mine = (lane < HD) if h == 0 else (lane >= HD)
        key_h = jnp.where(mine, keys, jnp.zeros_like(keys))
        for qb in range(NSEG):
            cols = pl.ds(qb * SEG, SEG)
            scores = dot(key_h, query[qb * SEG : (qb + 1) * SEG, :], 1, 1)
            parts = []
            for kb in range(NSEG):
                open_ = (valid_ref[b, kb] > 0) if kb == qb else ((valid_ref[b, kb] > 0) & (is_long > 0))
                shut = jnp.where(open_, 0.0, -1e30).astype(f32)
                parts.append(scores[kb * SEG : (kb + 1) * SEG, :] + (bias_ref[h, kb - qb + 3] + shut))
            scores = jnp.concatenate(parts, axis=0)
            top = jnp.max(scores, axis=0, keepdims=True)
            expo = jnp.exp(scores - top)
            total = jnp.sum(expo, axis=0, keepdims=True)
            p_ref[0, h, :, cols] = (expo * (1.0 / total)).astype(bf16)
        outs.append(dot(values_t[h * HD : (h + 1) * HD, :], p_ref[0, h]))
    o_ref[...] = jnp.concatenate(outs, axis=0).T.astype(bf16)


def attend(qkv, table, long_flag, valid_seg):
    pairs = 3
    return pl.pallas_call(
        attend_body,
        grid_spec=pltpu.PrefetchScalarGridSpec(
            num_scalar_prefetch=2,
            grid=(pairs, MICRO),
            in_specs=[
                pl.BlockSpec((L, 2 * HD), lambda g, b, *_: (b, g)),
                pl.BlockSpec((L, 2 * HD), lambda g, b, *_: (b, 3 + g)),
                pl.BlockSpec((L, 2 * HD), lambda g, b, *_: (b, 6 + g)),
                pl.BlockSpec((1, 2, 2 * L), lambda g, b, *_: (g, 0, 0)),
            ],
            out_specs=[
                pl.BlockSpec((L, 2 * HD), lambda g, b, *_: (b, g)),
                pl.BlockSpec((1, 2, L, L), lambda g, b, *_: (b, g, 0, 0)),
            ],
            scratch_shapes=[pltpu.VMEM((2, 7, SEG, SEG), f32)],
        ),
        out_shape=[
            jax.ShapeDtypeStruct((T, HALF), bf16),
            jax.ShapeDtypeStruct((MICRO, 6, L, L), bf16),
        ],
        compiler_params=params("arbitrary", "arbitrary"),
        cost_estimate=SHORT,
        name="attend",
    )(long_flag, valid_seg, qkv, qkv, qkv, table)


def middle_body(idx_ref, o1_ref, o2_ref, b_ref, x_ref, dy_ref, mod_ref, own, fetched, peer,
                h_ref, m_ref, attn_ref, dmlp_ref, db_ref, held, w_ref, sems):
    core = idx_ref[2]
    i = pl.program_id(0)

    @pl.when(i == 0)
    def _():
        copies = bring(
            proj_copies(idx_ref, own, 0, 1 - core, stacked(fetched), held)
            + proj_copies(idx_ref, own, 1, core, stacked(peer), held),
            sems,
        )
        go(copies)
        ready(copies)
        w_ref[...] = proj_weight(held)

    first = pl.multiple_of((1 - core) * HALF, HALF)
    second = pl.multiple_of(core * HALF, HALF)
    attn = dot(o1_ref[...], w_ref[pl.ds(first, HALF), :]) + dot(o2_ref[...], w_ref[pl.ds(second, HALF), :])
    attn = attn + b_ref[...]
    attn_ref[...] = attn.astype(bf16)
    total = jnp.zeros((1, D), f32)
    for s in range(NSEG):
        rows = pl.ds(s * SEG, SEG)
        at = pl.ds(i * NSEG + s, 1)
        hidden = x_ref[rows, :].astype(f32) + mod_ref[2, at, :] * attn[s * SEG : (s + 1) * SEG, :]
        h_ref[rows, :] = hidden
        norm, _ = norm_of(hidden)
        m_ref[rows, :] = (norm * (1.0 + mod_ref[4, at, :]) + mod_ref[3, at, :]).astype(bf16)
        dmlp = (dy_ref[rows, :].astype(f32) * mod_ref[5, at, :]).astype(bf16)
        dmlp_ref[rows, :] = dmlp
        total = total + jnp.sum(dmlp.astype(f32), axis=0, keepdims=True)

    @pl.when(pl.program_id(0) == 0)
    def _():
        db_ref[...] = jnp.zeros_like(db_ref)

    db_ref[0:1, :] += total


def middle(idx, o1, o2, b, x, dy, mods, own, one, two):
    row = lambda i: (i, 0)
    return pl.pallas_call(
        middle_body,
        grid=(MICRO,),
        in_specs=[
            SMEM,
            pl.BlockSpec((L, HALF), row),
            pl.BlockSpec((L, HALF), row),
            whole((1, D)),
            pl.BlockSpec((L, D), row),
            pl.BlockSpec((L, D), row),
            whole((6, MICRO * NSEG, D)),
        ] + [ANY] * 3,
        out_specs=[
            pl.BlockSpec((L, D), row),
            pl.BlockSpec((L, D), row),
            pl.BlockSpec((L, D), row),
            pl.BlockSpec((L, D), row),
            whole((8, D)),
        ],
        out_shape=[
            jax.ShapeDtypeStruct((T, D), f32),
            jax.ShapeDtypeStruct((T, D), bf16),
            jax.ShapeDtypeStruct((T, D), bf16),
            jax.ShapeDtypeStruct((T, D), bf16),
            jax.ShapeDtypeStruct((8, D), f32),
        ],
        scratch_shapes=[
            pltpu.VMEM((2, 4, 4, UR, HALF), bf16),
            pltpu.VMEM((D, D), bf16),
            pltpu.SemaphoreType.DMA((26,)),
        ],
        compiler_params=params("arbitrary"),
        cost_estimate=LONG,
        name="middle",
    )(idx, o1, o2, b, x, dy, mods, own, one, two)


FB = 768


def mlp_body(has_acc, idx_ref, m_ref, dmlp_ref, b_ref, own1, own2, fetched, *refs):
    if has_acc:
        acc_o, acc_d, out_o, out_d, dw1_ref, dw2_ref, db_ref, g_s, du_s, held1, held2, sems = refs
    else:
        out_o, out_d, dw1_ref, dw2_ref, db_ref, g_s, du_s, held1, held2, sems = refs
    f = pl.program_id(0)
    half_index = 1 if has_acc else 0

    @pl.when(f == 0)
    def _():
        copies = bring(
            fc1_copies(idx_ref, own1, half_index, stacked(fetched), held1)
            + fc2_copies(idx_ref, own2, half_index, stacked(fetched), held2),
            sems,
        )
        go(copies)
        ready(copies)

    w1 = jnp.concatenate([held1[2 * f + n].reshape(D, HALF) for n in range(2)], axis=1)
    w2 = jnp.concatenate([held2[j, pl.ds(2 * f, 2)].reshape(D, HALF) for j in range(2)], axis=1)
    bias = b_ref[0:1, :]
    chunk = 256
    total = jnp.zeros((1, FB), f32)
    c0 = (2.0 / jnp.pi) ** 0.5
    for r in range(T // chunk):
        rows = pl.ds(r * chunk, chunk)
        u = dot(m_ref[rows, :], w1) + bias
        dg = dot(dmlp_ref[rows, :], w2, 1, 1)
        u2 = u * u
        th = jnp.tanh(u * (c0 + (c0 * 0.044715) * u2))
        half = 0.5 + 0.5 * th
        g_s[rows, :] = (u * half).astype(bf16)
        slope = half + u * (0.5 - 0.5 * th * th) * (c0 + (3.0 * c0 * 0.044715) * u2)
        du = (dg * slope).astype(bf16)
        du_s[rows, :] = du
        total = total + jnp.sum(du.astype(f32), axis=0, keepdims=True)
    db_ref[0:1, :] = total

    @pl.when(f == 0)
    def _():
        if has_acc:
            out_o[...] = acc_o[...] + dot(g_s[...], w2)
            out_d[...] = acc_d[...] + dot(du_s[...], w1, 1, 1)
        else:
            out_o[...] = dot(g_s[...], w2)
            out_d[...] = dot(du_s[...], w1, 1, 1)

    @pl.when(f > 0)
    def _():
        out_o[...] += dot(g_s[...], w2)
        out_d[...] += dot(du_s[...], w1, 1, 1)

    dw2_ref[...] = dot(g_s[...], dmlp_ref[...], 0, 0).astype(bf16)
    dw1_ref[...] = dot(m_ref[...], du_s[...], 0, 0).astype(bf16)


def mlp(idx, m_in, dmlp, b1, own1, own2, fetched, acc=None):
    zero = lambda f: (0, 0)
    col = lambda f: (0, f)
    once = pl.Buffered(1)
    specs = [
        SMEM,
        pl.BlockSpec((T, D), zero, pipeline_mode=once),
        pl.BlockSpec((T, D), zero, pipeline_mode=once),
        pl.BlockSpec((1, FB), col),
    ] + [ANY] * 3
    args = [idx, m_in, dmlp, b1, own1, own2, fetched]
    if acc is not None:
        specs += [pl.BlockSpec((T, D), zero, pipeline_mode=once)] * 2
        args += list(acc)
    return pl.pallas_call(
        partial(mlp_body, acc is not None),
        grid=(FH // FB,),
        in_specs=specs,
        out_specs=[
            pl.BlockSpec((T, D), zero),
            pl.BlockSpec((T, D), zero),
            pl.BlockSpec((D, FB), col),
            pl.BlockSpec((FB, D), lambda f: (f, 0)),
            pl.BlockSpec((8, FB), col),
        ],
        out_shape=[
            jax.ShapeDtypeStruct((T, D), f32),
            jax.ShapeDtypeStruct((T, D), f32),
            jax.ShapeDtypeStruct((D, FH), bf16),
            jax.ShapeDtypeStruct((FH, D), bf16),
            jax.ShapeDtypeStruct((8, FH), f32),
        ],
        scratch_shapes=[
            pltpu.VMEM((T, FB), bf16),
            pltpu.VMEM((T, FB), bf16),
            pltpu.VMEM((4, 4, 4, UR, HALF), bf16),
            pltpu.VMEM((2, 4, 2, 4, UR, HALF), bf16),
            pltpu.SemaphoreType.DMA((39,)),
        ],
        compiler_params=params("arbitrary"),
        cost_estimate=LONG,
        name="mlp",
    )(*args)


def back_middle_body(idx_ref, h_ref, dy_ref, mlp_ref, b2_ref, dm_ref, attn_ref, mod_ref, o1_ref, o2_ref,
                     own, fetched, peer,
                     y_ref, dh_ref, do1_ref, do2_ref, dws_ref, dwk_ref, dmod_ref, db_ref,
                     dattn_s, dw_s, held, w_ref, sems):
    i = pl.program_id(0)
    core = idx_ref[2]
    first = pl.multiple_of((1 - core) * HALF, HALF)
    second = pl.multiple_of(core * HALF, HALF)
    copies = bring(
        proj_copies(idx_ref, own, 0, 1 - core, stacked(fetched), held)
        + proj_copies(idx_ref, own, 1, core, stacked(peer), held),
        sems,
    )

    @pl.when(i == 0)
    def _():
        go(copies)

    total = jnp.zeros((1, D), f32)
    for s in range(NSEG):
        rows = pl.ds(s * SEG, SEG)
        at = pl.ds(i * NSEG + s, 1)
        hidden = h_ref[rows, :]
        dy = dy_ref[rows, :].astype(f32)
        ff = mlp_ref[rows, :] + b2_ref[...]
        y_ref[rows, :] = (hidden + mod_ref[5, at, :] * ff).astype(bf16)
        dmod_ref[5, at, :] = jnp.sum(dy * ff, axis=0, keepdims=True)
        norm, inverse = norm_of(hidden)
        dm = dm_ref[rows, :]
        dmod_ref[3, at, :] = jnp.sum(dm, axis=0, keepdims=True)
        dmod_ref[4, at, :] = jnp.sum(dm * norm, axis=0, keepdims=True)
        dh = dy + norm_back(dm * (1.0 + mod_ref[4, at, :]), norm, inverse)
        dh_ref[rows, :] = dh
        dmod_ref[2, at, :] = jnp.sum(dh * attn_ref[rows, :].astype(f32), axis=0, keepdims=True)
        dattn = (dh * mod_ref[2, at, :]).astype(bf16)
        dattn_s[rows, :] = dattn
        total = total + jnp.sum(dattn.astype(f32), axis=0, keepdims=True)
    dattn = dattn_s[...]

    @pl.when(i == 0)
    def _():
        ready(copies)
        w_ref[...] = proj_weight(held)

    do1_ref[...] = dot(dattn, w_ref[pl.ds(first, HALF), :], 1, 1).astype(bf16)
    do2_ref[...] = dot(dattn, w_ref[pl.ds(second, HALF), :], 1, 1).astype(bf16)

    @pl.when(i == 0)
    def _():
        db_ref[...] = jnp.zeros_like(db_ref)
        dmod_ref[0:2] = jnp.zeros((2, MICRO * NSEG, D), f32)
        dw_s[...] = jnp.zeros_like(dw_s)

    db_ref[0:1, :] += total
    dw_s[pl.ds(first, HALF), :] += dot(o1_ref[...], dattn, 0, 0)
    dw_s[pl.ds(second, HALF), :] += dot(o2_ref[...], dattn, 0, 0)

    @pl.when(i == MICRO - 1)
    def _():
        dws_ref[...] = dw_s[:, pl.ds(first, HALF)].astype(bf16)
        dwk_ref[...] = dw_s[:, pl.ds(second, HALF)].astype(bf16)


def back_middle(idx, h, dy, ff, b2, dm, attn, mods, o1, o2, own, one, two):
    row = lambda i: (i, 0)
    full = pl.BlockSpec((L, D), row)
    part = pl.BlockSpec((L, HALF), row)
    modspec = whole((6, MICRO * NSEG, D))
    return pl.pallas_call(
        back_middle_body,
        grid=(MICRO,),
        in_specs=[SMEM, full, full, full, whole((1, D)), full, full, modspec, part, part] + [ANY] * 3,
        out_specs=[full, full, part, part, whole((D, HALF)), whole((D, HALF)), modspec, whole((8, D))],
        scratch_shapes=[
            pltpu.VMEM((L, D), bf16),
            pltpu.VMEM((D, D), f32),
            pltpu.VMEM((2, 4, 4, UR, HALF), bf16),
            pltpu.VMEM((D, D), bf16),
            pltpu.SemaphoreType.DMA((26,)),
        ],
        out_shape=[
            jax.ShapeDtypeStruct((T, D), bf16),
            jax.ShapeDtypeStruct((T, D), f32),
            jax.ShapeDtypeStruct((T, HALF), bf16),
            jax.ShapeDtypeStruct((T, HALF), bf16),
            jax.ShapeDtypeStruct((D, HALF), bf16),
            jax.ShapeDtypeStruct((D, HALF), bf16),
            jax.ShapeDtypeStruct((6, MICRO * NSEG, D), f32),
            jax.ShapeDtypeStruct((8, D), f32),
        ],
        compiler_params=params("arbitrary"),
        cost_estimate=LONG,
        name="back_middle",
    )(idx, h, dy, ff, b2, dm, attn, mods, o1, o2, own, one, two)


def attend_back_body(q_ref, k_ref, v_ref, p_ref, do_ref, o_ref, dq_ref, dk_ref, dv_ref, dt_ref, db_ref, acc_ref, ds_s):
    b = pl.program_id(1)

    @pl.when(b == 0)
    def _():
        acc_ref[...] = jnp.zeros_like(acc_ref)
        db_ref[...] = jnp.zeros_like(db_ref)

    lane = lax.broadcasted_iota(jnp.int32, (L, 2 * HD), 1)
    query = q_ref[...]
    keys_t = k_ref[...].T
    values = v_ref[...]
    dout = do_ref[...]
    prod = (dout.astype(f32) * o_ref[...].astype(f32)).T
    dqs, dks, dvs = [], [], []
    for h in range(2):
        mine = (lane < HD) if h == 0 else (lane >= HD)
        value_h = jnp.where(mine, values, jnp.zeros_like(values))
        delta = jnp.sum(prod[h * HD : (h + 1) * HD, :], axis=0, keepdims=True)
        for qb in range(NSEG):
            cols = slice(qb * SEG, (qb + 1) * SEG)
            dp = dot(value_h, dout[cols, :], 1, 1)
            ds = (p_ref[0, h, :, cols].astype(f32) * (dp - delta[:, cols])).astype(bf16)
            ds_s[h, :, cols] = ds
            for kb in range(NSEG):
                acc_ref[h, kb - qb + 3] += ds[kb * SEG : (kb + 1) * SEG, :].astype(f32)
        dvs.append(dot(p_ref[0, h], dout))
        dks.append(dot(ds_s[h], query))
        dqs.append(dot(keys_t[h * HD : (h + 1) * HD, :], ds_s[h]))
    low = lane < HD
    scale = HD**-0.5
    dq = (jnp.concatenate(dqs, axis=0).T * scale).astype(bf16)
    dk = (jnp.where(low, dks[0], dks[1]) * scale).astype(bf16)
    dv = jnp.where(low, dvs[0], dvs[1]).astype(bf16)
    dq_ref[...] = dq
    dk_ref[...] = dk
    dv_ref[...] = dv
    db_ref[0:1, :] += jnp.sum(dq.astype(f32), axis=0, keepdims=True)
    db_ref[1:2, :] += jnp.sum(dv.astype(f32), axis=0, keepdims=True)

    @pl.when(b == MICRO - 1)
    def _():
        sums = []
        for h in range(2):
            for d in range(7):
                wide = jnp.concatenate([acc_ref[h, d], jnp.zeros((SEG, SEG), f32)], axis=1)
                rows = SEG
                while rows > 1:
                    rows //= 2
                    wide = pltpu.roll(wide[:rows], rows, 1) + wide[rows:]
                sums.append(wide)
        sums = lane_reverse(jnp.concatenate(sums + sums[:2], axis=0))
        dt_ref[...] = jnp.zeros_like(dt_ref)
        for h in range(2):
            for d in range(7):
                dt_ref[0, h : h + 1, d * SEG : (d + 2) * SEG] += sums[h * 7 + d : h * 7 + d + 1, :]


def attend_back(qkv, p, dout, out, cost):
    col = lambda g, b: (b, g)
    part = pl.BlockSpec((L, 2 * HD), col)
    return pl.pallas_call(
        attend_back_body,
        grid=(3, MICRO),
        in_specs=[
            part,
            pl.BlockSpec((L, 2 * HD), lambda g, b: (b, 3 + g)),
            pl.BlockSpec((L, 2 * HD), lambda g, b: (b, 6 + g)),
            pl.BlockSpec((1, 2, L, L), lambda g, b: (b, g, 0, 0)),
            part,
            part,
        ],
        out_specs=[part, part, part, pl.BlockSpec((1, 8, 2 * L), lambda g, b: (g, 0, 0)),
                   pl.BlockSpec((8, 2 * HD), lambda g, b: (0, g))],
        out_shape=[jax.ShapeDtypeStruct((T, HALF), bf16)] * 3
        + [jax.ShapeDtypeStruct((3, 8, 2 * L), f32), jax.ShapeDtypeStruct((8, HALF), f32)],
        scratch_shapes=[pltpu.VMEM((2, 7, SEG, SEG), f32), pltpu.VMEM((2, L, L), bf16)],
        compiler_params=params("arbitrary", "arbitrary"),
        cost_estimate=cost,
        name="attend_back",
    )(qkv, qkv, qkv, p, dout, out)


def qkv_weight_body(a_ref, dq_ref, dk_ref, dv_ref, proj_ref, out_ref):
    a = a_ref[...]
    grads = jnp.concatenate([dq_ref[...], dk_ref[...]], axis=1)
    out_ref[0] = dot(a, grads, 0, 0).astype(bf16)
    out_ref[1, :, :HALF] = dot(a, dv_ref[...], 0, 0).astype(bf16)
    out_ref[1, :, HALF:] = proj_ref[...]


def qkv_weight(a, dq, dk, dv, proj, cost):
    return pl.pallas_call(
        qkv_weight_body,
        out_shape=jax.ShapeDtypeStruct((2, D, D), bf16),
        compiler_params=params(),
        cost_estimate=cost,
        name="qkv_weight",
    )(a, dq, dk, dv, proj)


def back_entry_body(idx_ref, long_ref, valid_ref, dq1, dk1, dv1, dq2, dk2, dv2, x_ref, dh_ref, mod_ref, mid_ref, cond_ref,
                    own, fetched, peer, own_c, fetched_c, peer_c,
                    dx_ref, out_ref, held1, held2, held3, held4, entry_ref, sems, sems_c):
    i = pl.program_id(0)
    core = idx_ref[2]
    copies_c = bring(
        ada_copies(idx_ref, own_c, 0, stacked(fetched_c), held3) + ada_copies(idx_ref, own_c, 1, stacked(peer_c), held4),
        sems_c,
    )

    @pl.when(i == 0)
    def _():
        copies = bring(
            entry_copies(idx_ref, own, 0, stacked(fetched), held1) + entry_copies(idx_ref, own, 1, stacked(peer), held2),
            sems,
        )
        go(copies)
        go(copies_c)
        ready(copies)

    one = jnp.concatenate([dq1[...], dk1[...], dv1[...]], axis=1)
    two = jnp.concatenate([dq2[...], dk2[...], dv2[...]], axis=1)
    da = dot(one, entry_weight(held1), 1, 1) + dot(two, entry_weight(held2), 1, 1)
    for s in range(NSEG):
        rows = pl.ds(s * SEG, SEG)
        at = pl.ds(i * NSEG + s, 1)
        piece = da[s * SEG : (s + 1) * SEG, :]
        norm, inverse = norm_of(x_ref[rows, :].astype(f32))
        entry_ref[0, at, :] = jnp.sum(piece, axis=0, keepdims=True)
        entry_ref[1, at, :] = jnp.sum(piece * norm, axis=0, keepdims=True)
        dx_ref[rows, :] = (
            dh_ref[rows, :] + norm_back(piece * (1.0 + mod_ref[1, at, :]), norm, inverse)
        ).astype(bf16)

    @pl.when(i == MICRO - 1)
    def _():
        ready(copies_c)
        slots = MICRO * NSEG
        row = lax.broadcasted_iota(jnp.int32, (slots, 1), 0)
        upper = row < NSEG
        is_long = jnp.where(upper, long_ref[0], long_ref[1]) > 0
        valid = jnp.zeros((slots, 1), f32)
        for n in range(slots):
            valid = jnp.where(row == n, valid_ref[n // NSEG, n % NSEG].astype(f32), valid)
        lead = (row == 0) | (row == NSEG)
        blocks = []
        for j in range(6):
            value = entry_ref[j] if j < 2 else mid_ref[j]
            if j % 3 == 2:
                value = value * valid
            total = jnp.where(
                upper,
                jnp.sum(value[:NSEG], axis=0, keepdims=True),
                jnp.sum(value[NSEG:], axis=0, keepdims=True),
            )
            value = jnp.where(is_long, jnp.where(lead, total, 0.0), value)
            blocks += [value[:, :HALF], value[:, HALF:]]
        low = [block.astype(bf16) for block in blocks]
        sides = []
        for held in (held3, held4):
            grad = jnp.zeros((slots, HALF), f32)
            for c in range(3):
                for z in range(4):
                    weight = jnp.concatenate([held[2 * c + n, z].reshape(192, HALF) for n in range(2)], axis=0)
                    grad += dot(low[3 * z + c], weight, 1, 1)
            sides.append(grad)
        swapped = core > 0
        d_act = jnp.concatenate(
            [jnp.where(swapped, sides[0], sides[1]), jnp.where(swapped, sides[1], sides[0])], axis=1
        )
        cond = cond_ref[...]
        sigma = 1.0 / (1.0 + jnp.exp(-cond))
        d_cond = d_act * (sigma * (1.0 + cond * (1.0 - sigma)))
        blank = jnp.zeros((slots, HALF), f32)
        for z in range(4):
            out_ref[z] = jnp.concatenate(
                [
                    jnp.concatenate(blocks[3 * z : 3 * z + 2], axis=1),
                    jnp.concatenate([blocks[3 * z + 2], blank], axis=1),
                    d_cond,
                    jnp.zeros((slots, D), f32),
                ],
                axis=0,
            ).astype(bf16)


def back_entry(idx, long_flag, valid_seg, parts, x, dh, mods, mid, cond, own, near, peer, own_c, near_c, peer_c):
    row = lambda i: (i, 0)
    full = pl.BlockSpec((L, D), row)
    part = pl.BlockSpec((L, HALF), row)
    slots = MICRO * NSEG
    return pl.pallas_call(
        back_entry_body,
        grid=(MICRO,),
        in_specs=[SMEM] * 3 + [part] * 6 + [full, full, whole((6, slots, D)), whole((6, slots, D)), whole((slots, D))]
        + [ANY] * 6,
        out_specs=[full, whole((4, 4 * slots, D))],
        out_shape=[jax.ShapeDtypeStruct((T, D), bf16), jax.ShapeDtypeStruct((4, 4 * slots, D), bf16)],
        scratch_shapes=[
            pltpu.VMEM(ENTRY_HELD, bf16),
            pltpu.VMEM(ENTRY_HELD, bf16),
            pltpu.VMEM((6, 4, 4, UR, HALF), bf16),
            pltpu.VMEM((6, 4, 4, UR, HALF), bf16),
            pltpu.VMEM((2, slots, D), f32),
            pltpu.SemaphoreType.DMA((26,)),
            pltpu.SemaphoreType.DMA((26,)),
        ],
        compiler_params=params("arbitrary"),
        cost_estimate=LONG,
        name="back_entry",
    )(idx, long_flag, valid_seg, *parts, x, dh, mods, mid, cond, own, near, peer, own_c, near_c, peer_c)


def pack_small_body(idx_ref, q1, q2, proj_ref, u1, u2, fc2_ref, t1, t2, out_ref):
    core = idx_ref[2]
    for z in range(4):
        half = z // 2
        tail = []
        for t in range(3):
            n = (z % 2) * 3 + t
            row = jnp.where(core == half, t2[n // 2, n % 2 : n % 2 + 1, :], t1[n // 2, n % 2 : n % 2 + 1, :])
            out_ref[z, t : t + 1, :] = row[:, :D]
            tail.append(row[:, D:])
        out_ref[z, 3:4, :] = jnp.concatenate(tail, axis=1)
        for h in range(2):
            block = slice(z * HALF, (z + 1) * HALF)
            out_ref[z, 4:5, h * HALF : (h + 1) * HALF] = jnp.where(core == h, u2[0:1, block], u1[0:1, block])
        half, kind = z % 2, z // 2
        out_ref[z, 5:6, 0:HALF] = jnp.where(core == half, q2[kind : kind + 1, :], q1[kind : kind + 1, :])
        out_ref[z, 5:6, HALF:] = jnp.zeros((1, HALF), f32)
        out_ref[z, 6:7, :] = proj_ref[0:1, :]
        out_ref[z, 7:8, :] = fc2_ref[0:1, :]


def pack_small(idx, *arrays):
    return pl.pallas_call(
        pack_small_body,
        in_specs=[SMEM] + [VMEM] * 8,
        out_specs=VMEM,
        out_shape=jax.ShapeDtypeStruct((4, 8, D), f32),
        compiler_params=params(),
        cost_estimate=SHORT,
        name="pack_small",
    )(idx, *arrays)


def finish_ff_body(idx_ref, mine_ref, peer_ref, fc1_ref, fc2_ref):
    spot, core = idx_ref[1], idx_ref[2]
    for source, half in ((mine_ref, core), (peer_ref, 1 - core)):
        for j in range(4):
            place_at = lax.bitwise_xor(spot, j)
            row = pl.multiple_of(place_at * 48, 16)
            for z in range(4):
                source_rows = pl.ds(48 * (z // 2), 48)
                block = source[j, source_rows, (z % 2) * HALF : (z % 2 + 1) * HALF]
                column = pl.multiple_of((2 * z + half) * HALF, 128)
                fc1_ref[pl.ds(row, 48), pl.ds(column, HALF)] = block.astype(f32)
            row = pl.multiple_of(half * HALF + place_at * 96, 16)
            fc2_ref[pl.ds(row, 96), :] = source[j, 96:192, :].astype(f32)


def finish_ff(idx, mine, peer):
    vmem = pl.BlockSpec(memory_space=pltpu.VMEM)
    return pl.pallas_call(
        finish_ff_body,
        in_specs=[pl.BlockSpec(memory_space=pltpu.SMEM), vmem, vmem],
        out_specs=[vmem, vmem],
        out_shape=[jax.ShapeDtypeStruct((D // 4, FF), f32), jax.ShapeDtypeStruct((FF // 4, D), f32)],
        compiler_params=params(),
        cost_estimate=SHORT,
        name="finish_ff",
    )(idx, mine, peer)


def finish_attn_body(idx_ref, mine_ref, peer_ref, qkv_ref, proj_ref):
    spot, core = idx_ref[1], idx_ref[2]
    for source, half in ((mine_ref, core), (peer_ref, 1 - core)):
        column = half * HALF
        for j in range(4):
            place_at = lax.bitwise_xor(spot, j)
            row = pl.multiple_of(place_at * 48, 16)
            for t in range(4):
                block = source[j, 48 * (t // 2) : 48 * (t // 2 + 1), (t % 2) * HALF : (t % 2 + 1) * HALF].astype(f32)
                if t < 3:
                    qkv_ref[pl.ds(row, 48), pl.ds(pl.multiple_of(t * D + column, 128), HALF)] = block
                else:
                    proj_ref[pl.ds(row, 48), pl.ds(pl.multiple_of(column, 128), HALF)] = block


def finish_attn(idx, mine, peer):
    vmem = pl.BlockSpec(memory_space=pltpu.VMEM)
    return pl.pallas_call(
        finish_attn_body,
        in_specs=[pl.BlockSpec(memory_space=pltpu.SMEM), vmem, vmem],
        out_specs=[vmem, vmem],
        out_shape=[jax.ShapeDtypeStruct((D // 4, 3 * D), f32), jax.ShapeDtypeStruct((D // 4, D), f32)],
        compiler_params=params(),
        cost_estimate=SHORT,
        name="finish_attn",
    )(idx, mine, peer)


def swap(array, bit):
    count = lax.axis_size("dp")
    return lax.ppermute(array, "dp", [(i, i ^ bit) for i in range(count)])


def shift(array, step):
    count = lax.axis_size("mod")
    return lax.ppermute(array, "mod", [(i, (i + step) % count) for i in range(count)])


def take(array, index, size, axis=0):
    return lax.dynamic_slice_in_dim(array, index * size, size, axis)


def after(value, *earlier):
    return lax.optimization_barrier((value, *earlier))[0]


def fence(*values):
    return lax.optimization_barrier(values)


def around(piece):
    return [shift(piece, k) for k in range(1, 4)]


def three(near):
    return [near, swap(near, 2), swap(near, 4), swap(near, 6)]


def add(*terms):
    total = terms[0].astype(f32)
    for term in terms[1:]:
        total = total + term.astype(f32)
    return total.astype(bf16)


def spread_chips(grad):
    bit = 8
    while bit < lax.axis_size("dp"):
        grad = add(grad, swap(grad, bit))
        bit *= 2
    return grad


def pick_mod(grad, index):
    return lax.dynamic_index_in_dim(grad, index, 0, keepdims=False)


def local(
    block_input,
    grad_out,
    long_flag,
    valid_mask,
    labels,
    tsteps,
    time_table,
    class_table,
    w_ada,
    b_ada,
    w_qkv,
    qv_bias,
    w_proj,
    proj_bias,
    w_fc1,
    fc1_bias,
    w_fc2,
    fc2_bias,
    rel_table,
):
    mods_n = lax.axis_size("mod")
    me = lax.axis_index("mod")
    core = lax.axis_index("dp") % 2
    spot = (lax.axis_index("dp") // 2) % 4
    idx = jnp.stack([me, spot, core]).astype(jnp.int32)
    slots_n = MICRO * NSEG
    x = block_input.reshape(T, D)
    dy = grad_out.reshape(T, D)
    long_one = long_flag.reshape(MICRO)
    valid_seg = valid_mask.reshape(MICRO, NSEG, SEG)[:, :, 0]

    step_flat = tsteps.reshape(slots_n)
    label_flat = labels.reshape(slots_n)
    cond = time_table[step_flat].astype(f32) + class_table[label_flat].astype(f32)
    biases = jnp.concatenate([qv_bias, fc1_bias, proj_bias, fc2_bias]).reshape(4, HALF)
    own_a, payload = pick_entry(
        idx, tsteps.reshape(MICRO, NSEG), labels.reshape(MICRO, NSEG), w_qkv, w_proj, cond, biases, rel_table
    )
    payloads = [payload] + around(payload)
    own_1, own_2, piece_b = pick_ff(idx, w_fc1, w_fc2)
    own_c, piece_c = pick_ada(idx, w_ada)
    piece_b, piece_c, payloads[0], *payloads[1:] = fence(piece_b, piece_c, *payloads)

    def sides(got, also_x=None, also_y=None):
        near = jnp.concatenate([g[0] for g in got])
        units = near.shape[0]
        outs = []
        for bit, also in ((2, also_x), (4, also_y)):
            outs.append(swap(near if also is None else jnp.concatenate([near, also]), bit))
        return near, outs, jnp.concatenate([g[1] for g in got]), units

    def assemble(near, outs, diag, units):
        return jnp.stack([near, outs[0][:units], outs[1][:units], diag]).reshape(4, 3, units // 3, UR, HALF)

    packets = jnp.stack([p[8] for p in payloads])
    set_a = list(sides([p[:8].reshape(2, 4, UR, HALF) for p in payloads[1:]], packets, packets))
    columns = mod_columns(w_ada, b_ada.reshape(1, -1), payloads)
    back = [columns[0]] + [shift(columns[k], mods_n - k) for k in range(1, mods_n)]
    got_b = around(piece_b)
    mods, qkv_b1, qkv_b2, proj_b, fc1_b1, fc1_b2, fc2_b, rel_1, rel_2 = prepare(
        idx, long_one, valid_seg, back, payloads
    )
    mods, *set_a[1] = fence(mods, *set_a[1])
    units = set_a[3]
    plane = [packets, set_a[1][0][units:], set_a[1][1][units:]]
    set_a = assemble(*set_a)
    peer_a = swap(set_a, 1)
    a, qkv1 = qkv_first(idx, x, mods, qkv_b1, own_a, set_a)
    o1, p1 = attend(qkv1, rel_1, long_one, valid_seg)
    a, o1, peer_a = fence(a, o1, peer_a)
    qkv2 = qkv_second(idx, a, qkv_b2, own_a, peer_a)
    o2, p2 = attend(qkv2, rel_2, long_one, valid_seg)
    hidden, m_in, attn, d_mlp, db_fc2 = middle(idx, o1, o2, proj_b, x, dy, mods, own_a, set_a, peer_a)
    m_in, *got_b = fence(m_in, *got_b)
    set_b = list(sides(got_b, None, plane[1]))
    m_in, piece_c, *set_b[1] = fence(m_in, piece_c, *set_b[1])
    plane = jnp.stack(plane + [set_b[1][1][set_b[3] :]])
    set_b = assemble(*set_b)
    peer_b = swap(set_b, 1)
    got_c = around(piece_c)
    acc_o, acc_d, dw1_send, dw2_send, db1_first = mlp(idx, m_in, d_mlp, fc1_b1, own_1, own_2, set_b)
    acc_o, peer_b, *got_c = fence(acc_o, peer_b, *got_c)
    set_c = three(jnp.stack(got_c))
    from_core = [swap(dw1_send, 1), swap(dw2_send, 1)]
    ff, dm, dw1_keep, dw2_keep, db1_second = mlp(
        idx, m_in, d_mlp, fc1_b2, own_1, own_2, peer_b, (acc_o, acc_d)
    )
    ff, dw1_keep, dw2_keep, *rest = fence(ff, dw1_keep, dw2_keep, *from_core, *set_c)
    from_core, set_c = rest[:2], rest[2:]

    def quarters_of(grads):
        return [g.reshape(g.shape[0], mods_n, 4, -1, g.shape[-1]) for g in grads]

    def mine(grads, other):
        return add(*[lax.dynamic_index_in_dim(g, lax.bitwise_xor(spot, other), 2, keepdims=False) for g in grads])

    dw1 = quarters_of([g[None] for g in (dw1_keep, from_core[0])])
    dw2 = quarters_of([g[None] for g in (dw2_keep, from_core[1])])

    def ff_quarter(other):
        one, two = mine(dw1, other)[0], mine(dw2, other)[0]
        return jnp.concatenate([one[:, :, :D], one[:, :, D:], two], axis=1)

    ff_plane = [swap(ff_quarter(n), 2 * n) for n in (1, 2, 3)]
    y, d_h, do1, do2, dwp_send, dwp_keep, dmod_mid, db_proj = back_middle(
        idx, hidden, dy, ff, fc2_b, dm, attn, mods, o1, o2, own_a, set_a, peer_a
    )
    dq1, dk1, dv1, dt1, dbq1 = attend_back(qkv1, p1, do1, o1, SHORT)
    dw_send = qkv_weight(a, dq1, dk1, dv1, dwp_send, SHORT)
    dq2, dk2, dv2, dt2, dbq2 = attend_back(qkv2, p2, after(do2, dw_send), o2, SHORT)
    dq2, dk2, dv2, dt2, dbq2, dw_send, dwp_keep, *ff_plane = fence(
        dq2, dk2, dv2, dt2, dbq2, dw_send, dwp_keep, *ff_plane
    )
    ff_parts = spread_chips(add(ff_quarter(0), *ff_plane))
    set_c = jnp.stack(set_c)
    peer_c = swap(set_c, 1)
    dw_in = swap(dw_send, 1)
    plane_peer = swap(plane, 1)

    def ring(step, total):
        block = pick_mod(ff_parts, (me + 2 * mods_n - 1 - step) % mods_n)
        return block if total is None else add(block, total)

    ff_ring = shift(ring(0, None), 1)
    dw_keep = qkv_weight(a, dq2, dk2, dv2, dwp_keep, LONG)
    dw_keep, dt2, dbq2, ff_ring, dw_in, peer_c, plane_peer = fence(
        dw_keep, dt2, dbq2, ff_ring, dw_in, peer_c, plane_peer
    )
    packed = pack_small(idx, dbq1, dbq2, db_proj, db1_first, db1_second, db_fc2, dt1, dt2).astype(bf16)
    packed = add(packed, swap(packed, 1))
    ff_ring = shift(ring(1, ff_ring), 1)
    d_h, ff_ring = fence(d_h, ff_ring)
    ff_ring = shift(ring(2, ff_ring), 1)

    dw = quarters_of([dw_keep, dw_in])

    def quarter(other):
        total = mine(dw, other)
        return jnp.concatenate([total[0], total[1], packed], axis=1)

    from_plane = [swap(quarter(n), 2 * n) for n in (1, 2, 3)]
    dx, d_cond = back_entry(
        idx, long_one, valid_seg, (dq1, dk1, dv1, dq2, dk2, dv2), x, d_h, mods, dmod_mid, cond,
        own_a, set_a, peer_a, own_c, set_c, peer_c
    )
    d_cond, dx, ff_ring, *from_plane = fence(d_cond, dx, ff_ring, *from_plane)
    parts = spread_chips(add(quarter(0), *from_plane))
    tail_parts = jnp.concatenate([parts, d_cond], axis=1)
    tail_in = [shift(pick_mod(tail_parts, (me + k) % mods_n), k) for k in range(1, mods_n)]
    ff_part = ring(3, ff_ring)
    ff_set = [ff_part, swap(ff_part, 2), swap(ff_part, 4)]
    def gather_chips(piece):
        mine = jnp.stack(three(piece))
        return mine, swap(mine, 1)

    *ff_set, tail_in[0], tail_in[1], tail_in[2] = fence(*ff_set, *tail_in)
    count = parts.shape[1]
    arrived = [pick_mod(tail_parts, me)] + tail_in
    part = add(*[t[:count] for t in arrived])
    rows = D // 8
    conds = [t[count : count + 3 * slots_n] for t in arrived]
    gathered = gather_chips(jnp.concatenate([part[:rows]] + conds))
    small_all = part[rows:].astype(f32)
    ff_set = jnp.stack(ff_set + [swap(ff_part, 6)])
    grad_fc1, grad_fc2 = finish_ff(idx, ff_set, swap(ff_set, 1))
    grad_qkv, grad_proj = finish_attn(idx, *gathered)

    conds = jnp.stack([g[:, rows:] for g in gathered]).reshape(-1, 3, slots_n, D)
    acts = jnp.stack([plane, plane_peer]).reshape(-1, UR, HALF)
    bit = 8
    while bit < lax.axis_size("dp"):
        conds = jnp.concatenate([conds, swap(conds, bit)])
        acts = jnp.concatenate([acts, swap(acts, bit)])
        bit *= 2
    width = w_ada.shape[1]
    d_mod_all = jnp.concatenate([conds[:, 0].reshape(-1, D), conds[:, 1].reshape(-1, D)[:, : width - D]], axis=1)
    d_cond_all = conds[:, 2].reshape(-1, D)
    act_all = jnp.concatenate(
        [acts[:, n * slots_n : (n + 1) * slots_n].reshape(-1, HALF) for n in range(2)], axis=1
    )
    digits_all = acts[:, 2 * slots_n : 3 * slots_n, :4].reshape(-1, 4).astype(jnp.int32)
    grad_ada = lax.dot_general(act_all, d_mod_all, (((0,), (0,)), ((), ())), preferred_element_type=f32)
    grad_ada_b = jnp.sum(d_mod_all.astype(f32), axis=0)

    def table_grad(high, low, rows):
        share = rows // mods_n
        index = digits_all[:, high] * 32 + digits_all[:, low]
        hot = (index[None, :] == me * share + jnp.arange(share)[:, None]).astype(bf16)
        return jnp.dot(hot, d_cond_all, preferred_element_type=f32)

    grad_rel = jnp.concatenate([small_all[:3], small_all[3].reshape(3, 2 * L - D)], axis=1)
    return (
        y.reshape(block_input.shape),
        dx.reshape(block_input.shape),
        table_grad(0, 1, time_table.shape[0]),
        table_grad(2, 3, class_table.shape[0]),
        grad_ada,
        grad_ada_b,
        grad_qkv,
        small_all[5, : qv_bias.shape[0]],
        grad_proj,
        take(small_all[6], me, proj_bias.shape[0]),
        grad_fc1,
        small_all[4],
        grad_fc2,
        take(small_all[7], me, fc2_bias.shape[0]),
        grad_rel[:, : rel_table.shape[1]],
    )


def solution(mesh):
    in_specs = (
        P(None, ("dp", "mod"), None),
        P(None, ("dp", "mod"), None),
        P(None, ("dp", "mod")),
        P(None, ("dp", "mod")),
        P(None, ("dp", "mod")),
        P(None, ("dp", "mod")),
        P(),
        P(),
        P(None, "mod"),
        P("mod"),
        P("mod", None),
        P("mod"),
        P("mod", None),
        P("mod"),
        P("mod", None),
        P("mod"),
        P("mod", None),
        P("mod"),
        P("mod", None),
    )
    out_specs = (
        P(None, ("dp", "mod"), None),
        P(None, ("dp", "mod"), None),
        P("mod", None),
        P("mod", None),
        P(None, "mod"),
        P("mod"),
        P("mod", None),
        P("mod"),
        P("mod", None),
        P("mod"),
        P("mod", None),
        P("mod"),
        P("mod", None),
        P("mod"),
        P("mod", None),
    )
    return jax.shard_map(local, mesh=mesh, in_specs=in_specs, out_specs=out_specs, check_vma=False)
```

```python
from functools import partial
import jax
import jax.numpy as jnp
from jax import lax
from jax.experimental import pallas as pl
from jax.experimental.pallas import tpu as pltpu
from jax.sharding import PartitionSpec as P

f32 = jnp.float32
bf16 = jnp.bfloat16
D = 768
H = 12
HD = 64
FF = 3072
L = 512
SEG = 128
NSEG = 4
MICRO = 2
T = MICRO * L
HALF = 384
FH = 1536
VMEM_LIMIT = 56 * 1024 * 1024


LONG = pl.CostEstimate(flops=30_000_000_000, bytes_accessed=1_000_000, transcendentals=0)
SHORT = pl.CostEstimate(flops=1, bytes_accessed=1, transcendentals=0)


def params(*sem, size=16):
    return pltpu.CompilerParams(vmem_limit_bytes=size * 1024 * 1024, dimension_semantics=sem)


def dot(a, b, ca=1, cb=0):
    return lax.dot_general(a, b, (((ca,), (cb,)), ((), ())), preferred_element_type=f32)


def norm_of(values):
    centred = values - jnp.mean(values, axis=1, keepdims=True)
    inverse = lax.rsqrt(jnp.mean(centred * centred, axis=1, keepdims=True) + 1e-6)
    return centred * inverse, inverse


def norm_back(grad, normed, inverse):
    return inverse * (
        grad
        - jnp.mean(grad, axis=1, keepdims=True)
        - normed * jnp.mean(grad * normed, axis=1, keepdims=True)
    )


UR = 48
PR = 64
ANY = pl.BlockSpec(memory_space=pltpu.HBM)
SMEM = pl.BlockSpec(memory_space=pltpu.SMEM)
VMEM = pl.BlockSpec(memory_space=pltpu.VMEM)


def whole(shape):
    return pl.BlockSpec(shape, lambda *_: (0,) * len(shape))


def bring(copies, sems):
    made = [pltpu.make_async_copy(source, target, sems.at[n]) for n, (source, target) in enumerate(copies)]
    return made


def go(made):
    for copy in made:
        copy.start()


def ready(made):
    for copy in made:
        copy.wait()


def quarters(idx_ref, sources):
    me, spot = idx_ref[0], idx_ref[1]
    for ref, lead, other in sources:
        for k in range(1, 4):
            yield (
                ref.at[k - 1] if lead is None else ref.at[lead, k - 1],
                lax.rem(me + 4 - k, 4),
                lax.bitwise_xor(spot, other),
            )


def pick_entry_body(idx_ref, w_ref, proj_ref, own_ref, out_ref):
    spot, core = idx_ref[1], idx_ref[2]
    for n, half in enumerate((1 - core, core)):
        for u in range(3):
            column = pl.multiple_of((2 * u + half) * HALF, HALF)
            own_ref[n, u] = w_ref[:, pl.ds(column, HALF)].reshape(4, UR, HALF)
        own_ref[n, 3] = proj_ref[:, pl.ds(pl.multiple_of(half * HALF, HALF), HALF)].reshape(4, UR, HALF)
    for n, q in enumerate((spot, lax.bitwise_xor(spot, 3))):
        for u in range(4):
            out_ref[n, u] = own_ref[0, u, q]


def pick_entry(idx, w, proj):
    return pl.pallas_call(
        pick_entry_body,
        in_specs=[SMEM, VMEM, VMEM],
        out_specs=[VMEM, VMEM],
        out_shape=[pltpu.HBM((2, 4, 4, UR, HALF), bf16), pltpu.HBM((2, 4, UR, HALF), bf16)],
        compiler_params=params(),
        cost_estimate=SHORT,
        name="pick_entry",
    )(idx, w, proj)


def packet_body(idx_ref, step_ref, label_ref, cond_ref, bias_ref, rel_ref, out_ref):
    me = idx_ref[0]
    slots = MICRO * NSEG
    cond = cond_ref[...]
    sigma = 1.0 / (1.0 + jnp.exp(-cond))
    act = cond / (1.0 + jnp.exp(-cond))
    slope = sigma * (1.0 + cond * (1.0 - sigma))
    row = lax.broadcasted_iota(jnp.int32, (slots, HALF), 0)
    lane = lax.broadcasted_iota(jnp.int32, (slots, HALF), 1)
    digits = jnp.zeros((slots, HALF), jnp.int32)
    for n in range(slots):
        step, label = step_ref[n // NSEG, n % NSEG], label_ref[n // NSEG, n % NSEG]
        values = (step // 32, step % 32, label // 32, label % 32)
        for m, value in enumerate(values):
            digits = jnp.where((row == n) & (lane == m), value, digits)
    rel = rel_ref[...].astype(f32)
    rel = jnp.concatenate([rel, jnp.zeros((3, 1), f32)], axis=1)
    bias = bias_ref[...].astype(f32)
    pair = jnp.broadcast_to(bias[3:4], (8, HALF))
    lane = lax.broadcasted_iota(jnp.int32, (8, HALF), 1)
    blank = jnp.zeros((8, HALF), f32)
    proj_b = jnp.concatenate([jnp.where(lane < 192, pair, 0.0), blank], axis=1)
    fc2_b = jnp.concatenate([jnp.where(lane < 192, 0.0, pair), blank], axis=1)
    proj_b = pltpu.roll(proj_b, me * 192, 1)
    fc2_b = pltpu.roll(fc2_b, lax.rem(me + 3, 4) * 192, 1)
    out_ref[...] = jnp.concatenate(
        [
            act[:, :HALF],
            act[:, HALF:],
            digits.astype(f32),
            rel[:, :HALF],
            rel[:, HALF : 2 * HALF],
            jnp.concatenate([rel[:, 2 * HALF :], jnp.zeros((3, 128), f32)], axis=1),
            bias[0:3],
            proj_b[0:1, :HALF],
            proj_b[0:1, HALF:],
            fc2_b[0:1, :HALF],
            fc2_b[0:1, HALF:],
            jnp.zeros((8, HALF), f32),
            slope[:, :HALF],
            slope[:, HALF:],
        ],
        axis=0,
    ).astype(bf16)


def make_packet(idx, steps, labels, cond, bias, rel):
    return pl.pallas_call(
        packet_body,
        in_specs=[SMEM, SMEM, SMEM, VMEM, VMEM, VMEM],
        out_specs=VMEM,
        out_shape=jax.ShapeDtypeStruct((PR, HALF), bf16),
        compiler_params=params(),
        cost_estimate=SHORT,
        name="packet",
    )(idx, steps, labels, cond, bias, rel)


def pick_ff_body(idx_ref, fc1_ref, fc2_ref, own1_ref, own2_ref, piece1_ref, piece2_ref):
    spot, core = idx_ref[1], idx_ref[2]
    for n, half in enumerate((1 - core, core)):
        for z in range(4):
            column = pl.multiple_of((2 * z + half) * HALF, HALF)
            own1_ref[n, z] = fc1_ref[:, pl.ds(column, HALF)].reshape(4, UR, HALF)
        for j in range(2):
            for i in range(2):
                row = pl.multiple_of(half * HALF + i * 192, 192)
                own2_ref[n, 2 * j + i] = fc2_ref[pl.ds(row, 192), j * HALF : (j + 1) * HALF].reshape(4, UR, HALF)
    for n, q in enumerate((spot, lax.bitwise_xor(spot, 3))):
        for u in range(4):
            piece1_ref[n, u] = own1_ref[0, u, q]
            piece2_ref[n, u] = own2_ref[0, u, q]


def pick_ff(idx, fc1, fc2):
    return pl.pallas_call(
        pick_ff_body,
        in_specs=[SMEM, VMEM, VMEM],
        out_specs=[VMEM] * 4,
        out_shape=[pltpu.HBM((2, 4, 4, UR, HALF), bf16)] * 2 + [pltpu.HBM((2, 4, UR, HALF), bf16)] * 2,
        compiler_params=params(),
        cost_estimate=SHORT,
        name="pick_ff",
    )(idx, fc1, fc2)


def entry_copies(idx_ref, own, half, sources, held):
    return [(own.at[half, pl.ds(0, 3)], held.at[:, idx_ref[0]])] + [
        (ref.at[pl.ds(0, 3)], held.at[:, z, q]) for ref, z, q in quarters(idx_ref, sources)
    ]


def stacked(ref):
    return [(ref, n, n) for n in range(4)]


def proj_copies(idx_ref, own, half, at, sources, held):
    return [(own.at[half, 3], held.at[at, idx_ref[0]])] + [
        (ref.at[3], held.at[at, z, q]) for ref, z, q in quarters(idx_ref, sources)
    ]


def fc1_copies(idx_ref, own, half, sources, held):
    return [(own.at[half], held.at[:, idx_ref[0]])] + [
        (ref, held.at[:, z, q]) for ref, z, q in quarters(idx_ref, sources)
    ]


def fc2_copies(idx_ref, own, half, sources, held):
    return [(own.at[half, pl.ds(2 * j, 2)], held.at[j, idx_ref[0]]) for j in range(2)] + [
        (ref.at[pl.ds(2 * j, 2)], held.at[j, z, :, q]) for ref, z, q in quarters(idx_ref, sources) for j in range(2)
    ]


def entry_weight(held):
    return jnp.concatenate([held[u].reshape(D, HALF) for u in range(3)], axis=1)


def proj_weight(held):
    return jnp.concatenate([held[n].reshape(D, HALF) for n in range(2)], axis=1)


ENTRY_HELD = (3, 4, 4, UR, HALF)


def columns_body(w_ref, b_ref, p0, p1, p2, p3, c0, c1, c2, c3, held, sems):
    copies = bring([(p, held.at[k]) for k, p in enumerate((p0, p1, p2, p3))], sems)
    go(copies)
    ready(copies)
    slots = MICRO * NSEG
    units = [held[k].astype(f32) for k in range(4)]
    act = jnp.concatenate(
        [jnp.concatenate([u[:slots], u[slots : 2 * slots]], axis=1) for u in units], axis=0
    ).astype(bf16)
    out = dot(act, w_ref[...]) + b_ref[...].astype(f32)
    for k, c in enumerate((c0, c1, c2, c3)):
        c[...] = out[k * slots : (k + 1) * slots]


def mod_columns(w, b, payloads):
    return pl.pallas_call(
        columns_body,
        in_specs=[VMEM, VMEM] + [ANY] * 4,
        out_specs=[VMEM] * 4,
        out_shape=[jax.ShapeDtypeStruct((MICRO * NSEG, 3 * HALF), f32)] * 4,
        scratch_shapes=[pltpu.VMEM((4, PR, HALF), bf16), pltpu.SemaphoreType.DMA((4,))],
        compiler_params=params(),
        cost_estimate=SHORT,
        name="mod_columns",
    )(w, b, *payloads)


def prepare_body(idx_ref, long_ref, valid_ref, c0, c1, c2, c3, p0, p1, p2, p3,
                 mod_ref, qb1, qb2, pb_ref, ub1, ub2, fb_ref, r1, r2, cols, held, rows, sems):
    me, core = idx_ref[0], idx_ref[2]
    copies = bring([(p, held.at[lax.rem(me + 4 - k, 4)]) for k, p in enumerate((p0, p1, p2, p3))], sems)
    go(copies)
    for k, c in enumerate((c0, c1, c2, c3)):
        cols[lax.rem(me + k, 4)] = c[...]
    ready(copies)
    rows[...] = held[...].astype(f32)
    slots = MICRO * NSEG
    row = lax.broadcasted_iota(jnp.int32, (slots, 1), 0)
    upper = row < NSEG
    is_long = jnp.where(upper, long_ref[0], long_ref[1]) > 0
    valid = jnp.zeros((slots, 1), f32)
    for n in range(slots):
        valid = jnp.where(row == n, valid_ref[n // NSEG, n % NSEG].astype(f32), valid)
    for g in range(12):
        value = cols[g // 3, :, (g % 3) * HALF : (g % 3 + 1) * HALF]
        value = jnp.where(is_long, jnp.where(upper, value[0:1], value[NSEG : NSEG + 1]), value)
        if (g // 2) % 3 == 2:
            value = value * valid
        mod_ref[g // 2, :, (g % 2) * HALF : (g % 2 + 1) * HALF] = value
    for half, qb, ub, r in ((1 - core, qb1, ub1, r1), (core, qb2, ub2, r2)):
        qb[:, :HALF] = rows[half, 33:34, :]
        qb[:, HALF : 2 * HALF] = jnp.zeros((1, HALF), f32)
        qb[:, 2 * HALF :] = rows[2 + half, 33:34, :]
        for z in range(4):
            ub[:, z * HALF : (z + 1) * HALF] = jnp.where(half > 0, rows[z, 35:36, :], rows[z, 34:35, :])
        for n in range(6):
            z, t, to = 2 * half + n // 3, n % 3, slice(n % 2, n % 2 + 1)
            r[n // 2, to, :HALF] = rows[z, 24 + t : 25 + t, :]
            r[n // 2, to, HALF : 2 * HALF] = rows[z, 27 + t : 28 + t, :]
            r[n // 2, to, 2 * HALF :] = rows[z, 30 + t : 31 + t, :256]
    for ref, at in ((pb_ref, 36), (fb_ref, 38)):
        for n in range(2):
            ref[:, n * HALF : (n + 1) * HALF] = (
                rows[0, at + n : at + n + 1, :]
                + rows[1, at + n : at + n + 1, :]
                + rows[2, at + n : at + n + 1, :]
                + rows[3, at + n : at + n + 1, :]
            )


def prepare(idx, long_flag, valid_seg, columns, payloads):
    shapes = [(6, MICRO * NSEG, D), (1, 3 * HALF), (1, 3 * HALF), (1, D), (1, FH), (1, FH), (1, D),
              (3, 2, 2 * L), (3, 2, 2 * L)]
    return pl.pallas_call(
        prepare_body,
        in_specs=[SMEM] * 3 + [VMEM] * 4 + [ANY] * 4,
        out_specs=[VMEM] * 9,
        out_shape=[jax.ShapeDtypeStruct(shape, f32) for shape in shapes],
        scratch_shapes=[
            pltpu.VMEM((4, MICRO * NSEG, 3 * HALF), f32),
            pltpu.VMEM((4, PR, HALF), bf16),
            pltpu.VMEM((4, PR, HALF), f32),
            pltpu.SemaphoreType.DMA((4,)),
        ],
        compiler_params=params(),
        cost_estimate=SHORT,
        name="prepare",
    )(idx, long_flag, valid_seg, *columns, *payloads)


def entry_norm_body(x_ref, mod_ref, a_ref):
    i = pl.program_id(0)
    for s in range(2):
        rows = pl.ds(s * SEG, SEG)
        at = pl.ds(i * 2 + s, 1)
        norm, _ = norm_of(x_ref[rows, :].astype(f32))
        a_ref[rows, :] = (norm * (1.0 + mod_ref[1, at, :]) + mod_ref[0, at, :]).astype(bf16)


def entry_norm(x, mods):
    block = pl.BlockSpec((2 * SEG, D), lambda i: (i, 0))
    return pl.pallas_call(
        entry_norm_body,
        grid=(4,),
        in_specs=[block, whole((6, MICRO * NSEG, D))],
        out_specs=block,
        out_shape=jax.ShapeDtypeStruct((T, D), bf16),
        compiler_params=params("arbitrary"),
        cost_estimate=LONG,
        name="entry_norm",
    )(x, mods)


def qkv_body(half, idx_ref, a_ref, b_ref, own, fetched, qkv_ref, held, sems):
    copies = bring(entry_copies(idx_ref, own, half, stacked(fetched), held), sems)

    @pl.when(pl.program_id(0) == 0)
    def _():
        go(copies)
        ready(copies)

    qkv_ref[...] = (dot(a_ref[...], entry_weight(held)) + b_ref[...]).astype(bf16)


def qkv_half(half, idx, a, b, own, near):
    return pl.pallas_call(
        partial(qkv_body, half),
        grid=(MICRO,),
        in_specs=[
            SMEM,
            pl.BlockSpec((L, D), lambda i: (i, 0)),
            whole((1, 3 * HALF)),
            ANY,
            ANY,
        ],
        out_specs=pl.BlockSpec((L, 3 * HALF), lambda i: (i, 0)),
        out_shape=jax.ShapeDtypeStruct((T, 3 * HALF), bf16),
        scratch_shapes=[pltpu.VMEM(ENTRY_HELD, bf16), pltpu.SemaphoreType.DMA((13,))],
        compiler_params=params("arbitrary"),
        cost_estimate=SHORT,
        name="qkv_half",
    )(idx, a, b, own, near)


def lane_reverse(rows):
    at = lax.broadcasted_iota(jnp.int32, (2 * SEG, 2 * SEG), 0) + lax.broadcasted_iota(jnp.int32, (2 * SEG, 2 * SEG), 1)
    turn = (at == 2 * SEG - 2).astype(f32)
    return lax.dot_general(
        rows, turn, (((1,), (0,)), ((), ())), precision=lax.Precision.HIGHEST, preferred_element_type=f32
    )


def attend_body(long_ref, valid_ref, q_ref, k_ref, v_ref, t_ref, o_ref, p_ref, bias_ref):
    b = pl.program_id(1)

    @pl.when(b == 0)
    def _():
        windows = [t_ref[0, h : h + 1, d * SEG : (d + 2) * SEG] for h in range(2) for d in range(7)]
        windows = lane_reverse(jnp.concatenate(windows + windows[:2], axis=0))
        for h in range(2):
            for d in range(7):
                row = jnp.broadcast_to(windows[h * 7 + d : h * 7 + d + 1, :], (SEG, 2 * SEG))
                bias_ref[h, d] = pltpu.roll(row, SEG + 1, 1, stride=1, stride_axis=0)[:, :SEG]

    is_long = long_ref[b]
    lane = lax.broadcasted_iota(jnp.int32, (L, 2 * HD), 1)
    query = q_ref[...] * jnp.asarray(HD**-0.5, bf16)
    keys = k_ref[...]
    values_t = v_ref[...].T
    outs = []
    for h in range(2):
        mine = (lane < HD) if h == 0 else (lane >= HD)
        key_h = jnp.where(mine, keys, jnp.zeros_like(keys))
        for qb in range(NSEG):
            cols = pl.ds(qb * SEG, SEG)
            scores = dot(key_h, query[qb * SEG : (qb + 1) * SEG, :], 1, 1)
            parts = []
            for kb in range(NSEG):
                open_ = (valid_ref[b, kb] > 0) if kb == qb else ((valid_ref[b, kb] > 0) & (is_long > 0))
                shut = jnp.where(open_, 0.0, -1e30).astype(f32)
                parts.append(scores[kb * SEG : (kb + 1) * SEG, :] + (bias_ref[h, kb - qb + 3] + shut))
            scores = jnp.concatenate(parts, axis=0)
            top = jnp.max(scores, axis=0, keepdims=True)
            expo = jnp.exp(scores - top)
            total = jnp.sum(expo, axis=0, keepdims=True)
            p_ref[0, h, :, cols] = (expo * (1.0 / total)).astype(bf16)
        outs.append(dot(values_t[h * HD : (h + 1) * HD, :], p_ref[0, h]))
    o_ref[...] = jnp.concatenate(outs, axis=0).T.astype(bf16)


def attend(qkv, table, long_flag, valid_seg, cost):
    pairs = 3
    return pl.pallas_call(
        attend_body,
        grid_spec=pltpu.PrefetchScalarGridSpec(
            num_scalar_prefetch=2,
            grid=(pairs, MICRO),
            in_specs=[
                pl.BlockSpec((L, 2 * HD), lambda g, b, *_: (b, g)),
                pl.BlockSpec((L, 2 * HD), lambda g, b, *_: (b, 3 + g)),
                pl.BlockSpec((L, 2 * HD), lambda g, b, *_: (b, 6 + g)),
                pl.BlockSpec((1, 2, 2 * L), lambda g, b, *_: (g, 0, 0)),
            ],
            out_specs=[
                pl.BlockSpec((L, 2 * HD), lambda g, b, *_: (b, g)),
                pl.BlockSpec((1, 2, L, L), lambda g, b, *_: (b, g, 0, 0)),
            ],
            scratch_shapes=[pltpu.VMEM((2, 7, SEG, SEG), f32)],
        ),
        out_shape=[
            jax.ShapeDtypeStruct((T, HALF), bf16),
            pltpu.HBM((MICRO, 6, L, L), bf16),
        ],
        compiler_params=params("arbitrary", "arbitrary"),
        cost_estimate=cost,
        name="attend",
    )(long_flag, valid_seg, qkv, qkv, qkv, table)


def middle_body(idx_ref, o1_ref, o2_ref, b_ref, x_ref, dy_ref, mod_ref, own, fetched, peer,
                h_ref, m_ref, attn_ref, dmlp_ref, db_ref, held, w_ref, sems):
    core = idx_ref[2]
    i = pl.program_id(0)

    @pl.when(i == 0)
    def _():
        copies = bring(
            proj_copies(idx_ref, own, 0, 1 - core, stacked(fetched), held)
            + proj_copies(idx_ref, own, 1, core, stacked(peer), held),
            sems,
        )
        go(copies)
        ready(copies)
        w_ref[...] = proj_weight(held)

    first = pl.multiple_of((1 - core) * HALF, HALF)
    second = pl.multiple_of(core * HALF, HALF)
    attn = dot(o1_ref[...], w_ref[pl.ds(first, HALF), :]) + dot(o2_ref[...], w_ref[pl.ds(second, HALF), :])
    attn = attn + b_ref[...]
    attn_ref[...] = attn.astype(bf16)
    total = jnp.zeros((1, D), f32)
    for s in range(NSEG):
        rows = pl.ds(s * SEG, SEG)
        at = pl.ds(i * NSEG + s, 1)
        hidden = x_ref[rows, :].astype(f32) + mod_ref[2, at, :] * attn[s * SEG : (s + 1) * SEG, :]
        h_ref[rows, :] = hidden
        norm, _ = norm_of(hidden)
        m_ref[rows, :] = (norm * (1.0 + mod_ref[4, at, :]) + mod_ref[3, at, :]).astype(bf16)
        dmlp = (dy_ref[rows, :].astype(f32) * mod_ref[5, at, :]).astype(bf16)
        dmlp_ref[rows, :] = dmlp
        total = total + jnp.sum(dmlp.astype(f32), axis=0, keepdims=True)

    @pl.when(pl.program_id(0) == 0)
    def _():
        db_ref[...] = jnp.zeros_like(db_ref)

    db_ref[0:1, :] += total


def middle(idx, o1, o2, b, x, dy, mods, own, one, two):
    row = lambda i: (i, 0)
    return pl.pallas_call(
        middle_body,
        grid=(MICRO,),
        in_specs=[
            SMEM,
            pl.BlockSpec((L, HALF), row),
            pl.BlockSpec((L, HALF), row),
            whole((1, D)),
            pl.BlockSpec((L, D), row),
            pl.BlockSpec((L, D), row),
            whole((6, MICRO * NSEG, D)),
        ] + [ANY] * 3,
        out_specs=[
            pl.BlockSpec((L, D), row),
            pl.BlockSpec((L, D), row),
            pl.BlockSpec((L, D), row),
            pl.BlockSpec((L, D), row),
            whole((8, D)),
        ],
        out_shape=[
            pltpu.HBM((T, D), f32),
            jax.ShapeDtypeStruct((T, D), bf16),
            pltpu.HBM((T, D), bf16),
            jax.ShapeDtypeStruct((T, D), bf16),
            jax.ShapeDtypeStruct((8, D), f32),
        ],
        scratch_shapes=[
            pltpu.VMEM((2, 4, 4, UR, HALF), bf16),
            pltpu.VMEM((D, D), bf16),
            pltpu.SemaphoreType.DMA((26,)),
        ],
        compiler_params=params("arbitrary"),
        cost_estimate=LONG,
        name="middle",
    )(idx, o1, o2, b, x, dy, mods, own, one, two)


FB = 768


def mlp_body(has_acc, idx_ref, m_ref, dmlp_ref, b_ref, own1, own2, fetched1, fetched2, *refs):
    if has_acc:
        acc_o, acc_d, out_o, out_d, dw1_ref, dw2_ref, db_ref, g_s, du_s, held1, held2, sems = refs
    else:
        out_o, out_d, dw1_ref, dw2_ref, db_ref, g_s, du_s, held1, held2, sems = refs
    f = pl.program_id(0)
    half_index = 1 if has_acc else 0

    @pl.when(f == 0)
    def _():
        copies = bring(
            fc1_copies(idx_ref, own1, half_index, stacked(fetched1), held1)
            + fc2_copies(idx_ref, own2, half_index, stacked(fetched2), held2),
            sems,
        )
        go(copies)
        ready(copies)

    w1 = jnp.concatenate([held1[2 * f + n].reshape(D, HALF) for n in range(2)], axis=1)
    w2 = jnp.concatenate([held2[j, pl.ds(2 * f, 2)].reshape(D, HALF) for j in range(2)], axis=1)
    bias = b_ref[0:1, :]
    chunk = 256
    total = jnp.zeros((1, FB), f32)
    c0 = (2.0 / jnp.pi) ** 0.5
    for r in range(T // chunk):
        rows = pl.ds(r * chunk, chunk)
        u = dot(m_ref[rows, :], w1) + bias
        dg = dot(dmlp_ref[rows, :], w2, 1, 1)
        u2 = u * u
        th = jnp.tanh(u * (c0 + (c0 * 0.044715) * u2))
        half = 0.5 + 0.5 * th
        g_s[rows, :] = (u * half).astype(bf16)
        slope = half + u * (0.5 - 0.5 * th * th) * (c0 + (3.0 * c0 * 0.044715) * u2)
        du = (dg * slope).astype(bf16)
        du_s[rows, :] = du
        total = total + jnp.sum(du.astype(f32), axis=0, keepdims=True)
    db_ref[0:1, :] = total

    @pl.when(f == 0)
    def _():
        if has_acc:
            out_o[...] = acc_o[...] + dot(g_s[...], w2)
            out_d[...] = acc_d[...] + dot(du_s[...], w1, 1, 1)
        else:
            out_o[...] = dot(g_s[...], w2)
            out_d[...] = dot(du_s[...], w1, 1, 1)

    @pl.when(f > 0)
    def _():
        out_o[...] += dot(g_s[...], w2)
        out_d[...] += dot(du_s[...], w1, 1, 1)

    dw2_ref[...] = dot(g_s[...], dmlp_ref[...], 0, 0).astype(bf16)
    dw1_ref[...] = dot(m_ref[...], du_s[...], 0, 0).astype(bf16)


def mlp(idx, m_in, dmlp, b1, own1, own2, fetched1, fetched2, acc=None):
    zero = lambda f: (0, 0)
    col = lambda f: (0, f)
    once = pl.Buffered(1)
    specs = [
        SMEM,
        pl.BlockSpec((T, D), zero, pipeline_mode=once),
        pl.BlockSpec((T, D), zero, pipeline_mode=once),
        pl.BlockSpec((1, FB), col),
    ] + [ANY] * 4
    args = [idx, m_in, dmlp, b1, own1, own2, fetched1, fetched2]
    if acc is not None:
        specs += [pl.BlockSpec((T, D), zero, pipeline_mode=once)] * 2
        args += list(acc)
    return pl.pallas_call(
        partial(mlp_body, acc is not None),
        grid=(FH // FB,),
        in_specs=specs,
        out_specs=[
            pl.BlockSpec((T, D), zero),
            pl.BlockSpec((T, D), zero),
            pl.BlockSpec((D, FB), col),
            pl.BlockSpec((FB, D), lambda f: (f, 0)),
            pl.BlockSpec((8, FB), col),
        ],
        out_shape=[
            jax.ShapeDtypeStruct((T, D), f32),
            jax.ShapeDtypeStruct((T, D), f32),
            pltpu.HBM((D, FH), bf16),
            pltpu.HBM((FH, D), bf16),
            jax.ShapeDtypeStruct((8, FH), f32),
        ],
        scratch_shapes=[
            pltpu.VMEM((T, FB), bf16),
            pltpu.VMEM((T, FB), bf16),
            pltpu.VMEM((4, 4, 4, UR, HALF), bf16),
            pltpu.VMEM((2, 4, 2, 4, UR, HALF), bf16),
            pltpu.SemaphoreType.DMA((39,)),
        ],
        compiler_params=params("arbitrary", size=44),
        cost_estimate=LONG,
        name="mlp",
    )(*args)


def back_middle_body(idx_ref, h_ref, dy_ref, mlp_ref, b2_ref, dm_ref, attn_ref, mod_ref, o1_ref, o2_ref,
                     own, fetched, peer,
                     y_ref, dh_ref, do1_ref, do2_ref, dws_ref, dwk_ref, dmod_ref, db_ref,
                     dattn_s, dw_s, held, w_ref, sems):
    i = pl.program_id(0)
    core = idx_ref[2]
    first = pl.multiple_of((1 - core) * HALF, HALF)
    second = pl.multiple_of(core * HALF, HALF)
    copies = bring(
        proj_copies(idx_ref, own, 0, 1 - core, stacked(fetched), held)
        + proj_copies(idx_ref, own, 1, core, stacked(peer), held),
        sems,
    )

    @pl.when(i == 0)
    def _():
        go(copies)

    total = jnp.zeros((1, D), f32)
    for s in range(NSEG):
        rows = pl.ds(s * SEG, SEG)
        at = pl.ds(i * NSEG + s, 1)
        hidden = h_ref[rows, :]
        dy = dy_ref[rows, :].astype(f32)
        ff = mlp_ref[rows, :] + b2_ref[...]
        y_ref[rows, :] = (hidden + mod_ref[5, at, :] * ff).astype(bf16)
        dmod_ref[5, at, :] = jnp.sum(dy * ff, axis=0, keepdims=True)
        norm, inverse = norm_of(hidden)
        dm = dm_ref[rows, :]
        dmod_ref[3, at, :] = jnp.sum(dm, axis=0, keepdims=True)
        dmod_ref[4, at, :] = jnp.sum(dm * norm, axis=0, keepdims=True)
        dh = dy + norm_back(dm * (1.0 + mod_ref[4, at, :]), norm, inverse)
        dh_ref[rows, :] = dh
        dmod_ref[2, at, :] = jnp.sum(dh * attn_ref[rows, :].astype(f32), axis=0, keepdims=True)
        dattn = (dh * mod_ref[2, at, :]).astype(bf16)
        dattn_s[rows, :] = dattn
        total = total + jnp.sum(dattn.astype(f32), axis=0, keepdims=True)
    dattn = dattn_s[...]

    @pl.when(i == 0)
    def _():
        ready(copies)
        w_ref[...] = proj_weight(held)

    do1_ref[...] = dot(dattn, w_ref[pl.ds(first, HALF), :], 1, 1).astype(bf16)
    do2_ref[...] = dot(dattn, w_ref[pl.ds(second, HALF), :], 1, 1).astype(bf16)

    @pl.when(i == 0)
    def _():
        db_ref[...] = jnp.zeros_like(db_ref)
        dmod_ref[0:2] = jnp.zeros((2, MICRO * NSEG, D), f32)
        dw_s[...] = jnp.zeros_like(dw_s)

    db_ref[0:1, :] += total
    dw_s[pl.ds(first, HALF), :] += dot(o1_ref[...], dattn, 0, 0)
    dw_s[pl.ds(second, HALF), :] += dot(o2_ref[...], dattn, 0, 0)

    @pl.when(i == MICRO - 1)
    def _():
        dws_ref[...] = dw_s[:, pl.ds(first, HALF)].astype(bf16)
        dwk_ref[...] = dw_s[:, pl.ds(second, HALF)].astype(bf16)


def back_middle(idx, h, dy, ff, b2, dm, attn, mods, o1, o2, own, one, two):
    row = lambda i: (i, 0)
    full = pl.BlockSpec((L, D), row)
    part = pl.BlockSpec((L, HALF), row)
    modspec = whole((6, MICRO * NSEG, D))
    return pl.pallas_call(
        back_middle_body,
        grid=(MICRO,),
        in_specs=[SMEM, full, full, full, whole((1, D)), full, full, modspec, part, part] + [ANY] * 3,
        out_specs=[full, full, part, part, whole((D, HALF)), whole((D, HALF)), modspec, whole((8, D))],
        scratch_shapes=[
            pltpu.VMEM((L, D), bf16),
            pltpu.VMEM((D, D), f32),
            pltpu.VMEM((2, 4, 4, UR, HALF), bf16),
            pltpu.VMEM((D, D), bf16),
            pltpu.SemaphoreType.DMA((26,)),
        ],
        out_shape=[
            pltpu.HBM((T, D), bf16),
            pltpu.HBM((T, D), f32),
            jax.ShapeDtypeStruct((T, HALF), bf16),
            jax.ShapeDtypeStruct((T, HALF), bf16),
            jax.ShapeDtypeStruct((D, HALF), bf16),
            jax.ShapeDtypeStruct((D, HALF), bf16),
            jax.ShapeDtypeStruct((6, MICRO * NSEG, D), f32),
            jax.ShapeDtypeStruct((8, D), f32),
        ],
        compiler_params=params("arbitrary", size=28),
        cost_estimate=LONG,
        name="back_middle",
    )(idx, h, dy, ff, b2, dm, attn, mods, o1, o2, own, one, two)


def attend_back_body(q_ref, k_ref, v_ref, p_ref, do_ref, o_ref, dq_ref, dk_ref, dv_ref, dt_ref, db_ref, acc_ref, ds_s):
    b = pl.program_id(1)

    @pl.when(b == 0)
    def _():
        acc_ref[...] = jnp.zeros_like(acc_ref)
        db_ref[...] = jnp.zeros_like(db_ref)

    lane = lax.broadcasted_iota(jnp.int32, (L, 2 * HD), 1)
    query = q_ref[...]
    keys_t = k_ref[...].T
    values = v_ref[...]
    dout = do_ref[...]
    prod = (dout.astype(f32) * o_ref[...].astype(f32)).T
    dqs, dks, dvs = [], [], []
    for h in range(2):
        mine = (lane < HD) if h == 0 else (lane >= HD)
        value_h = jnp.where(mine, values, jnp.zeros_like(values))
        delta = jnp.sum(prod[h * HD : (h + 1) * HD, :], axis=0, keepdims=True)
        for qb in range(NSEG):
            cols = slice(qb * SEG, (qb + 1) * SEG)
            dp = dot(value_h, dout[cols, :], 1, 1)
            ds = (p_ref[0, h, :, cols].astype(f32) * (dp - delta[:, cols])).astype(bf16)
            ds_s[h, :, cols] = ds
            for kb in range(NSEG):
                acc_ref[h, kb - qb + 3] += ds[kb * SEG : (kb + 1) * SEG, :].astype(f32)
        dvs.append(dot(p_ref[0, h], dout))
        dks.append(dot(ds_s[h], query))
        dqs.append(dot(keys_t[h * HD : (h + 1) * HD, :], ds_s[h]))
    low = lane < HD
    scale = HD**-0.5
    dq = (jnp.concatenate(dqs, axis=0).T * scale).astype(bf16)
    dk = (jnp.where(low, dks[0], dks[1]) * scale).astype(bf16)
    dv = jnp.where(low, dvs[0], dvs[1]).astype(bf16)
    dq_ref[...] = dq
    dk_ref[...] = dk
    dv_ref[...] = dv
    db_ref[0:1, :] += jnp.sum(dq.astype(f32), axis=0, keepdims=True)
    db_ref[1:2, :] += jnp.sum(dv.astype(f32), axis=0, keepdims=True)

    @pl.when(b == MICRO - 1)
    def _():
        sums = []
        for h in range(2):
            for d in range(7):
                wide = jnp.concatenate([acc_ref[h, d], jnp.zeros((SEG, SEG), f32)], axis=1)
                rows = SEG
                while rows > 1:
                    rows //= 2
                    wide = pltpu.roll(wide[:rows], rows, 1) + wide[rows:]
                sums.append(wide)
        sums = lane_reverse(jnp.concatenate(sums + sums[:2], axis=0))
        dt_ref[...] = jnp.zeros_like(dt_ref)
        for h in range(2):
            for d in range(7):
                dt_ref[0, h : h + 1, d * SEG : (d + 2) * SEG] += sums[h * 7 + d : h * 7 + d + 1, :]


def attend_back(qkv, p, dout, out, cost):
    col = lambda g, b: (b, g)
    part = pl.BlockSpec((L, 2 * HD), col)
    return pl.pallas_call(
        attend_back_body,
        grid=(3, MICRO),
        in_specs=[
            part,
            pl.BlockSpec((L, 2 * HD), lambda g, b: (b, 3 + g)),
            pl.BlockSpec((L, 2 * HD), lambda g, b: (b, 6 + g)),
            pl.BlockSpec((1, 2, L, L), lambda g, b: (b, g, 0, 0)),
            part,
            part,
        ],
        out_specs=[part, part, part, pl.BlockSpec((1, 8, 2 * L), lambda g, b: (g, 0, 0)),
                   pl.BlockSpec((8, 2 * HD), lambda g, b: (0, g))],
        out_shape=[jax.ShapeDtypeStruct((T, HALF), bf16)] * 3
        + [jax.ShapeDtypeStruct((3, 8, 2 * L), f32), jax.ShapeDtypeStruct((8, HALF), f32)],
        scratch_shapes=[pltpu.VMEM((2, 7, SEG, SEG), f32), pltpu.VMEM((2, L, L), bf16)],
        compiler_params=params("arbitrary", "arbitrary"),
        cost_estimate=cost,
        name="attend_back",
    )(qkv, qkv, qkv, p, dout, out)


def qkv_weight_body(a_ref, dq_ref, dk_ref, dv_ref, proj_ref, out_ref):
    a = a_ref[...]
    grads = jnp.concatenate([dq_ref[...], dk_ref[...]], axis=1)
    out_ref[0] = dot(a, grads, 0, 0).astype(bf16)
    out_ref[1, :, :HALF] = dot(a, dv_ref[...], 0, 0).astype(bf16)
    out_ref[1, :, HALF:] = proj_ref[...]


def qkv_weight(a, dq, dk, dv, proj, cost):
    return pl.pallas_call(
        qkv_weight_body,
        out_shape=jax.ShapeDtypeStruct((2, D, D), bf16),
        compiler_params=params(),
        cost_estimate=cost,
        name="qkv_weight",
    )(a, dq, dk, dv, proj)


def back_entry_body(idx_ref, long_ref, valid_ref, dq1, dk1, dv1, dq2, dk2, dv2, x_ref, dh_ref, mod_ref, mid_ref,
                    own, fetched, peer, dx_ref, out_ref, held1, held2, entry_ref, sems):
    i = pl.program_id(0)

    @pl.when(i == 0)
    def _():
        copies = bring(
            entry_copies(idx_ref, own, 0, stacked(fetched), held1) + entry_copies(idx_ref, own, 1, stacked(peer), held2),
            sems,
        )
        go(copies)
        ready(copies)

    one = jnp.concatenate([dq1[...], dk1[...], dv1[...]], axis=1)
    two = jnp.concatenate([dq2[...], dk2[...], dv2[...]], axis=1)
    da = dot(one, entry_weight(held1), 1, 1) + dot(two, entry_weight(held2), 1, 1)
    for s in range(NSEG):
        rows = pl.ds(s * SEG, SEG)
        at = pl.ds(i * NSEG + s, 1)
        piece = da[s * SEG : (s + 1) * SEG, :]
        norm, inverse = norm_of(x_ref[rows, :].astype(f32))
        entry_ref[0, at, :] = jnp.sum(piece, axis=0, keepdims=True)
        entry_ref[1, at, :] = jnp.sum(piece * norm, axis=0, keepdims=True)
        dx_ref[rows, :] = (
            dh_ref[rows, :] + norm_back(piece * (1.0 + mod_ref[1, at, :]), norm, inverse)
        ).astype(bf16)

    @pl.when(i == MICRO - 1)
    def _():
        slots = MICRO * NSEG
        row = lax.broadcasted_iota(jnp.int32, (slots, 1), 0)
        upper = row < NSEG
        is_long = jnp.where(upper, long_ref[0], long_ref[1]) > 0
        valid = jnp.zeros((slots, 1), f32)
        for n in range(slots):
            valid = jnp.where(row == n, valid_ref[n // NSEG, n % NSEG].astype(f32), valid)
        lead = (row == 0) | (row == NSEG)
        blocks = []
        for j in range(6):
            value = entry_ref[j] if j < 2 else mid_ref[j]
            if j % 3 == 2:
                value = value * valid
            total = jnp.where(
                upper,
                jnp.sum(value[:NSEG], axis=0, keepdims=True),
                jnp.sum(value[NSEG:], axis=0, keepdims=True),
            )
            value = jnp.where(is_long, jnp.where(lead, total, 0.0), value)
            blocks += [value[:, :HALF], value[:, HALF:]]
        blank = jnp.zeros((slots, HALF), f32)
        for z in range(4):
            out_ref[z] = jnp.concatenate(
                [
                    jnp.concatenate(blocks[3 * z : 3 * z + 2], axis=1),
                    jnp.concatenate([blocks[3 * z + 2], blank], axis=1),
                ],
                axis=0,
            ).astype(bf16)


def back_entry(idx, long_flag, valid_seg, parts, x, dh, mods, mid, own, near, peer):
    row = lambda i: (i, 0)
    full = pl.BlockSpec((L, D), row)
    part = pl.BlockSpec((L, HALF), row)
    slots = MICRO * NSEG
    return pl.pallas_call(
        back_entry_body,
        grid=(MICRO,),
        in_specs=[SMEM] * 3 + [part] * 6 + [full, full, whole((6, slots, D)), whole((6, slots, D))] + [ANY] * 3,
        out_specs=[full, whole((4, 2 * slots, D))],
        out_shape=[pltpu.HBM((T, D), bf16), jax.ShapeDtypeStruct((4, 2 * slots, D), bf16)],
        scratch_shapes=[
            pltpu.VMEM(ENTRY_HELD, bf16),
            pltpu.VMEM(ENTRY_HELD, bf16),
            pltpu.VMEM((2, slots, D), f32),
            pltpu.SemaphoreType.DMA((26,)),
        ],
        compiler_params=params("arbitrary", size=24),
        cost_estimate=LONG,
        name="back_entry",
    )(idx, long_flag, valid_seg, *parts, x, dh, mods, mid, own, near, peer)


def cond_share_body(w_ref, d0, d1, d2, d3, out_ref):
    slots = MICRO * NSEG
    rows = [d[...].astype(f32) for d in (d0, d1, d2, d3)]
    rows = [jnp.concatenate([r[:slots], r[slots:, :HALF]], axis=1) for r in rows]
    out_ref[...] = dot(jnp.concatenate(rows, axis=0).astype(bf16), w_ref[...], 1, 1).astype(bf16)


def cond_share(w, blocks):
    return pl.pallas_call(
        cond_share_body,
        in_specs=[VMEM] * 5,
        out_specs=VMEM,
        out_shape=jax.ShapeDtypeStruct((4 * MICRO * NSEG, D), bf16),
        compiler_params=params(),
        cost_estimate=SHORT,
        name="cond_share",
    )(w, *blocks)


def pack_small_body(idx_ref, q1, q2, proj_ref, u1, u2, fc2_ref, t1, t2, out_ref):
    core = idx_ref[2]
    for z in range(4):
        half = z // 2
        tail = []
        for t in range(3):
            n = (z % 2) * 3 + t
            row = jnp.where(core == half, t2[n // 2, n % 2 : n % 2 + 1, :], t1[n // 2, n % 2 : n % 2 + 1, :])
            out_ref[z, t : t + 1, :] = row[:, :D]
            tail.append(row[:, D:])
        out_ref[z, 3:4, :] = jnp.concatenate(tail, axis=1)
        for h in range(2):
            block = slice(z * HALF, (z + 1) * HALF)
            out_ref[z, 4:5, h * HALF : (h + 1) * HALF] = jnp.where(core == h, u2[0:1, block], u1[0:1, block])
        half, kind = z % 2, z // 2
        out_ref[z, 5:6, 0:HALF] = jnp.where(core == half, q2[kind : kind + 1, :], q1[kind : kind + 1, :])
        out_ref[z, 5:6, HALF:] = jnp.zeros((1, HALF), f32)
        out_ref[z, 6:7, :] = proj_ref[0:1, :]
        out_ref[z, 7:8, :] = fc2_ref[0:1, :]


def pack_small(idx, *arrays):
    return pl.pallas_call(
        pack_small_body,
        in_specs=[SMEM] + [VMEM] * 8,
        out_specs=VMEM,
        out_shape=jax.ShapeDtypeStruct((4, 8, D), f32),
        compiler_params=params(),
        cost_estimate=SHORT,
        name="pack_small",
    )(idx, *arrays)


def finish_ff_body(idx_ref, mine_ref, peer_ref, fc1_ref, fc2_ref):
    spot, core = idx_ref[1], idx_ref[2]
    for source, half in ((mine_ref, core), (peer_ref, 1 - core)):
        for j in range(4):
            place_at = lax.bitwise_xor(spot, j)
            row = pl.multiple_of(place_at * 48, 16)
            for z in range(4):
                source_rows = pl.ds(48 * (z // 2), 48)
                block = source[j, source_rows, (z % 2) * HALF : (z % 2 + 1) * HALF]
                column = pl.multiple_of((2 * z + half) * HALF, 128)
                fc1_ref[pl.ds(row, 48), pl.ds(column, HALF)] = block.astype(f32)
            row = pl.multiple_of(half * HALF + place_at * 96, 16)
            fc2_ref[pl.ds(row, 96), :] = source[j, 96:192, :].astype(f32)


def finish_ff(idx, mine, peer):
    vmem = pl.BlockSpec(memory_space=pltpu.VMEM)
    return pl.pallas_call(
        finish_ff_body,
        in_specs=[pl.BlockSpec(memory_space=pltpu.SMEM), vmem, vmem],
        out_specs=[vmem, vmem],
        out_shape=[jax.ShapeDtypeStruct((D // 4, FF), f32), jax.ShapeDtypeStruct((FF // 4, D), f32)],
        compiler_params=params(),
        cost_estimate=SHORT,
        name="finish_ff",
    )(idx, mine, peer)


def finish_attn_body(idx_ref, mine_ref, peer_ref, qkv_ref, proj_ref):
    spot, core = idx_ref[1], idx_ref[2]
    for source, half in ((mine_ref, core), (peer_ref, 1 - core)):
        column = half * HALF
        for j in range(4):
            place_at = lax.bitwise_xor(spot, j)
            row = pl.multiple_of(place_at * 48, 16)
            for t in range(4):
                block = source[j, 48 * (t // 2) : 48 * (t // 2 + 1), (t % 2) * HALF : (t % 2 + 1) * HALF].astype(f32)
                if t < 3:
                    qkv_ref[pl.ds(row, 48), pl.ds(pl.multiple_of(t * D + column, 128), HALF)] = block
                else:
                    proj_ref[pl.ds(row, 48), pl.ds(pl.multiple_of(column, 128), HALF)] = block


def finish_attn(idx, mine, peer):
    vmem = pl.BlockSpec(memory_space=pltpu.VMEM)
    return pl.pallas_call(
        finish_attn_body,
        in_specs=[pl.BlockSpec(memory_space=pltpu.SMEM), vmem, vmem],
        out_specs=[vmem, vmem],
        out_shape=[jax.ShapeDtypeStruct((D // 4, 3 * D), f32), jax.ShapeDtypeStruct((D // 4, D), f32)],
        compiler_params=params(),
        cost_estimate=SHORT,
        name="finish_attn",
    )(idx, mine, peer)


def swap(array, bit):
    count = lax.axis_size("dp")
    return lax.ppermute(array, "dp", [(i, i ^ bit) for i in range(count)])


def shift(array, step):
    count = lax.axis_size("mod")
    return lax.ppermute(array, "mod", [(i, (i + step) % count) for i in range(count)])


def take(array, index, size, axis=0):
    return lax.dynamic_slice_in_dim(array, index * size, size, axis)


def after(value, *earlier):
    return lax.optimization_barrier((value, *earlier))[0]


def fence(*values):
    return lax.optimization_barrier(values)


def around(piece):
    return [shift(piece, k) for k in range(1, 4)]


def three(near):
    return [near, swap(near, 2), swap(near, 4), swap(near, 6)]


def add(*terms):
    total = terms[0].astype(f32)
    for term in terms[1:]:
        total = total + term.astype(f32)
    return total.astype(bf16)


def spread_chips(grad):
    bit = 8
    while bit < lax.axis_size("dp"):
        grad = add(grad, swap(grad, bit))
        bit *= 2
    return grad


def pick_mod(grad, index):
    return lax.dynamic_index_in_dim(grad, index, 0, keepdims=False)


def local(
    block_input,
    grad_out,
    long_flag,
    valid_mask,
    labels,
    tsteps,
    time_table,
    class_table,
    w_ada,
    b_ada,
    w_qkv,
    qv_bias,
    w_proj,
    proj_bias,
    w_fc1,
    fc1_bias,
    w_fc2,
    fc2_bias,
    rel_table,
):
    mods_n = lax.axis_size("mod")
    me = lax.axis_index("mod")
    core = lax.axis_index("dp") % 2
    spot = (lax.axis_index("dp") // 2) % 4
    idx = jnp.stack([me, spot, core]).astype(jnp.int32)
    slots_n = MICRO * NSEG
    x = block_input.reshape(T, D)
    dy = grad_out.reshape(T, D)
    long_one = long_flag.reshape(MICRO)
    valid_seg = valid_mask.reshape(MICRO, NSEG, SEG)[:, :, 0]

    step_flat = tsteps.reshape(slots_n)
    label_flat = labels.reshape(slots_n)
    cond = time_table[step_flat].astype(f32) + class_table[label_flat].astype(f32)
    biases = jnp.concatenate([qv_bias, fc1_bias, proj_bias, fc2_bias]).reshape(4, HALF)
    own_a, piece_a = pick_entry(idx, w_qkv, w_proj)
    up_a, down_a = shift(piece_a, 1), shift(piece_a, mods_n - 1)
    own_1, own_2, piece_1, piece_2 = pick_ff(idx, w_fc1, w_fc2)
    packet = make_packet(
        idx, tsteps.reshape(MICRO, NSEG), labels.reshape(MICRO, NSEG), cond, biases, rel_table
    )
    up_a, down_a, packet, piece_1, piece_2 = fence(up_a, down_a, packet, piece_1, piece_2)
    far_a = shift(up_a, 1)
    packets = [packet] + around(packet)
    far_a, *packets = fence(far_a, *packets)

    def sides(got, also_x=None, also_y=None):
        near = jnp.concatenate([g[0] for g in got])
        units = near.shape[0]
        outs = []
        for bit, also in ((2, also_x), (4, also_y)):
            outs.append(swap(near if also is None else jnp.concatenate([near, also]), bit))
        return near, outs, jnp.concatenate([g[1] for g in got]), units

    def assemble(near, outs, diag, units):
        return jnp.stack([near, outs[0][:units], outs[1][:units], diag]).reshape(4, 3, units // 3, UR, HALF)

    shared = jnp.stack([p[:UR] for p in packets])
    near_a, side_a, diag_a, units = sides([up_a, far_a, down_a], shared, shared)
    columns = mod_columns(w_ada, b_ada.reshape(1, -1), packets)
    back = [columns[0]] + [shift(columns[k], mods_n - k) for k in range(1, mods_n)]
    mods, qkv_b1, qkv_b2, proj_b, fc1_b1, fc1_b2, fc2_b, rel_1, rel_2 = prepare(
        idx, long_one, valid_seg, back, packets
    )
    piece_1, mods = fence(piece_1, mods)
    up_1, down_1 = shift(piece_1, 1), shift(piece_1, mods_n - 1)
    a = entry_norm(x, mods)
    plane = [shared, side_a[0][units:], side_a[1][units:]]
    set_a = assemble(near_a, side_a, diag_a, units)
    qkv1 = qkv_half(0, idx, a, qkv_b1, own_a, set_a)
    qkv1, a, set_a, up_1, down_1, piece_2 = fence(qkv1, a, set_a, up_1, down_1, piece_2)
    peer_a = swap(set_a, 1)
    far_1 = shift(up_1, 1)
    up_2, down_2 = shift(piece_2, 1), shift(piece_2, mods_n - 1)
    o1, p1 = attend(qkv1, rel_1, long_one, valid_seg, LONG)
    qkv2 = qkv_half(1, idx, after(a, o1), qkv_b2, own_a, peer_a)
    qkv2, far_1, up_2, down_2 = fence(qkv2, far_1, up_2, down_2)
    set_1 = list(sides([up_1, far_1, down_1], None, plane[1]))
    far_2 = shift(up_2, 1)
    o2, p2 = attend(qkv2, rel_2, long_one, valid_seg, LONG)
    o2, far_2, *set_1[1] = fence(o2, far_2, *set_1[1])
    set_2 = list(sides([up_2, far_2, down_2]))
    hidden, m_in, attn, d_mlp, db_fc2 = middle(idx, o1, o2, proj_b, x, dy, mods, own_a, set_a, peer_a)
    m_in, *set_2[1] = fence(m_in, *set_2[1])
    plane = jnp.stack(plane + [set_1[1][1][set_1[3] :]])
    set_1, set_2 = assemble(*set_1), assemble(*set_2)
    peer_1, peer_2 = swap(set_1, 1), swap(set_2, 1)
    acc_o, acc_d, dw1_send, dw2_send, db1_first = mlp(idx, m_in, d_mlp, fc1_b1, own_1, own_2, set_1, set_2)
    acc_o, peer_1, peer_2 = fence(acc_o, peer_1, peer_2)
    from_core = [swap(dw1_send, 1), swap(dw2_send, 1)]
    ff, dm, dw1_keep, dw2_keep, db1_second = mlp(
        idx, m_in, d_mlp, fc1_b2, own_1, own_2, peer_1, peer_2, (acc_o, acc_d)
    )
    ff, dw1_keep, dw2_keep, *from_core = fence(ff, dw1_keep, dw2_keep, *from_core)

    def quarters_of(grads):
        return [g.reshape(g.shape[0], mods_n, 4, -1, g.shape[-1]) for g in grads]

    def mine(grads, other):
        return add(*[lax.dynamic_index_in_dim(g, lax.bitwise_xor(spot, other), 2, keepdims=False) for g in grads])

    dw1 = quarters_of([g[None] for g in (dw1_keep, from_core[0])])
    dw2 = [g.reshape(mods_n, HALF, D) for g in (dw2_keep, from_core[1])]

    def fc2_block(step):
        return [pick_mod(g, (me + step) % mods_n) for g in dw2]

    fc2_far = shift(add(*fc2_block(2)), 1)
    y, d_h, do1, do2, dwp_send, dwp_keep, dmod_mid, db_proj = back_middle(
        idx, hidden, dy, ff, fc2_b, dm, attn, mods, o1, o2, own_a, set_a, peer_a
    )
    do1, fc2_far = fence(do1, fc2_far)
    fc2_up = shift(add(*fc2_block(1), fc2_far), 1)
    fc2_down = shift(add(*fc2_block(mods_n - 1)), mods_n - 1)
    fc1_plane = [swap(mine(dw1, n)[0], 2 * n) for n in (1, 2, 3)]
    dq1, dk1, dv1, dt1, dbq1 = attend_back(qkv1, p1, do1, o1, LONG)
    dw_send = qkv_weight(a, dq1, dk1, dv1, dwp_send, SHORT)
    dq2, dk2, dv2, dt2, dbq2 = attend_back(qkv2, p2, after(do2, dw_send), o2, SHORT)
    dq2, dk2, dv2, dt2, dbq2, dw_send, dwp_keep, fc2_up, fc2_down, *fc1_plane = fence(
        dq2, dk2, dv2, dt2, dbq2, dw_send, dwp_keep, fc2_up, fc2_down, *fc1_plane
    )
    fc1_parts = spread_chips(add(mine(dw1, 0)[0], *fc1_plane))
    fc2_mine = add(*fc2_block(0), fc2_up, fc2_down).reshape(4, -1, D)
    dw_in = swap(dw_send, 1)
    plane_peer = swap(plane, 1)

    def ring(step, total):
        block = pick_mod(fc1_parts, (me + 2 * mods_n - 1 - step) % mods_n)
        return block if total is None else add(block, total)

    ff_ring = shift(ring(0, None), 1)
    dw_keep = qkv_weight(a, dq2, dk2, dv2, dwp_keep, LONG)
    dw_keep, dt2, dbq2, ff_ring, dw_in, plane_peer = fence(dw_keep, dt2, dbq2, ff_ring, dw_in, plane_peer)
    packed = pack_small(idx, dbq1, dbq2, db_proj, db1_first, db1_second, db_fc2, dt1, dt2).astype(bf16)
    packed = add(packed, swap(packed, 1))
    ff_ring = shift(ring(1, ff_ring), 1)
    d_h, ff_ring = fence(d_h, ff_ring)
    ff_ring = shift(ring(2, ff_ring), 1)

    dw = quarters_of([dw_keep, dw_in])

    def quarter(other):
        total = mine(dw, other)
        total = jnp.concatenate([total[0], total[1], packed], axis=1).reshape(-1, D)
        return jnp.concatenate([total, pick_mod(fc2_mine, lax.bitwise_xor(spot, other))])

    from_plane = [swap(quarter(n), 2 * n) for n in (1, 2, 3)]
    dx, d_mod = back_entry(
        idx, long_one, valid_seg, (dq1, dk1, dv1, dq2, dk2, dv2), x, d_h, mods, dmod_mid, own_a, set_a, peer_a
    )
    d_mod, dx, ff_ring = fence(d_mod, dx, ff_ring)
    mod_in = [pick_mod(d_mod, me)] + [shift(pick_mod(d_mod, (me + k) % mods_n), k) for k in range(1, mods_n)]
    share = cond_share(w_ada, mod_in)
    share, *from_plane = fence(share, *from_plane)
    parts = spread_chips(add(quarter(0), *from_plane))
    fc2_part = parts[-D // 8 :]
    parts = parts[: -D // 8].reshape(mods_n, -1, D)
    tail = [jnp.concatenate([pick_mod(parts, (me + k) % mods_n), share]) for k in range(mods_n)]
    tail_in = [shift(tail[k], k) for k in range(1, mods_n)]
    fc1_part = ring(3, ff_ring)
    ff_part = jnp.concatenate([fc1_part[:, :D], fc1_part[:, D:], fc2_part])
    ff_set = [ff_part, swap(ff_part, 2), swap(ff_part, 4)]
    def gather_chips(piece):
        mine = jnp.stack(three(piece))
        return mine, swap(mine, 1)

    *ff_set, tail_in[0], tail_in[1], tail_in[2] = fence(*ff_set, *tail_in)
    count = parts.shape[1]
    arrived = [tail[0]] + tail_in
    part = add(*[t[:count] for t in arrived])
    rows = D // 8

    def of_group(k):
        terms = [
            lax.slice_in_dim(t, count + (k - j) % mods_n * slots_n, count + ((k - j) % mods_n + 1) * slots_n)
            for j, t in enumerate(arrived)
        ]
        total = sum(term.astype(f32) for term in terms)
        slope = packets[k][UR:].astype(f32)
        return (total * jnp.concatenate([slope[:slots_n], slope[slots_n:]], axis=1)).astype(bf16)

    conds = [piece for k in range(mods_n) for piece in (mod_in[k], of_group(k))]
    gathered = gather_chips(jnp.concatenate([part[:rows]] + conds))
    small_all = part[rows:].astype(f32)
    ff_set = jnp.stack(ff_set + [swap(ff_part, 6)])
    grad_fc1, grad_fc2 = finish_ff(idx, ff_set, swap(ff_set, 1))
    grad_qkv, grad_proj = finish_attn(idx, *gathered)

    conds = jnp.stack([g[:, rows:] for g in gathered]).reshape(-1, 3, slots_n, D)
    acts = jnp.stack([plane, plane_peer]).reshape(-1, UR, HALF)
    bit = 8
    while bit < lax.axis_size("dp"):
        conds = jnp.concatenate([conds, swap(conds, bit)])
        acts = jnp.concatenate([acts, swap(acts, bit)])
        bit *= 2
    width = w_ada.shape[1]
    d_mod_all = jnp.concatenate([conds[:, 0].reshape(-1, D), conds[:, 1].reshape(-1, D)[:, : width - D]], axis=1)
    d_cond_all = conds[:, 2].reshape(-1, D)
    act_all = jnp.concatenate(
        [acts[:, n * slots_n : (n + 1) * slots_n].reshape(-1, HALF) for n in range(2)], axis=1
    )
    digits_all = acts[:, 2 * slots_n : 3 * slots_n, :4].reshape(-1, 4).astype(jnp.int32)
    grad_ada = lax.dot_general(act_all, d_mod_all, (((0,), (0,)), ((), ())), preferred_element_type=f32)
    grad_ada_b = jnp.sum(d_mod_all.astype(f32), axis=0)

    def table_grad(high, low, rows):
        share = rows // mods_n
        index = digits_all[:, high] * 32 + digits_all[:, low]
        hot = (index[None, :] == me * share + jnp.arange(share)[:, None]).astype(bf16)
        return jnp.dot(hot, d_cond_all, preferred_element_type=f32)

    grad_rel = jnp.concatenate([small_all[:3], small_all[3].reshape(3, 2 * L - D)], axis=1)
    return (
        y.reshape(block_input.shape),
        dx.reshape(block_input.shape),
        table_grad(0, 1, time_table.shape[0]),
        table_grad(2, 3, class_table.shape[0]),
        grad_ada,
        grad_ada_b,
        grad_qkv,
        small_all[5, : qv_bias.shape[0]],
        grad_proj,
        take(small_all[6], me, proj_bias.shape[0]),
        grad_fc1,
        small_all[4],
        grad_fc2,
        take(small_all[7], me, fc2_bias.shape[0]),
        grad_rel[:, : rel_table.shape[1]],
    )


def solution(mesh):
    in_specs = (
        P(None, ("dp", "mod"), None),
        P(None, ("dp", "mod"), None),
        P(None, ("dp", "mod")),
        P(None, ("dp", "mod")),
        P(None, ("dp", "mod")),
        P(None, ("dp", "mod")),
        P(),
        P(),
        P(None, "mod"),
        P("mod"),
        P("mod", None),
        P("mod"),
        P("mod", None),
        P("mod"),
        P("mod", None),
        P("mod"),
        P("mod", None),
        P("mod"),
        P("mod", None),
    )
    out_specs = (
        P(None, ("dp", "mod"), None),
        P(None, ("dp", "mod"), None),
        P("mod", None),
        P("mod", None),
        P(None, "mod"),
        P("mod"),
        P("mod", None),
        P("mod"),
        P("mod", None),
        P("mod"),
        P("mod", None),
        P("mod"),
        P("mod", None),
        P("mod"),
        P("mod", None),
    )
    return jax.shard_map(local, mesh=mesh, in_specs=in_specs, out_specs=out_specs, check_vma=False)
```

```python
from functools import partial
import jax
import jax.numpy as jnp
from jax import lax
from jax.experimental import pallas as pl
from jax.experimental.pallas import tpu as pltpu
from jax.sharding import PartitionSpec as P

f32 = jnp.float32
bf16 = jnp.bfloat16
D = 768
H = 12
HD = 64
FF = 3072
L = 512
SEG = 128
NSEG = 4
MICRO = 2
T = MICRO * L
HALF = 384
FH = 1536
VMEM_LIMIT = 56 * 1024 * 1024


LONG = pl.CostEstimate(flops=30_000_000_000, bytes_accessed=1_000_000, transcendentals=0)
SHORT = pl.CostEstimate(flops=1, bytes_accessed=1, transcendentals=0)


def params(*sem, size=16):
    return pltpu.CompilerParams(vmem_limit_bytes=size * 1024 * 1024, dimension_semantics=sem)


def dot(a, b, ca=1, cb=0):
    return lax.dot_general(a, b, (((ca,), (cb,)), ((), ())), preferred_element_type=f32)


def norm_of(values):
    centred = values - jnp.mean(values, axis=1, keepdims=True)
    inverse = lax.rsqrt(jnp.mean(centred * centred, axis=1, keepdims=True) + 1e-6)
    return centred * inverse, inverse


def norm_back(grad, normed, inverse):
    return inverse * (
        grad
        - jnp.mean(grad, axis=1, keepdims=True)
        - normed * jnp.mean(grad * normed, axis=1, keepdims=True)
    )


UR = 48
PR = 64
ANY = pl.BlockSpec(memory_space=pltpu.HBM)
SMEM = pl.BlockSpec(memory_space=pltpu.SMEM)
VMEM = pl.BlockSpec(memory_space=pltpu.VMEM)


def whole(shape):
    return pl.BlockSpec(shape, lambda *_: (0,) * len(shape))


def bring(copies, sems):
    made = [pltpu.make_async_copy(source, target, sems.at[n]) for n, (source, target) in enumerate(copies)]
    return made


def go(made):
    for copy in made:
        copy.start()


def ready(made):
    for copy in made:
        copy.wait()


def quarters(idx_ref, sources):
    me, spot = idx_ref[0], idx_ref[1]
    for ref, lead, other in sources:
        for k in range(1, 4):
            yield (
                ref.at[k - 1] if lead is None else ref.at[lead, k - 1],
                lax.rem(me + 4 - k, 4),
                lax.bitwise_xor(spot, other),
            )


def pick_entry_body(idx_ref, w_ref, proj_ref, own_ref, out_ref):
    spot, core = idx_ref[1], idx_ref[2]
    for n, half in enumerate((1 - core, core)):
        for u in range(3):
            column = pl.multiple_of((2 * u + half) * HALF, HALF)
            own_ref[n, u] = w_ref[:, pl.ds(column, HALF)].reshape(4, UR, HALF)
        own_ref[n, 3] = proj_ref[:, pl.ds(pl.multiple_of(half * HALF, HALF), HALF)].reshape(4, UR, HALF)
    for n, q in enumerate((spot, lax.bitwise_xor(spot, 3))):
        for u in range(4):
            out_ref[n, u] = own_ref[0, u, q]


def pick_entry(idx, w, proj):
    return pl.pallas_call(
        pick_entry_body,
        in_specs=[SMEM, VMEM, VMEM],
        out_specs=[VMEM, VMEM],
        out_shape=[pltpu.HBM((2, 4, 4, UR, HALF), bf16), pltpu.HBM((2, 4, UR, HALF), bf16)],
        compiler_params=params(),
        cost_estimate=SHORT,
        name="pick_entry",
    )(idx, w, proj)


def packet_body(idx_ref, step_ref, label_ref, cond_ref, bias_ref, rel_ref, out_ref):
    me = idx_ref[0]
    slots = MICRO * NSEG
    cond = cond_ref[...]
    sigma = 1.0 / (1.0 + jnp.exp(-cond))
    act = cond / (1.0 + jnp.exp(-cond))
    slope = sigma * (1.0 + cond * (1.0 - sigma))
    row = lax.broadcasted_iota(jnp.int32, (slots, HALF), 0)
    lane = lax.broadcasted_iota(jnp.int32, (slots, HALF), 1)
    digits = jnp.zeros((slots, HALF), jnp.int32)
    for n in range(slots):
        step, label = step_ref[n // NSEG, n % NSEG], label_ref[n // NSEG, n % NSEG]
        values = (step // 32, step % 32, label // 32, label % 32)
        for m, value in enumerate(values):
            digits = jnp.where((row == n) & (lane == m), value, digits)
    rel = rel_ref[...].astype(f32)
    rel = jnp.concatenate([rel, jnp.zeros((3, 1), f32)], axis=1)
    bias = bias_ref[...].astype(f32)
    pair = jnp.broadcast_to(bias[3:4], (8, HALF))
    lane = lax.broadcasted_iota(jnp.int32, (8, HALF), 1)
    blank = jnp.zeros((8, HALF), f32)
    proj_b = jnp.concatenate([jnp.where(lane < 192, pair, 0.0), blank], axis=1)
    fc2_b = jnp.concatenate([jnp.where(lane < 192, 0.0, pair), blank], axis=1)
    proj_b = pltpu.roll(proj_b, me * 192, 1)
    fc2_b = pltpu.roll(fc2_b, lax.rem(me + 3, 4) * 192, 1)
    out_ref[...] = jnp.concatenate(
        [
            act[:, :HALF],
            act[:, HALF:],
            digits.astype(f32),
            rel[:, :HALF],
            rel[:, HALF : 2 * HALF],
            jnp.concatenate([rel[:, 2 * HALF :], jnp.zeros((3, 128), f32)], axis=1),
            bias[0:3],
            proj_b[0:1, :HALF],
            proj_b[0:1, HALF:],
            fc2_b[0:1, :HALF],
            fc2_b[0:1, HALF:],
            jnp.zeros((8, HALF), f32),
            slope[:, :HALF],
            slope[:, HALF:],
        ],
        axis=0,
    ).astype(bf16)


def make_packet(idx, steps, labels, cond, bias, rel):
    return pl.pallas_call(
        packet_body,
        in_specs=[SMEM, SMEM, SMEM, VMEM, VMEM, VMEM],
        out_specs=VMEM,
        out_shape=jax.ShapeDtypeStruct((PR, HALF), bf16),
        compiler_params=params(),
        cost_estimate=SHORT,
        name="packet",
    )(idx, steps, labels, cond, bias, rel)


def pick_ff_body(idx_ref, fc1_ref, fc2_ref, own1_ref, own2_ref, piece1_ref, piece2_ref):
    spot, core = idx_ref[1], idx_ref[2]
    for n, half in enumerate((1 - core, core)):
        for z in range(4):
            column = pl.multiple_of((2 * z + half) * HALF, HALF)
            own1_ref[n, z] = fc1_ref[:, pl.ds(column, HALF)].reshape(4, UR, HALF)
        for j in range(2):
            for i in range(2):
                row = pl.multiple_of(half * HALF + i * 192, 192)
                own2_ref[n, 2 * j + i] = fc2_ref[pl.ds(row, 192), j * HALF : (j + 1) * HALF].reshape(4, UR, HALF)
    for n, q in enumerate((spot, lax.bitwise_xor(spot, 3))):
        for u in range(4):
            piece1_ref[n, u] = own1_ref[0, u, q]
            piece2_ref[n, u] = own2_ref[0, u, q]


def pick_ff(idx, fc1, fc2):
    return pl.pallas_call(
        pick_ff_body,
        in_specs=[SMEM, VMEM, VMEM],
        out_specs=[VMEM] * 4,
        out_shape=[pltpu.HBM((2, 4, 4, UR, HALF), bf16)] * 2 + [pltpu.HBM((2, 4, UR, HALF), bf16)] * 2,
        compiler_params=params(),
        cost_estimate=SHORT,
        name="pick_ff",
    )(idx, fc1, fc2)


def entry_copies(idx_ref, own, half, sources, held):
    return [(own.at[half, pl.ds(0, 3)], held.at[:, idx_ref[0]])] + [
        (ref.at[pl.ds(0, 3)], held.at[:, z, q]) for ref, z, q in quarters(idx_ref, sources)
    ]


def stacked(ref):
    return [(ref, n, n) for n in range(4)]


def proj_copies(idx_ref, own, half, at, sources, held):
    return [(own.at[half, 3], held.at[at, idx_ref[0]])] + [
        (ref.at[3], held.at[at, z, q]) for ref, z, q in quarters(idx_ref, sources)
    ]


def fc1_copies(idx_ref, own, half, sources, held):
    return [(own.at[half], held.at[:, idx_ref[0]])] + [
        (ref, held.at[:, z, q]) for ref, z, q in quarters(idx_ref, sources)
    ]


def fc2_copies(idx_ref, own, half, sources, held):
    return [(own.at[half, pl.ds(2 * j, 2)], held.at[j, idx_ref[0]]) for j in range(2)] + [
        (ref.at[pl.ds(2 * j, 2)], held.at[j, z, :, q]) for ref, z, q in quarters(idx_ref, sources) for j in range(2)
    ]


def entry_weight(held):
    return jnp.concatenate([held[u].reshape(D, HALF) for u in range(3)], axis=1)


def proj_weight(held):
    return jnp.concatenate([held[n].reshape(D, HALF) for n in range(2)], axis=1)


ENTRY_HELD = (3, 4, 4, UR, HALF)


def columns_body(w_ref, b_ref, p0, p1, p2, p3, c0, c1, c2, c3, held, sems):
    copies = bring([(p, held.at[k]) for k, p in enumerate((p0, p1, p2, p3))], sems)
    go(copies)
    ready(copies)
    slots = MICRO * NSEG
    units = [held[k].astype(f32) for k in range(4)]
    act = jnp.concatenate(
        [jnp.concatenate([u[:slots], u[slots : 2 * slots]], axis=1) for u in units], axis=0
    ).astype(bf16)
    out = dot(act, w_ref[...]) + b_ref[...].astype(f32)
    for k, c in enumerate((c0, c1, c2, c3)):
        c[...] = out[k * slots : (k + 1) * slots]


def mod_columns(w, b, payloads):
    return pl.pallas_call(
        columns_body,
        in_specs=[VMEM, VMEM] + [ANY] * 4,
        out_specs=[VMEM] * 4,
        out_shape=[jax.ShapeDtypeStruct((MICRO * NSEG, 3 * HALF), f32)] * 4,
        scratch_shapes=[pltpu.VMEM((4, PR, HALF), bf16), pltpu.SemaphoreType.DMA((4,))],
        compiler_params=params(),
        cost_estimate=SHORT,
        name="mod_columns",
    )(w, b, *payloads)


def prepare_body(idx_ref, long_ref, valid_ref, c0, c1, c2, c3, p0, p1, p2, p3,
                 mod_ref, qb1, qb2, pb_ref, ub1, ub2, fb_ref, r1, r2, cols, held, rows, sems):
    me, core = idx_ref[0], idx_ref[2]
    copies = bring([(p, held.at[lax.rem(me + 4 - k, 4)]) for k, p in enumerate((p0, p1, p2, p3))], sems)
    go(copies)
    for k, c in enumerate((c0, c1, c2, c3)):
        cols[lax.rem(me + k, 4)] = c[...]
    ready(copies)
    rows[...] = held[...].astype(f32)
    slots = MICRO * NSEG
    row = lax.broadcasted_iota(jnp.int32, (slots, 1), 0)
    upper = row < NSEG
    is_long = jnp.where(upper, long_ref[0], long_ref[1]) > 0
    valid = jnp.zeros((slots, 1), f32)
    for n in range(slots):
        valid = jnp.where(row == n, valid_ref[n // NSEG, n % NSEG].astype(f32), valid)
    for g in range(12):
        value = cols[g // 3, :, (g % 3) * HALF : (g % 3 + 1) * HALF]
        value = jnp.where(is_long, jnp.where(upper, value[0:1], value[NSEG : NSEG + 1]), value)
        if (g // 2) % 3 == 2:
            value = value * valid
        mod_ref[g // 2, :, (g % 2) * HALF : (g % 2 + 1) * HALF] = value
    for half, qb, ub, r in ((1 - core, qb1, ub1, r1), (core, qb2, ub2, r2)):
        qb[:, :HALF] = rows[half, 33:34, :]
        qb[:, HALF : 2 * HALF] = jnp.zeros((1, HALF), f32)
        qb[:, 2 * HALF :] = rows[2 + half, 33:34, :]
        for z in range(4):
            ub[:, z * HALF : (z + 1) * HALF] = jnp.where(half > 0, rows[z, 35:36, :], rows[z, 34:35, :])
        for n in range(6):
            z, t, to = 2 * half + n // 3, n % 3, slice(n % 2, n % 2 + 1)
            r[n // 2, to, :HALF] = rows[z, 24 + t : 25 + t, :]
            r[n // 2, to, HALF : 2 * HALF] = rows[z, 27 + t : 28 + t, :]
            r[n // 2, to, 2 * HALF :] = rows[z, 30 + t : 31 + t, :256]
    for ref, at in ((pb_ref, 36), (fb_ref, 38)):
        for n in range(2):
            ref[:, n * HALF : (n + 1) * HALF] = (
                rows[0, at + n : at + n + 1, :]
                + rows[1, at + n : at + n + 1, :]
                + rows[2, at + n : at + n + 1, :]
                + rows[3, at + n : at + n + 1, :]
            )


def prepare(idx, long_flag, valid_seg, columns, payloads):
    shapes = [(6, MICRO * NSEG, D), (1, 3 * HALF), (1, 3 * HALF), (1, D), (1, FH), (1, FH), (1, D),
              (3, 2, 2 * L), (3, 2, 2 * L)]
    return pl.pallas_call(
        prepare_body,
        in_specs=[SMEM] * 3 + [VMEM] * 4 + [ANY] * 4,
        out_specs=[VMEM] * 9,
        out_shape=[jax.ShapeDtypeStruct(shape, f32) for shape in shapes],
        scratch_shapes=[
            pltpu.VMEM((4, MICRO * NSEG, 3 * HALF), f32),
            pltpu.VMEM((4, PR, HALF), bf16),
            pltpu.VMEM((4, PR, HALF), f32),
            pltpu.SemaphoreType.DMA((4,)),
        ],
        compiler_params=params(),
        cost_estimate=SHORT,
        name="prepare",
    )(idx, long_flag, valid_seg, *columns, *payloads)


def entry_norm_body(x_ref, mod_ref, a_ref):
    i = pl.program_id(0)
    for s in range(2):
        rows = pl.ds(s * SEG, SEG)
        at = pl.ds(i * 2 + s, 1)
        norm, _ = norm_of(x_ref[rows, :].astype(f32))
        a_ref[rows, :] = (norm * (1.0 + mod_ref[1, at, :]) + mod_ref[0, at, :]).astype(bf16)


def entry_norm(x, mods):
    block = pl.BlockSpec((2 * SEG, D), lambda i: (i, 0))
    return pl.pallas_call(
        entry_norm_body,
        grid=(4,),
        in_specs=[block, whole((6, MICRO * NSEG, D))],
        out_specs=block,
        out_shape=jax.ShapeDtypeStruct((T, D), bf16),
        compiler_params=params("arbitrary"),
        cost_estimate=LONG,
        name="entry_norm",
    )(x, mods)


def qkv_body(half, idx_ref, a_ref, b_ref, own, fetched, qkv_ref, held, sems):
    copies = bring(entry_copies(idx_ref, own, half, stacked(fetched), held), sems)

    @pl.when(pl.program_id(0) == 0)
    def _():
        go(copies)
        ready(copies)

    qkv_ref[...] = (dot(a_ref[...], entry_weight(held)) + b_ref[...]).astype(bf16)


def qkv_half(half, idx, a, b, own, near):
    return pl.pallas_call(
        partial(qkv_body, half),
        grid=(MICRO,),
        in_specs=[
            SMEM,
            pl.BlockSpec((L, D), lambda i: (i, 0)),
            whole((1, 3 * HALF)),
            ANY,
            ANY,
        ],
        out_specs=pl.BlockSpec((L, 3 * HALF), lambda i: (i, 0)),
        out_shape=jax.ShapeDtypeStruct((T, 3 * HALF), bf16),
        scratch_shapes=[pltpu.VMEM(ENTRY_HELD, bf16), pltpu.SemaphoreType.DMA((13,))],
        compiler_params=params("arbitrary"),
        cost_estimate=SHORT,
        name="qkv_half",
    )(idx, a, b, own, near)


def lane_reverse(rows):
    at = lax.broadcasted_iota(jnp.int32, (2 * SEG, 2 * SEG), 0) + lax.broadcasted_iota(jnp.int32, (2 * SEG, 2 * SEG), 1)
    turn = (at == 2 * SEG - 2).astype(f32)
    return lax.dot_general(
        rows, turn, (((1,), (0,)), ((), ())), precision=lax.Precision.HIGHEST, preferred_element_type=f32
    )


def attend_body(long_ref, valid_ref, q_ref, k_ref, v_ref, t_ref, o_ref, p_ref, bias_ref):
    b = pl.program_id(1)

    @pl.when(b == 0)
    def _():
        windows = [t_ref[0, h : h + 1, d * SEG : (d + 2) * SEG] for h in range(2) for d in range(7)]
        windows = lane_reverse(jnp.concatenate(windows + windows[:2], axis=0))
        for h in range(2):
            for d in range(7):
                row = jnp.broadcast_to(windows[h * 7 + d : h * 7 + d + 1, :], (SEG, 2 * SEG))
                bias_ref[h, d] = pltpu.roll(row, SEG + 1, 1, stride=1, stride_axis=0)[:, :SEG]

    is_long = long_ref[b]
    lane = lax.broadcasted_iota(jnp.int32, (L, 2 * HD), 1)
    query = q_ref[...] * jnp.asarray(HD**-0.5, bf16)
    keys = k_ref[...]
    values_t = v_ref[...].T
    outs = []
    for h in range(2):
        mine = (lane < HD) if h == 0 else (lane >= HD)
        key_h = jnp.where(mine, keys, jnp.zeros_like(keys))
        for qb in range(NSEG):
            cols = pl.ds(qb * SEG, SEG)
            scores = dot(key_h, query[qb * SEG : (qb + 1) * SEG, :], 1, 1)
            parts = []
            for kb in range(NSEG):
                open_ = (valid_ref[b, kb] > 0) if kb == qb else ((valid_ref[b, kb] > 0) & (is_long > 0))
                shut = jnp.where(open_, 0.0, -1e30).astype(f32)
                parts.append(scores[kb * SEG : (kb + 1) * SEG, :] + (bias_ref[h, kb - qb + 3] + shut))
            scores = jnp.concatenate(parts, axis=0)
            top = jnp.max(scores, axis=0, keepdims=True)
            expo = jnp.exp(scores - top)
            total = jnp.sum(expo, axis=0, keepdims=True)
            p_ref[0, h, :, cols] = (expo * (1.0 / total)).astype(bf16)
        outs.append(dot(values_t[h * HD : (h + 1) * HD, :], p_ref[0, h]))
    o_ref[...] = jnp.concatenate(outs, axis=0).T.astype(bf16)


def attend(qkv, table, long_flag, valid_seg, cost):
    pairs = 3
    return pl.pallas_call(
        attend_body,
        grid_spec=pltpu.PrefetchScalarGridSpec(
            num_scalar_prefetch=2,
            grid=(pairs, MICRO),
            in_specs=[
                pl.BlockSpec((L, 2 * HD), lambda g, b, *_: (b, g)),
                pl.BlockSpec((L, 2 * HD), lambda g, b, *_: (b, 3 + g)),
                pl.BlockSpec((L, 2 * HD), lambda g, b, *_: (b, 6 + g)),
                pl.BlockSpec((1, 2, 2 * L), lambda g, b, *_: (g, 0, 0)),
            ],
            out_specs=[
                pl.BlockSpec((L, 2 * HD), lambda g, b, *_: (b, g)),
                pl.BlockSpec((1, 2, L, L), lambda g, b, *_: (b, g, 0, 0)),
            ],
            scratch_shapes=[pltpu.VMEM((2, 7, SEG, SEG), f32)],
        ),
        out_shape=[
            jax.ShapeDtypeStruct((T, HALF), bf16),
            pltpu.HBM((MICRO, 6, L, L), bf16),
        ],
        compiler_params=params("arbitrary", "arbitrary"),
        cost_estimate=cost,
        name="attend",
    )(long_flag, valid_seg, qkv, qkv, qkv, table)


def middle_body(idx_ref, o1_ref, o2_ref, b_ref, x_ref, dy_ref, mod_ref, own, fetched, peer,
                h_ref, m_ref, attn_ref, dmlp_ref, db_ref, held, w_ref, sems):
    core = idx_ref[2]
    i = pl.program_id(0)

    @pl.when(i == 0)
    def _():
        copies = bring(
            proj_copies(idx_ref, own, 0, 1 - core, stacked(fetched), held)
            + proj_copies(idx_ref, own, 1, core, stacked(peer), held),
            sems,
        )
        go(copies)
        ready(copies)
        w_ref[...] = proj_weight(held)

    first = pl.multiple_of((1 - core) * HALF, HALF)
    second = pl.multiple_of(core * HALF, HALF)
    attn = dot(o1_ref[...], w_ref[pl.ds(first, HALF), :]) + dot(o2_ref[...], w_ref[pl.ds(second, HALF), :])
    attn = attn + b_ref[...]
    attn_ref[...] = attn.astype(bf16)
    total = jnp.zeros((1, D), f32)
    for s in range(NSEG):
        rows = pl.ds(s * SEG, SEG)
        at = pl.ds(i * NSEG + s, 1)
        hidden = x_ref[rows, :].astype(f32) + mod_ref[2, at, :] * attn[s * SEG : (s + 1) * SEG, :]
        h_ref[rows, :] = hidden
        norm, _ = norm_of(hidden)
        m_ref[rows, :] = (norm * (1.0 + mod_ref[4, at, :]) + mod_ref[3, at, :]).astype(bf16)
        dmlp = (dy_ref[rows, :].astype(f32) * mod_ref[5, at, :]).astype(bf16)
        dmlp_ref[rows, :] = dmlp
        total = total + jnp.sum(dmlp.astype(f32), axis=0, keepdims=True)

    @pl.when(pl.program_id(0) == 0)
    def _():
        db_ref[...] = jnp.zeros_like(db_ref)

    db_ref[0:1, :] += total


def middle(idx, o1, o2, b, x, dy, mods, own, one, two):
    row = lambda i: (i, 0)
    return pl.pallas_call(
        middle_body,
        grid=(MICRO,),
        in_specs=[
            SMEM,
            pl.BlockSpec((L, HALF), row),
            pl.BlockSpec((L, HALF), row),
            whole((1, D)),
            pl.BlockSpec((L, D), row),
            pl.BlockSpec((L, D), row),
            whole((6, MICRO * NSEG, D)),
        ] + [ANY] * 3,
        out_specs=[
            pl.BlockSpec((L, D), row),
            pl.BlockSpec((L, D), row),
            pl.BlockSpec((L, D), row),
            pl.BlockSpec((L, D), row),
            whole((8, D)),
        ],
        out_shape=[
            pltpu.HBM((T, D), f32),
            jax.ShapeDtypeStruct((T, D), bf16),
            pltpu.HBM((T, D), bf16),
            jax.ShapeDtypeStruct((T, D), bf16),
            jax.ShapeDtypeStruct((8, D), f32),
        ],
        scratch_shapes=[
            pltpu.VMEM((2, 4, 4, UR, HALF), bf16),
            pltpu.VMEM((D, D), bf16),
            pltpu.SemaphoreType.DMA((26,)),
        ],
        compiler_params=params("arbitrary"),
        cost_estimate=LONG,
        name="middle",
    )(idx, o1, o2, b, x, dy, mods, own, one, two)


FB = 768


def mlp_body(has_acc, idx_ref, m_ref, dmlp_ref, b_ref, own1, own2, fetched1, fetched2, *refs):
    if has_acc:
        acc_o, acc_d, out_o, out_d, dw1_ref, dw2_ref, db_ref, g_s, du_s, held1, held2, sems = refs
    else:
        out_o, out_d, dw1_ref, dw2_ref, db_ref, g_s, du_s, held1, held2, sems = refs
    f = pl.program_id(0)
    half_index = 1 if has_acc else 0

    @pl.when(f == 0)
    def _():
        copies = bring(
            fc1_copies(idx_ref, own1, half_index, stacked(fetched1), held1)
            + fc2_copies(idx_ref, own2, half_index, stacked(fetched2), held2),
            sems,
        )
        go(copies)
        ready(copies)

    w1 = jnp.concatenate([held1[2 * f + n].reshape(D, HALF) for n in range(2)], axis=1)
    w2 = jnp.concatenate([held2[j, pl.ds(2 * f, 2)].reshape(D, HALF) for j in range(2)], axis=1)
    bias = b_ref[0:1, :]
    chunk = 256
    total = jnp.zeros((1, FB), f32)
    c0 = (2.0 / jnp.pi) ** 0.5
    for r in range(T // chunk):
        rows = pl.ds(r * chunk, chunk)
        u = dot(m_ref[rows, :], w1) + bias
        dg = dot(dmlp_ref[rows, :], w2, 1, 1)
        u2 = u * u
        th = jnp.tanh(u * (c0 + (c0 * 0.044715) * u2))
        half = 0.5 + 0.5 * th
        g_s[rows, :] = (u * half).astype(bf16)
        slope = half + u * (0.5 - 0.5 * th * th) * (c0 + (3.0 * c0 * 0.044715) * u2)
        du = (dg * slope).astype(bf16)
        du_s[rows, :] = du
        total = total + jnp.sum(du.astype(f32), axis=0, keepdims=True)
    db_ref[0:1, :] = total

    @pl.when(f == 0)
    def _():
        if has_acc:
            out_o[...] = acc_o[...] + dot(g_s[...], w2)
            out_d[...] = acc_d[...] + dot(du_s[...], w1, 1, 1)
        else:
            out_o[...] = dot(g_s[...], w2)
            out_d[...] = dot(du_s[...], w1, 1, 1)

    @pl.when(f > 0)
    def _():
        out_o[...] += dot(g_s[...], w2)
        out_d[...] += dot(du_s[...], w1, 1, 1)

    dw2_ref[...] = dot(g_s[...], dmlp_ref[...], 0, 0).astype(bf16)
    dw1_ref[...] = dot(m_ref[...], du_s[...], 0, 0).astype(bf16)


def mlp(idx, m_in, dmlp, b1, own1, own2, fetched1, fetched2, acc=None):
    zero = lambda f: (0, 0)
    col = lambda f: (0, f)
    once = pl.Buffered(1)
    specs = [
        SMEM,
        pl.BlockSpec((T, D), zero, pipeline_mode=once),
        pl.BlockSpec((T, D), zero, pipeline_mode=once),
        pl.BlockSpec((1, FB), col),
    ] + [ANY] * 4
    args = [idx, m_in, dmlp, b1, own1, own2, fetched1, fetched2]
    if acc is not None:
        specs += [pl.BlockSpec((T, D), zero, pipeline_mode=once)] * 2
        args += list(acc)
    return pl.pallas_call(
        partial(mlp_body, acc is not None),
        grid=(FH // FB,),
        in_specs=specs,
        out_specs=[
            pl.BlockSpec((T, D), zero),
            pl.BlockSpec((T, D), zero),
            pl.BlockSpec((D, FB), col),
            pl.BlockSpec((FB, D), lambda f: (f, 0)),
            pl.BlockSpec((8, FB), col),
        ],
        out_shape=[
            jax.ShapeDtypeStruct((T, D), f32),
            jax.ShapeDtypeStruct((T, D), f32),
            pltpu.HBM((D, FH), bf16),
            pltpu.HBM((FH, D), bf16),
            jax.ShapeDtypeStruct((8, FH), f32),
        ],
        scratch_shapes=[
            pltpu.VMEM((T, FB), bf16),
            pltpu.VMEM((T, FB), bf16),
            pltpu.VMEM((4, 4, 4, UR, HALF), bf16),
            pltpu.VMEM((2, 4, 2, 4, UR, HALF), bf16),
            pltpu.SemaphoreType.DMA((39,)),
        ],
        compiler_params=params("arbitrary", size=44),
        cost_estimate=LONG,
        name="mlp",
    )(*args)


def back_middle_body(idx_ref, h_ref, dy_ref, mlp_ref, b2_ref, dm_ref, attn_ref, mod_ref, o1_ref, o2_ref,
                     own, fetched, peer,
                     y_ref, dh_ref, do1_ref, do2_ref, dws_ref, dwk_ref, dmod_ref, db_ref,
                     dattn_s, dw_s, held, w_ref, sems):
    i = pl.program_id(0)
    core = idx_ref[2]
    first = pl.multiple_of((1 - core) * HALF, HALF)
    second = pl.multiple_of(core * HALF, HALF)
    copies = bring(
        proj_copies(idx_ref, own, 0, 1 - core, stacked(fetched), held)
        + proj_copies(idx_ref, own, 1, core, stacked(peer), held),
        sems,
    )

    @pl.when(i == 0)
    def _():
        go(copies)

    total = jnp.zeros((1, D), f32)
    for s in range(NSEG):
        rows = pl.ds(s * SEG, SEG)
        at = pl.ds(i * NSEG + s, 1)
        hidden = h_ref[rows, :]
        dy = dy_ref[rows, :].astype(f32)
        ff = mlp_ref[rows, :] + b2_ref[...]
        y_ref[rows, :] = (hidden + mod_ref[5, at, :] * ff).astype(bf16)
        dmod_ref[5, at, :] = jnp.sum(dy * ff, axis=0, keepdims=True)
        norm, inverse = norm_of(hidden)
        dm = dm_ref[rows, :]
        dmod_ref[3, at, :] = jnp.sum(dm, axis=0, keepdims=True)
        dmod_ref[4, at, :] = jnp.sum(dm * norm, axis=0, keepdims=True)
        dh = dy + norm_back(dm * (1.0 + mod_ref[4, at, :]), norm, inverse)
        dh_ref[rows, :] = dh
        dmod_ref[2, at, :] = jnp.sum(dh * attn_ref[rows, :].astype(f32), axis=0, keepdims=True)
        dattn = (dh * mod_ref[2, at, :]).astype(bf16)
        dattn_s[rows, :] = dattn
        total = total + jnp.sum(dattn.astype(f32), axis=0, keepdims=True)
    dattn = dattn_s[...]

    @pl.when(i == 0)
    def _():
        ready(copies)
        w_ref[...] = proj_weight(held)

    do1_ref[...] = dot(dattn, w_ref[pl.ds(first, HALF), :], 1, 1).astype(bf16)
    do2_ref[...] = dot(dattn, w_ref[pl.ds(second, HALF), :], 1, 1).astype(bf16)

    @pl.when(i == 0)
    def _():
        db_ref[...] = jnp.zeros_like(db_ref)
        dmod_ref[0:2] = jnp.zeros((2, MICRO * NSEG, D), f32)
        dw_s[...] = jnp.zeros_like(dw_s)

    db_ref[0:1, :] += total
    dw_s[pl.ds(first, HALF), :] += dot(o1_ref[...], dattn, 0, 0)
    dw_s[pl.ds(second, HALF), :] += dot(o2_ref[...], dattn, 0, 0)

    @pl.when(i == MICRO - 1)
    def _():
        dws_ref[...] = dw_s[:, pl.ds(first, HALF)].astype(bf16)
        dwk_ref[...] = dw_s[:, pl.ds(second, HALF)].astype(bf16)


def back_middle(idx, h, dy, ff, b2, dm, attn, mods, o1, o2, own, one, two):
    row = lambda i: (i, 0)
    full = pl.BlockSpec((L, D), row)
    part = pl.BlockSpec((L, HALF), row)
    modspec = whole((6, MICRO * NSEG, D))
    return pl.pallas_call(
        back_middle_body,
        grid=(MICRO,),
        in_specs=[SMEM, full, full, full, whole((1, D)), full, full, modspec, part, part] + [ANY] * 3,
        out_specs=[full, full, part, part, whole((D, HALF)), whole((D, HALF)), modspec, whole((8, D))],
        scratch_shapes=[
            pltpu.VMEM((L, D), bf16),
            pltpu.VMEM((D, D), f32),
            pltpu.VMEM((2, 4, 4, UR, HALF), bf16),
            pltpu.VMEM((D, D), bf16),
            pltpu.SemaphoreType.DMA((26,)),
        ],
        out_shape=[
            pltpu.HBM((T, D), bf16),
            pltpu.HBM((T, D), f32),
            jax.ShapeDtypeStruct((T, HALF), bf16),
            jax.ShapeDtypeStruct((T, HALF), bf16),
            jax.ShapeDtypeStruct((D, HALF), bf16),
            jax.ShapeDtypeStruct((D, HALF), bf16),
            jax.ShapeDtypeStruct((6, MICRO * NSEG, D), f32),
            jax.ShapeDtypeStruct((8, D), f32),
        ],
        compiler_params=params("arbitrary", size=28),
        cost_estimate=LONG,
        name="back_middle",
    )(idx, h, dy, ff, b2, dm, attn, mods, o1, o2, own, one, two)


def attend_back_body(q_ref, k_ref, v_ref, p_ref, do_ref, o_ref, dq_ref, dk_ref, dv_ref, dt_ref, db_ref, acc_ref, ds_s):
    b = pl.program_id(1)

    @pl.when(b == 0)
    def _():
        acc_ref[...] = jnp.zeros_like(acc_ref)
        db_ref[...] = jnp.zeros_like(db_ref)

    lane = lax.broadcasted_iota(jnp.int32, (L, 2 * HD), 1)
    query = q_ref[...]
    keys_t = k_ref[...].T
    values = v_ref[...]
    dout = do_ref[...]
    prod = (dout.astype(f32) * o_ref[...].astype(f32)).T
    dqs, dks, dvs = [], [], []
    for h in range(2):
        mine = (lane < HD) if h == 0 else (lane >= HD)
        value_h = jnp.where(mine, values, jnp.zeros_like(values))
        delta = jnp.sum(prod[h * HD : (h + 1) * HD, :], axis=0, keepdims=True)
        for qb in range(NSEG):
            cols = slice(qb * SEG, (qb + 1) * SEG)
            dp = dot(value_h, dout[cols, :], 1, 1)
            ds = (p_ref[0, h, :, cols].astype(f32) * (dp - delta[:, cols])).astype(bf16)
            ds_s[h, :, cols] = ds
            for kb in range(NSEG):
                acc_ref[h, kb - qb + 3] += ds[kb * SEG : (kb + 1) * SEG, :].astype(f32)
        dvs.append(dot(p_ref[0, h], dout))
        dks.append(dot(ds_s[h], query))
        dqs.append(dot(keys_t[h * HD : (h + 1) * HD, :], ds_s[h]))
    low = lane < HD
    scale = HD**-0.5
    dq = (jnp.concatenate(dqs, axis=0).T * scale).astype(bf16)
    dk = (jnp.where(low, dks[0], dks[1]) * scale).astype(bf16)
    dv = jnp.where(low, dvs[0], dvs[1]).astype(bf16)
    dq_ref[...] = dq
    dk_ref[...] = dk
    dv_ref[...] = dv
    db_ref[0:1, :] += jnp.sum(dq.astype(f32), axis=0, keepdims=True)
    db_ref[1:2, :] += jnp.sum(dv.astype(f32), axis=0, keepdims=True)

    @pl.when(b == MICRO - 1)
    def _():
        sums = []
        for h in range(2):
            for d in range(7):
                wide = jnp.concatenate([acc_ref[h, d], jnp.zeros((SEG, SEG), f32)], axis=1)
                rows = SEG
                while rows > 1:
                    rows //= 2
                    wide = pltpu.roll(wide[:rows], rows, 1) + wide[rows:]
                sums.append(wide)
        sums = lane_reverse(jnp.concatenate(sums + sums[:2], axis=0))
        dt_ref[...] = jnp.zeros_like(dt_ref)
        for h in range(2):
            for d in range(7):
                dt_ref[0, h : h + 1, d * SEG : (d + 2) * SEG] += sums[h * 7 + d : h * 7 + d + 1, :]


def attend_back(qkv, p, dout, out, cost):
    col = lambda g, b: (b, g)
    part = pl.BlockSpec((L, 2 * HD), col)
    return pl.pallas_call(
        attend_back_body,
        grid=(3, MICRO),
        in_specs=[
            part,
            pl.BlockSpec((L, 2 * HD), lambda g, b: (b, 3 + g)),
            pl.BlockSpec((L, 2 * HD), lambda g, b: (b, 6 + g)),
            pl.BlockSpec((1, 2, L, L), lambda g, b: (b, g, 0, 0)),
            part,
            part,
        ],
        out_specs=[part, part, part, pl.BlockSpec((1, 8, 2 * L), lambda g, b: (g, 0, 0)),
                   pl.BlockSpec((8, 2 * HD), lambda g, b: (0, g))],
        out_shape=[jax.ShapeDtypeStruct((T, HALF), bf16)] * 3
        + [jax.ShapeDtypeStruct((3, 8, 2 * L), f32), jax.ShapeDtypeStruct((8, HALF), f32)],
        scratch_shapes=[pltpu.VMEM((2, 7, SEG, SEG), f32), pltpu.VMEM((2, L, L), bf16)],
        compiler_params=params("arbitrary", "arbitrary"),
        cost_estimate=cost,
        name="attend_back",
    )(qkv, qkv, qkv, p, dout, out)


def qkv_weight_body(a_ref, dq_ref, dk_ref, dv_ref, proj_ref, out_ref):
    a = a_ref[...]
    grads = jnp.concatenate([dq_ref[...], dk_ref[...]], axis=1)
    out_ref[0] = dot(a, grads, 0, 0).astype(bf16)
    out_ref[1, :, :HALF] = dot(a, dv_ref[...], 0, 0).astype(bf16)
    out_ref[1, :, HALF:] = proj_ref[...]


def qkv_weight(a, dq, dk, dv, proj, cost):
    return pl.pallas_call(
        qkv_weight_body,
        out_shape=jax.ShapeDtypeStruct((2, D, D), bf16),
        compiler_params=params(),
        cost_estimate=cost,
        name="qkv_weight",
    )(a, dq, dk, dv, proj)


def back_entry_body(idx_ref, long_ref, valid_ref, dq1, dk1, dv1, dq2, dk2, dv2, x_ref, dh_ref, mod_ref, mid_ref,
                    own, fetched, peer, dx_ref, out_ref, held1, held2, entry_ref, sems):
    i = pl.program_id(0)

    @pl.when(i == 0)
    def _():
        copies = bring(
            entry_copies(idx_ref, own, 0, stacked(fetched), held1) + entry_copies(idx_ref, own, 1, stacked(peer), held2),
            sems,
        )
        go(copies)
        ready(copies)

    one = jnp.concatenate([dq1[...], dk1[...], dv1[...]], axis=1)
    two = jnp.concatenate([dq2[...], dk2[...], dv2[...]], axis=1)
    da = dot(one, entry_weight(held1), 1, 1) + dot(two, entry_weight(held2), 1, 1)
    for s in range(NSEG):
        rows = pl.ds(s * SEG, SEG)
        at = pl.ds(i * NSEG + s, 1)
        piece = da[s * SEG : (s + 1) * SEG, :]
        norm, inverse = norm_of(x_ref[rows, :].astype(f32))
        entry_ref[0, at, :] = jnp.sum(piece, axis=0, keepdims=True)
        entry_ref[1, at, :] = jnp.sum(piece * norm, axis=0, keepdims=True)
        dx_ref[rows, :] = (
            dh_ref[rows, :] + norm_back(piece * (1.0 + mod_ref[1, at, :]), norm, inverse)
        ).astype(bf16)

    @pl.when(i == MICRO - 1)
    def _():
        slots = MICRO * NSEG
        row = lax.broadcasted_iota(jnp.int32, (slots, 1), 0)
        upper = row < NSEG
        is_long = jnp.where(upper, long_ref[0], long_ref[1]) > 0
        valid = jnp.zeros((slots, 1), f32)
        for n in range(slots):
            valid = jnp.where(row == n, valid_ref[n // NSEG, n % NSEG].astype(f32), valid)
        lead = (row == 0) | (row == NSEG)
        blocks = []
        for j in range(6):
            value = entry_ref[j] if j < 2 else mid_ref[j]
            if j % 3 == 2:
                value = value * valid
            total = jnp.where(
                upper,
                jnp.sum(value[:NSEG], axis=0, keepdims=True),
                jnp.sum(value[NSEG:], axis=0, keepdims=True),
            )
            value = jnp.where(is_long, jnp.where(lead, total, 0.0), value)
            blocks += [value[:, :HALF], value[:, HALF:]]
        blank = jnp.zeros((slots, HALF), f32)
        for z in range(4):
            out_ref[z] = jnp.concatenate(
                [
                    jnp.concatenate(blocks[3 * z : 3 * z + 2], axis=1),
                    jnp.concatenate([blocks[3 * z + 2], blank], axis=1),
                ],
                axis=0,
            ).astype(bf16)


def back_entry(idx, long_flag, valid_seg, parts, x, dh, mods, mid, own, near, peer):
    row = lambda i: (i, 0)
    full = pl.BlockSpec((L, D), row)
    part = pl.BlockSpec((L, HALF), row)
    slots = MICRO * NSEG
    return pl.pallas_call(
        back_entry_body,
        grid=(MICRO,),
        in_specs=[SMEM] * 3 + [part] * 6 + [full, full, whole((6, slots, D)), whole((6, slots, D))] + [ANY] * 3,
        out_specs=[full, whole((4, 2 * slots, D))],
        out_shape=[pltpu.HBM((T, D), bf16), jax.ShapeDtypeStruct((4, 2 * slots, D), bf16)],
        scratch_shapes=[
            pltpu.VMEM(ENTRY_HELD, bf16),
            pltpu.VMEM(ENTRY_HELD, bf16),
            pltpu.VMEM((2, slots, D), f32),
            pltpu.SemaphoreType.DMA((26,)),
        ],
        compiler_params=params("arbitrary", size=24),
        cost_estimate=LONG,
        name="back_entry",
    )(idx, long_flag, valid_seg, *parts, x, dh, mods, mid, own, near, peer)


def cond_share_body(w_ref, d0, d1, d2, d3, out_ref):
    slots = MICRO * NSEG
    rows = [d[...].astype(f32) for d in (d0, d1, d2, d3)]
    rows = [jnp.concatenate([r[:slots], r[slots:, :HALF]], axis=1) for r in rows]
    out_ref[...] = dot(jnp.concatenate(rows, axis=0).astype(bf16), w_ref[...], 1, 1).astype(bf16)


def cond_share(w, blocks):
    return pl.pallas_call(
        cond_share_body,
        in_specs=[VMEM] * 5,
        out_specs=VMEM,
        out_shape=jax.ShapeDtypeStruct((4 * MICRO * NSEG, D), bf16),
        compiler_params=params(),
        cost_estimate=SHORT,
        name="cond_share",
    )(w, *blocks)


def pack_small_body(idx_ref, q1, q2, proj_ref, u1, u2, fc2_ref, t1, t2, out_ref):
    core = idx_ref[2]
    for z in range(4):
        half = z // 2
        tail = []
        for t in range(3):
            n = (z % 2) * 3 + t
            row = jnp.where(core == half, t2[n // 2, n % 2 : n % 2 + 1, :], t1[n // 2, n % 2 : n % 2 + 1, :])
            out_ref[z, t : t + 1, :] = row[:, :D]
            tail.append(row[:, D:])
        out_ref[z, 3:4, :] = jnp.concatenate(tail, axis=1)
        for h in range(2):
            block = slice(z * HALF, (z + 1) * HALF)
            out_ref[z, 4:5, h * HALF : (h + 1) * HALF] = jnp.where(core == h, u2[0:1, block], u1[0:1, block])
        half, kind = z % 2, z // 2
        out_ref[z, 5:6, 0:HALF] = jnp.where(core == half, q2[kind : kind + 1, :], q1[kind : kind + 1, :])
        out_ref[z, 5:6, HALF:] = jnp.zeros((1, HALF), f32)
        out_ref[z, 6:7, :] = proj_ref[0:1, :]
        out_ref[z, 7:8, :] = fc2_ref[0:1, :]


def pack_small(idx, *arrays):
    return pl.pallas_call(
        pack_small_body,
        in_specs=[SMEM] + [VMEM] * 8,
        out_specs=VMEM,
        out_shape=jax.ShapeDtypeStruct((4, 8, D), f32),
        compiler_params=params(),
        cost_estimate=SHORT,
        name="pack_small",
    )(idx, *arrays)


def finish_ff_body(idx_ref, mine_ref, peer_ref, fc1_ref, fc2_ref):
    spot, core = idx_ref[1], idx_ref[2]
    for source, half in ((mine_ref, core), (peer_ref, 1 - core)):
        for j in range(4):
            place_at = lax.bitwise_xor(spot, j)
            row = pl.multiple_of(place_at * 48, 16)
            for z in range(4):
                source_rows = pl.ds(48 * (z // 2), 48)
                block = source[j, source_rows, (z % 2) * HALF : (z % 2 + 1) * HALF]
                column = pl.multiple_of((2 * z + half) * HALF, 128)
                fc1_ref[pl.ds(row, 48), pl.ds(column, HALF)] = block.astype(f32)
            row = pl.multiple_of(half * HALF + place_at * 96, 16)
            fc2_ref[pl.ds(row, 96), :] = source[j, 96:192, :].astype(f32)


def finish_ff(idx, mine, peer):
    vmem = pl.BlockSpec(memory_space=pltpu.VMEM)
    return pl.pallas_call(
        finish_ff_body,
        in_specs=[pl.BlockSpec(memory_space=pltpu.SMEM), vmem, vmem],
        out_specs=[vmem, vmem],
        out_shape=[jax.ShapeDtypeStruct((D // 4, FF), f32), jax.ShapeDtypeStruct((FF // 4, D), f32)],
        compiler_params=params(),
        cost_estimate=SHORT,
        name="finish_ff",
    )(idx, mine, peer)


def finish_attn_body(idx_ref, mine_ref, peer_ref, qkv_ref, proj_ref):
    spot, core = idx_ref[1], idx_ref[2]
    for source, half in ((mine_ref, core), (peer_ref, 1 - core)):
        column = half * HALF
        for j in range(4):
            place_at = lax.bitwise_xor(spot, j)
            row = pl.multiple_of(place_at * 48, 16)
            for t in range(4):
                block = source[j, 48 * (t // 2) : 48 * (t // 2 + 1), (t % 2) * HALF : (t % 2 + 1) * HALF].astype(f32)
                if t < 3:
                    qkv_ref[pl.ds(row, 48), pl.ds(pl.multiple_of(t * D + column, 128), HALF)] = block
                else:
                    proj_ref[pl.ds(row, 48), pl.ds(pl.multiple_of(column, 128), HALF)] = block


def finish_attn(idx, mine, peer):
    vmem = pl.BlockSpec(memory_space=pltpu.VMEM)
    return pl.pallas_call(
        finish_attn_body,
        in_specs=[pl.BlockSpec(memory_space=pltpu.SMEM), vmem, vmem],
        out_specs=[vmem, vmem],
        out_shape=[jax.ShapeDtypeStruct((D // 4, 3 * D), f32), jax.ShapeDtypeStruct((D // 4, D), f32)],
        compiler_params=params(),
        cost_estimate=SHORT,
        name="finish_attn",
    )(idx, mine, peer)


def tail_sum_body(t0, t1, t2, t3, m0, m1, m2, m3, p0, p1, p2, p3, piece_ref, small_ref):
    slots = MICRO * NSEG
    arrived = [t[...].astype(f32) for t in (t0, t1, t2, t3)]
    rows = D // 8
    small_ref[...] = sum(t[rows : rows + 8] for t in arrived)
    blocks = [sum(t[:rows] for t in arrived)]
    for k, (m, p) in enumerate(((m0, p0), (m1, p1), (m2, p2), (m3, p3))):
        total = jnp.zeros((slots, D), f32)
        for j, t in enumerate(arrived):
            at = rows + 8 + (k - j) % 4 * slots
            total = total + t[at : at + slots]
        packet = p[...].astype(f32)
        slope = jnp.concatenate([packet[UR : UR + slots], packet[UR + slots : UR + 2 * slots]], axis=1)
        blocks += [m[...].astype(f32), total * slope]
    piece_ref[...] = jnp.concatenate(blocks, axis=0).astype(bf16)


def tail_sum(arrived, mods, packets):
    return pl.pallas_call(
        tail_sum_body,
        in_specs=[VMEM] * 12,
        out_specs=[VMEM, VMEM],
        out_shape=[jax.ShapeDtypeStruct((D // 4, D), bf16), jax.ShapeDtypeStruct((8, D), f32)],
        compiler_params=params(),
        cost_estimate=SHORT,
        name="tail_sum",
    )(*arrived, *mods, *packets)


def finish_cond_body(n, share, idx_ref, *refs):
    gathered, planes = refs[:n], refs[n : 2 * n]
    ada_ref, bias_ref, time_ref, class_ref = refs[2 * n :]
    slots = MICRO * NSEG
    acts, mods, conds, digits = [], [], [], []
    for g, p in zip(gathered, planes):
        for j in range(4):
            block = g[j, D // 8 :, :].astype(f32)
            for k in range(4):
                at = 3 * slots * k
                mods.append(
                    jnp.concatenate([block[at : at + slots], block[at + slots : at + 2 * slots, :HALF]], axis=1)
                )
                conds.append(block[at + 2 * slots : at + 3 * slots])
                unit = p[j, k].astype(f32)
                acts.append(jnp.concatenate([unit[:slots], unit[slots : 2 * slots]], axis=1))
                digits.append(unit[2 * slots : 3 * slots, :128])
    mods = jnp.concatenate(mods, axis=0)
    bias_ref[...] = jnp.sum(mods, axis=0, keepdims=True)
    ada_ref[...] = dot(jnp.concatenate(acts, axis=0).astype(bf16), mods.astype(bf16), 0, 0)
    conds = jnp.concatenate(conds, axis=0).astype(bf16)
    digits = jnp.concatenate(digits, axis=0)
    wide = (share + 127) // 128 * 128
    lane = lax.broadcasted_iota(jnp.int32, (digits.shape[0], wide), 1).astype(f32)
    first = (idx_ref[0] * share).astype(f32)
    for ref, n in ((time_ref, 0), (class_ref, 2)):
        index = digits[:, n : n + 1] * 32.0 + digits[:, n + 1 : n + 2] - first
        ref[...] = dot((index == lane).astype(bf16), conds, 0, 0)[:share]


def finish_cond(idx, gathered, planes, share, width):
    n = len(gathered)
    return pl.pallas_call(
        partial(finish_cond_body, n, share),
        in_specs=[SMEM] + [VMEM] * (2 * n),
        out_specs=[VMEM] * 4,
        out_shape=[
            jax.ShapeDtypeStruct((D, width), f32),
            jax.ShapeDtypeStruct((1, width), f32),
            jax.ShapeDtypeStruct((share, D), f32),
            jax.ShapeDtypeStruct((share, D), f32),
        ],
        compiler_params=params(size=40),
        cost_estimate=SHORT,
        name="finish_cond",
    )(idx, *gathered, *planes)


def swap(array, bit):
    count = lax.axis_size("dp")
    return lax.ppermute(array, "dp", [(i, i ^ bit) for i in range(count)])


def shift(array, step):
    count = lax.axis_size("mod")
    return lax.ppermute(array, "mod", [(i, (i + step) % count) for i in range(count)])


def take(array, index, size, axis=0):
    return lax.dynamic_slice_in_dim(array, index * size, size, axis)


def after(value, *earlier):
    return lax.optimization_barrier((value, *earlier))[0]


def fence(*values):
    return lax.optimization_barrier(values)


def around(piece):
    return [shift(piece, k) for k in range(1, 4)]


def three(near):
    return [near, swap(near, 2), swap(near, 4), swap(near, 6)]


def add(*terms):
    total = terms[0].astype(f32)
    for term in terms[1:]:
        total = total + term.astype(f32)
    return total.astype(bf16)


def spread_chips(grad):
    bit = 8
    while bit < lax.axis_size("dp"):
        grad = add(grad, swap(grad, bit))
        bit *= 2
    return grad


def pick_mod(grad, index):
    return lax.dynamic_index_in_dim(grad, index, 0, keepdims=False)


def local(
    block_input,
    grad_out,
    long_flag,
    valid_mask,
    labels,
    tsteps,
    time_table,
    class_table,
    w_ada,
    b_ada,
    w_qkv,
    qv_bias,
    w_proj,
    proj_bias,
    w_fc1,
    fc1_bias,
    w_fc2,
    fc2_bias,
    rel_table,
):
    mods_n = lax.axis_size("mod")
    me = lax.axis_index("mod")
    core = lax.axis_index("dp") % 2
    spot = (lax.axis_index("dp") // 2) % 4
    idx = jnp.stack([me, spot, core]).astype(jnp.int32)
    slots_n = MICRO * NSEG
    x = block_input.reshape(T, D)
    dy = grad_out.reshape(T, D)
    long_one = long_flag.reshape(MICRO)
    valid_seg = valid_mask.reshape(MICRO, NSEG, SEG)[:, :, 0]

    step_flat = tsteps.reshape(slots_n)
    label_flat = labels.reshape(slots_n)
    cond = time_table[step_flat].astype(f32) + class_table[label_flat].astype(f32)
    biases = jnp.concatenate([qv_bias, fc1_bias, proj_bias, fc2_bias]).reshape(4, HALF)
    own_a, piece_a = pick_entry(idx, w_qkv, w_proj)
    up_a, down_a = shift(piece_a, 1), shift(piece_a, mods_n - 1)
    own_1, own_2, piece_1, piece_2 = pick_ff(idx, w_fc1, w_fc2)
    packet = make_packet(
        idx, tsteps.reshape(MICRO, NSEG), labels.reshape(MICRO, NSEG), cond, biases, rel_table
    )
    up_a, down_a, packet, piece_1, piece_2 = fence(up_a, down_a, packet, piece_1, piece_2)
    far_a = shift(up_a, 1)
    packets = [packet] + around(packet)
    far_a, *packets = fence(far_a, *packets)

    def sides(got, also_x=None, also_y=None):
        near = jnp.concatenate([g[0] for g in got])
        units = near.shape[0]
        outs = []
        for bit, also in ((2, also_x), (4, also_y)):
            outs.append(swap(near if also is None else jnp.concatenate([near, also]), bit))
        return near, outs, jnp.concatenate([g[1] for g in got]), units

    def assemble(near, outs, diag, units):
        return jnp.stack([near, outs[0][:units], outs[1][:units], diag]).reshape(4, 3, units // 3, UR, HALF)

    shared = jnp.stack([p[:UR] for p in packets])
    near_a, side_a, diag_a, units = sides([up_a, far_a, down_a], shared, shared)
    columns = mod_columns(w_ada, b_ada.reshape(1, -1), packets)
    back = [columns[0]] + [shift(columns[k], mods_n - k) for k in range(1, mods_n)]
    mods, qkv_b1, qkv_b2, proj_b, fc1_b1, fc1_b2, fc2_b, rel_1, rel_2 = prepare(
        idx, long_one, valid_seg, back, packets
    )
    piece_1, mods = fence(piece_1, mods)
    up_1, down_1 = shift(piece_1, 1), shift(piece_1, mods_n - 1)
    a = entry_norm(x, mods)
    plane = [shared, side_a[0][units:], side_a[1][units:]]
    set_a = assemble(near_a, side_a, diag_a, units)
    qkv1 = qkv_half(0, idx, a, qkv_b1, own_a, set_a)
    qkv1, a, set_a, up_1, down_1, piece_2 = fence(qkv1, a, set_a, up_1, down_1, piece_2)
    peer_a = swap(set_a, 1)
    far_1 = shift(up_1, 1)
    up_2, down_2 = shift(piece_2, 1), shift(piece_2, mods_n - 1)
    o1, p1 = attend(qkv1, rel_1, long_one, valid_seg, LONG)
    qkv2 = qkv_half(1, idx, after(a, o1), qkv_b2, own_a, peer_a)
    qkv2, far_1, up_2, down_2 = fence(qkv2, far_1, up_2, down_2)
    set_1 = list(sides([up_1, far_1, down_1], None, plane[1]))
    far_2 = shift(up_2, 1)
    o2, p2 = attend(qkv2, rel_2, long_one, valid_seg, LONG)
    o2, far_2, *set_1[1] = fence(o2, far_2, *set_1[1])
    set_2 = list(sides([up_2, far_2, down_2]))
    hidden, m_in, attn, d_mlp, db_fc2 = middle(idx, o1, o2, proj_b, x, dy, mods, own_a, set_a, peer_a)
    m_in, *set_2[1] = fence(m_in, *set_2[1])
    plane = jnp.stack(plane + [set_1[1][1][set_1[3] :]])
    set_1, set_2 = assemble(*set_1), assemble(*set_2)
    peer_1, peer_2 = swap(set_1, 1), swap(set_2, 1)
    acc_o, acc_d, dw1_send, dw2_send, db1_first = mlp(idx, m_in, d_mlp, fc1_b1, own_1, own_2, set_1, set_2)
    acc_o, peer_1, peer_2 = fence(acc_o, peer_1, peer_2)
    from_core = [swap(dw1_send, 1), swap(dw2_send, 1)]
    ff, dm, dw1_keep, dw2_keep, db1_second = mlp(
        idx, m_in, d_mlp, fc1_b2, own_1, own_2, peer_1, peer_2, (acc_o, acc_d)
    )
    ff, dw1_keep, dw2_keep, *from_core = fence(ff, dw1_keep, dw2_keep, *from_core)

    def quarters_of(grads):
        return [g.reshape(g.shape[0], mods_n, 4, -1, g.shape[-1]) for g in grads]

    def mine(grads, other):
        return add(*[lax.dynamic_index_in_dim(g, lax.bitwise_xor(spot, other), 2, keepdims=False) for g in grads])

    dw1 = quarters_of([g[None] for g in (dw1_keep, from_core[0])])
    dw2 = [g.reshape(mods_n, HALF, D) for g in (dw2_keep, from_core[1])]

    def fc2_block(step):
        return [pick_mod(g, (me + step) % mods_n) for g in dw2]

    fc2_far = shift(add(*fc2_block(2)), 1)
    y, d_h, do1, do2, dwp_send, dwp_keep, dmod_mid, db_proj = back_middle(
        idx, hidden, dy, ff, fc2_b, dm, attn, mods, o1, o2, own_a, set_a, peer_a
    )
    do1, fc2_far = fence(do1, fc2_far)
    fc2_up = shift(add(*fc2_block(1), fc2_far), 1)
    fc2_down = shift(add(*fc2_block(mods_n - 1)), mods_n - 1)
    fc1_plane = [swap(mine(dw1, n)[0], 2 * n) for n in (1, 2, 3)]
    dq1, dk1, dv1, dt1, dbq1 = attend_back(qkv1, p1, do1, o1, LONG)
    dw_send = qkv_weight(a, dq1, dk1, dv1, dwp_send, SHORT)
    dq2, dk2, dv2, dt2, dbq2 = attend_back(qkv2, p2, after(do2, dw_send), o2, SHORT)
    dq2, dk2, dv2, dt2, dbq2, dw_send, dwp_keep, fc2_up, fc2_down, *fc1_plane = fence(
        dq2, dk2, dv2, dt2, dbq2, dw_send, dwp_keep, fc2_up, fc2_down, *fc1_plane
    )
    fc1_parts = spread_chips(add(mine(dw1, 0)[0], *fc1_plane))
    fc2_mine = add(*fc2_block(0), fc2_up, fc2_down).reshape(4, -1, D)
    dw_in = swap(dw_send, 1)
    plane_peer = swap(plane, 1)

    def ring(step, total):
        block = pick_mod(fc1_parts, (me + 2 * mods_n - 1 - step) % mods_n)
        return block if total is None else add(block, total)

    ff_ring = shift(ring(0, None), 1)
    dw_keep = qkv_weight(a, dq2, dk2, dv2, dwp_keep, LONG)
    dw_keep, dt2, dbq2, ff_ring, dw_in, plane_peer = fence(dw_keep, dt2, dbq2, ff_ring, dw_in, plane_peer)
    packed = pack_small(idx, dbq1, dbq2, db_proj, db1_first, db1_second, db_fc2, dt1, dt2).astype(bf16)
    packed = add(packed, swap(packed, 1))
    ff_ring = shift(ring(1, ff_ring), 1)
    d_h, ff_ring = fence(d_h, ff_ring)
    ff_ring = shift(ring(2, ff_ring), 1)

    dw = quarters_of([dw_keep, dw_in])

    def quarter(other):
        total = mine(dw, other)
        total = jnp.concatenate([total[0], total[1], packed], axis=1).reshape(-1, D)
        return jnp.concatenate([total, pick_mod(fc2_mine, lax.bitwise_xor(spot, other))])

    from_plane = [swap(quarter(n), 2 * n) for n in (1, 2, 3)]
    dx, d_mod = back_entry(
        idx, long_one, valid_seg, (dq1, dk1, dv1, dq2, dk2, dv2), x, d_h, mods, dmod_mid, own_a, set_a, peer_a
    )
    d_mod, dx, ff_ring = fence(d_mod, dx, ff_ring)
    mod_in = [pick_mod(d_mod, me)] + [shift(pick_mod(d_mod, (me + k) % mods_n), k) for k in range(1, mods_n)]
    share = cond_share(w_ada, mod_in)
    share, *from_plane = fence(share, *from_plane)
    parts = spread_chips(add(quarter(0), *from_plane))
    fc2_part = parts[-D // 8 :]
    parts = parts[: -D // 8].reshape(mods_n, -1, D)
    tail = [jnp.concatenate([pick_mod(parts, (me + k) % mods_n), share]) for k in range(mods_n)]
    tail_in = [shift(tail[k], k) for k in range(1, mods_n)]
    fc1_part = ring(3, ff_ring)
    ff_part = jnp.concatenate([fc1_part[:, :D], fc1_part[:, D:], fc2_part])
    ff_set = [ff_part, swap(ff_part, 2), swap(ff_part, 4)]
    def gather_chips(piece):
        mine = jnp.stack(three(piece))
        return mine, swap(mine, 1)

    *ff_set, tail_in[0], tail_in[1], tail_in[2] = fence(*ff_set, *tail_in)
    piece, small_all = tail_sum([tail[0]] + tail_in, mod_in, packets)
    grad_rel = jnp.concatenate([small_all[:3], small_all[3].reshape(3, 2 * L - D)], axis=1)[:, : rel_table.shape[1]]
    grad_qv, grad_fc1_b = small_all[5, : qv_bias.shape[0]], small_all[4]
    grad_proj_b, grad_fc2_b = take(small_all[6], me, proj_bias.shape[0]), take(small_all[7], me, fc2_bias.shape[0])
    grad_rel, grad_qv, grad_fc1_b, grad_proj_b, grad_fc2_b, *gathered = fence(
        grad_rel, grad_qv, grad_fc1_b, grad_proj_b, grad_fc2_b, *three(piece)
    )
    gathered = jnp.stack(gathered)
    gathered = gathered, swap(gathered, 1)
    ff_set = jnp.stack(ff_set + [swap(ff_part, 6)])
    grad_fc1, grad_fc2 = finish_ff(idx, ff_set, swap(ff_set, 1))
    grad_qkv, grad_proj = finish_attn(idx, *gathered)

    conds, acts = list(gathered), [plane, plane_peer]
    bit = 8
    while bit < lax.axis_size("dp"):
        conds += [swap(c, bit) for c in conds]
        acts += [swap(c, bit) for c in acts]
        bit *= 2
    grad_ada, grad_ada_b, grad_time, grad_class = finish_cond(
        idx, conds, acts, time_table.shape[0] // mods_n, w_ada.shape[1]
    )
    return (
        y.reshape(block_input.shape),
        dx.reshape(block_input.shape),
        grad_time,
        grad_class,
        grad_ada,
        grad_ada_b.reshape(-1),
        grad_qkv,
        grad_qv,
        grad_proj,
        grad_proj_b,
        grad_fc1,
        grad_fc1_b,
        grad_fc2,
        grad_fc2_b,
        grad_rel,
    )


def solution(mesh):
    in_specs = (
        P(None, ("dp", "mod"), None),
        P(None, ("dp", "mod"), None),
        P(None, ("dp", "mod")),
        P(None, ("dp", "mod")),
        P(None, ("dp", "mod")),
        P(None, ("dp", "mod")),
        P(),
        P(),
        P(None, "mod"),
        P("mod"),
        P("mod", None),
        P("mod"),
        P("mod", None),
        P("mod"),
        P("mod", None),
        P("mod"),
        P("mod", None),
        P("mod"),
        P("mod", None),
    )
    out_specs = (
        P(None, ("dp", "mod"), None),
        P(None, ("dp", "mod"), None),
        P("mod", None),
        P("mod", None),
        P(None, "mod"),
        P("mod"),
        P("mod", None),
        P("mod"),
        P("mod", None),
        P("mod"),
        P("mod", None),
        P("mod"),
        P("mod", None),
        P("mod"),
        P("mod", None),
    )
    return jax.shard_map(local, mesh=mesh, in_specs=in_specs, out_specs=out_specs, check_vma=False)
```

```python
from functools import partial
import jax
import jax.numpy as jnp
from jax import lax
from jax.experimental import pallas as pl
from jax.experimental.pallas import tpu as pltpu
from jax.sharding import PartitionSpec as P

f32 = jnp.float32
bf16 = jnp.bfloat16
D = 768
H = 12
HD = 64
FF = 3072
L = 512
SEG = 128
NSEG = 4
MICRO = 2
T = MICRO * L
HALF = 384
FH = 1536
VMEM_LIMIT = 56 * 1024 * 1024


LONG = pl.CostEstimate(flops=30_000_000_000, bytes_accessed=1_000_000, transcendentals=0)
SHORT = pl.CostEstimate(flops=1, bytes_accessed=1, transcendentals=0)


def params(*sem, size=16):
    return pltpu.CompilerParams(vmem_limit_bytes=size * 1024 * 1024, dimension_semantics=sem)


def dot(a, b, ca=1, cb=0):
    return lax.dot_general(a, b, (((ca,), (cb,)), ((), ())), preferred_element_type=f32)


def norm_of(values):
    centred = values - jnp.mean(values, axis=1, keepdims=True)
    inverse = lax.rsqrt(jnp.mean(centred * centred, axis=1, keepdims=True) + 1e-6)
    return centred * inverse, inverse


def norm_back(grad, normed, inverse):
    return inverse * (
        grad
        - jnp.mean(grad, axis=1, keepdims=True)
        - normed * jnp.mean(grad * normed, axis=1, keepdims=True)
    )


UR = 48
PR = 64
ANY = pl.BlockSpec(memory_space=pltpu.HBM)
SMEM = pl.BlockSpec(memory_space=pltpu.SMEM)
VMEM = pl.BlockSpec(memory_space=pltpu.VMEM)


def whole(shape):
    return pl.BlockSpec(shape, lambda *_: (0,) * len(shape))


def bring(copies, sems):
    made = [pltpu.make_async_copy(source, target, sems.at[n]) for n, (source, target) in enumerate(copies)]
    return made


def go(made):
    for copy in made:
        copy.start()


def ready(made):
    for copy in made:
        copy.wait()


def quarters(idx_ref, sources):
    me, spot = idx_ref[0], idx_ref[1]
    for ref, lead, other in sources:
        for k in range(1, 4):
            yield (
                ref.at[k - 1] if lead is None else ref.at[lead, k - 1],
                lax.rem(me + 4 - k, 4),
                lax.bitwise_xor(spot, other),
            )


def pick_entry_body(idx_ref, w_ref, proj_ref, own_ref, out_ref):
    spot, core = idx_ref[1], idx_ref[2]
    for n, half in enumerate((1 - core, core)):
        for u in range(3):
            column = pl.multiple_of((2 * u + half) * HALF, HALF)
            own_ref[n, u] = w_ref[:, pl.ds(column, HALF)].reshape(4, UR, HALF)
        own_ref[n, 3] = proj_ref[:, pl.ds(pl.multiple_of(half * HALF, HALF), HALF)].reshape(4, UR, HALF)
    for n, q in enumerate((spot, lax.bitwise_xor(spot, 3))):
        for u in range(4):
            out_ref[n, u] = own_ref[0, u, q]


def pick_entry(idx, w, proj):
    return pl.pallas_call(
        pick_entry_body,
        in_specs=[SMEM, VMEM, VMEM],
        out_specs=[VMEM, VMEM],
        out_shape=[pltpu.HBM((2, 4, 4, UR, HALF), bf16), pltpu.HBM((2, 4, UR, HALF), bf16)],
        compiler_params=params(),
        cost_estimate=SHORT,
        name="pick_entry",
    )(idx, w, proj)


def packet_body(idx_ref, step_ref, label_ref, cond_ref, bias_ref, rel_ref, out_ref):
    me = idx_ref[0]
    slots = MICRO * NSEG
    cond = cond_ref[...]
    sigma = 1.0 / (1.0 + jnp.exp(-cond))
    act = cond / (1.0 + jnp.exp(-cond))
    slope = sigma * (1.0 + cond * (1.0 - sigma))
    row = lax.broadcasted_iota(jnp.int32, (slots, HALF), 0)
    lane = lax.broadcasted_iota(jnp.int32, (slots, HALF), 1)
    digits = jnp.zeros((slots, HALF), jnp.int32)
    for n in range(slots):
        step, label = step_ref[n // NSEG, n % NSEG], label_ref[n // NSEG, n % NSEG]
        values = (step // 32, step % 32, label // 32, label % 32)
        for m, value in enumerate(values):
            digits = jnp.where((row == n) & (lane == m), value, digits)
    rel = rel_ref[...].astype(f32)
    rel = jnp.concatenate([rel, jnp.zeros((3, 1), f32)], axis=1)
    bias = bias_ref[...].astype(f32)
    pair = jnp.broadcast_to(bias[3:4], (8, HALF))
    lane = lax.broadcasted_iota(jnp.int32, (8, HALF), 1)
    blank = jnp.zeros((8, HALF), f32)
    proj_b = jnp.concatenate([jnp.where(lane < 192, pair, 0.0), blank], axis=1)
    fc2_b = jnp.concatenate([jnp.where(lane < 192, 0.0, pair), blank], axis=1)
    proj_b = pltpu.roll(proj_b, me * 192, 1)
    fc2_b = pltpu.roll(fc2_b, lax.rem(me + 3, 4) * 192, 1)
    out_ref[...] = jnp.concatenate(
        [
            act[:, :HALF],
            act[:, HALF:],
            digits.astype(f32),
            rel[:, :HALF],
            rel[:, HALF : 2 * HALF],
            jnp.concatenate([rel[:, 2 * HALF :], jnp.zeros((3, 128), f32)], axis=1),
            bias[0:3],
            proj_b[0:1, :HALF],
            proj_b[0:1, HALF:],
            fc2_b[0:1, :HALF],
            fc2_b[0:1, HALF:],
            jnp.zeros((8, HALF), f32),
            slope[:, :HALF],
            slope[:, HALF:],
        ],
        axis=0,
    ).astype(bf16)


def make_packet(idx, steps, labels, cond, bias, rel):
    return pl.pallas_call(
        packet_body,
        in_specs=[SMEM, SMEM, SMEM, VMEM, VMEM, VMEM],
        out_specs=VMEM,
        out_shape=jax.ShapeDtypeStruct((PR, HALF), bf16),
        compiler_params=params(),
        cost_estimate=SHORT,
        name="packet",
    )(idx, steps, labels, cond, bias, rel)


def pick_ff_body(idx_ref, fc1_ref, fc2_ref, own1_ref, own2_ref, piece1_ref, piece2_ref):
    spot, core = idx_ref[1], idx_ref[2]
    for n, half in enumerate((1 - core, core)):
        for z in range(4):
            column = pl.multiple_of((2 * z + half) * HALF, HALF)
            own1_ref[n, z] = fc1_ref[:, pl.ds(column, HALF)].reshape(4, UR, HALF)
        for j in range(2):
            for i in range(2):
                row = pl.multiple_of(half * HALF + i * 192, 192)
                own2_ref[n, 2 * j + i] = fc2_ref[pl.ds(row, 192), j * HALF : (j + 1) * HALF].reshape(4, UR, HALF)
    for n, q in enumerate((spot, lax.bitwise_xor(spot, 3))):
        for u in range(4):
            piece1_ref[n, u] = own1_ref[0, u, q]
            piece2_ref[n, u] = own2_ref[0, u, q]


def pick_ff(idx, fc1, fc2):
    return pl.pallas_call(
        pick_ff_body,
        in_specs=[SMEM, VMEM, VMEM],
        out_specs=[VMEM] * 4,
        out_shape=[pltpu.HBM((2, 4, 4, UR, HALF), bf16)] * 2 + [pltpu.HBM((2, 4, UR, HALF), bf16)] * 2,
        compiler_params=params(),
        cost_estimate=SHORT,
        name="pick_ff",
    )(idx, fc1, fc2)


def entry_copies(idx_ref, own, half, sources, held):
    return [(own.at[half, pl.ds(0, 3)], held.at[:, idx_ref[0]])] + [
        (ref.at[pl.ds(0, 3)], held.at[:, z, q]) for ref, z, q in quarters(idx_ref, sources)
    ]


def stacked(ref):
    return [(ref, n, n) for n in range(4)]


def proj_copies(idx_ref, own, half, at, sources, held):
    return [(own.at[half, 3], held.at[at, idx_ref[0]])] + [
        (ref.at[3], held.at[at, z, q]) for ref, z, q in quarters(idx_ref, sources)
    ]


def fc1_copies(idx_ref, own, half, sources, held):
    return [(own.at[half], held.at[:, idx_ref[0]])] + [
        (ref, held.at[:, z, q]) for ref, z, q in quarters(idx_ref, sources)
    ]


def fc2_copies(idx_ref, own, half, sources, held):
    return [(own.at[half, pl.ds(2 * j, 2)], held.at[j, idx_ref[0]]) for j in range(2)] + [
        (ref.at[pl.ds(2 * j, 2)], held.at[j, z, :, q]) for ref, z, q in quarters(idx_ref, sources) for j in range(2)
    ]


def entry_weight(held):
    return jnp.concatenate([held[u].reshape(D, HALF) for u in range(3)], axis=1)


def proj_weight(held):
    return jnp.concatenate([held[n].reshape(D, HALF) for n in range(2)], axis=1)


ENTRY_HELD = (3, 4, 4, UR, HALF)


def columns_body(w_ref, b_ref, p0, p1, p2, p3, c0, c1, c2, c3, held, sems):
    copies = bring([(p, held.at[k]) for k, p in enumerate((p0, p1, p2, p3))], sems)
    go(copies)
    ready(copies)
    slots = MICRO * NSEG
    units = [held[k].astype(f32) for k in range(4)]
    act = jnp.concatenate(
        [jnp.concatenate([u[:slots], u[slots : 2 * slots]], axis=1) for u in units], axis=0
    ).astype(bf16)
    out = dot(act, w_ref[...]) + b_ref[...].astype(f32)
    for k, c in enumerate((c0, c1, c2, c3)):
        c[...] = out[k * slots : (k + 1) * slots]


def mod_columns(w, b, payloads):
    return pl.pallas_call(
        columns_body,
        in_specs=[VMEM, VMEM] + [ANY] * 4,
        out_specs=[VMEM] * 4,
        out_shape=[jax.ShapeDtypeStruct((MICRO * NSEG, 3 * HALF), f32)] * 4,
        scratch_shapes=[pltpu.VMEM((4, PR, HALF), bf16), pltpu.SemaphoreType.DMA((4,))],
        compiler_params=params(),
        cost_estimate=SHORT,
        name="mod_columns",
    )(w, b, *payloads)


def prepare_body(idx_ref, long_ref, valid_ref, c0, c1, c2, c3, p0, p1, p2, p3,
                 mod_ref, qb1, qb2, pb_ref, ub1, ub2, fb_ref, r1, r2, cols, held, rows, sems):
    me, core = idx_ref[0], idx_ref[2]
    copies = bring([(p, held.at[lax.rem(me + 4 - k, 4)]) for k, p in enumerate((p0, p1, p2, p3))], sems)
    go(copies)
    for k, c in enumerate((c0, c1, c2, c3)):
        cols[lax.rem(me + k, 4)] = c[...]
    ready(copies)
    rows[...] = held[...].astype(f32)
    slots = MICRO * NSEG
    row = lax.broadcasted_iota(jnp.int32, (slots, 1), 0)
    upper = row < NSEG
    is_long = jnp.where(upper, long_ref[0], long_ref[1]) > 0
    valid = jnp.zeros((slots, 1), f32)
    for n in range(slots):
        valid = jnp.where(row == n, valid_ref[n // NSEG, n % NSEG].astype(f32), valid)
    for g in range(12):
        value = cols[g // 3, :, (g % 3) * HALF : (g % 3 + 1) * HALF]
        value = jnp.where(is_long, jnp.where(upper, value[0:1], value[NSEG : NSEG + 1]), value)
        if (g // 2) % 3 == 2:
            value = value * valid
        mod_ref[g // 2, :, (g % 2) * HALF : (g % 2 + 1) * HALF] = value
    for half, qb, ub, r in ((1 - core, qb1, ub1, r1), (core, qb2, ub2, r2)):
        qb[:, :HALF] = rows[half, 33:34, :]
        qb[:, HALF : 2 * HALF] = jnp.zeros((1, HALF), f32)
        qb[:, 2 * HALF :] = rows[2 + half, 33:34, :]
        for z in range(4):
            ub[:, z * HALF : (z + 1) * HALF] = jnp.where(half > 0, rows[z, 35:36, :], rows[z, 34:35, :])
        for n in range(6):
            z, t, to = 2 * half + n // 3, n % 3, slice(n % 2, n % 2 + 1)
            r[n // 2, to, :HALF] = rows[z, 24 + t : 25 + t, :]
            r[n // 2, to, HALF : 2 * HALF] = rows[z, 27 + t : 28 + t, :]
            r[n // 2, to, 2 * HALF :] = rows[z, 30 + t : 31 + t, :256]
    for ref, at in ((pb_ref, 36), (fb_ref, 38)):
        for n in range(2):
            ref[:, n * HALF : (n + 1) * HALF] = (
                rows[0, at + n : at + n + 1, :]
                + rows[1, at + n : at + n + 1, :]
                + rows[2, at + n : at + n + 1, :]
                + rows[3, at + n : at + n + 1, :]
            )


def prepare(idx, long_flag, valid_seg, columns, payloads):
    shapes = [(6, MICRO * NSEG, D), (1, 3 * HALF), (1, 3 * HALF), (1, D), (1, FH), (1, FH), (1, D),
              (3, 2, 2 * L), (3, 2, 2 * L)]
    return pl.pallas_call(
        prepare_body,
        in_specs=[SMEM] * 3 + [VMEM] * 4 + [ANY] * 4,
        out_specs=[VMEM] * 9,
        out_shape=[jax.ShapeDtypeStruct(shape, f32) for shape in shapes],
        scratch_shapes=[
            pltpu.VMEM((4, MICRO * NSEG, 3 * HALF), f32),
            pltpu.VMEM((4, PR, HALF), bf16),
            pltpu.VMEM((4, PR, HALF), f32),
            pltpu.SemaphoreType.DMA((4,)),
        ],
        compiler_params=params(),
        cost_estimate=SHORT,
        name="prepare",
    )(idx, long_flag, valid_seg, *columns, *payloads)


def entry_norm_body(x_ref, mod_ref, a_ref):
    i = pl.program_id(0)
    for s in range(2):
        rows = pl.ds(s * SEG, SEG)
        at = pl.ds(i * 2 + s, 1)
        norm, _ = norm_of(x_ref[rows, :].astype(f32))
        a_ref[rows, :] = (norm * (1.0 + mod_ref[1, at, :]) + mod_ref[0, at, :]).astype(bf16)


def entry_norm(x, mods):
    block = pl.BlockSpec((2 * SEG, D), lambda i: (i, 0))
    return pl.pallas_call(
        entry_norm_body,
        grid=(4,),
        in_specs=[block, whole((6, MICRO * NSEG, D))],
        out_specs=block,
        out_shape=jax.ShapeDtypeStruct((T, D), bf16),
        compiler_params=params("arbitrary"),
        cost_estimate=LONG,
        name="entry_norm",
    )(x, mods)


def qkv_body(half, idx_ref, a_ref, b_ref, own, fetched, qkv_ref, held, sems):
    copies = bring(entry_copies(idx_ref, own, half, stacked(fetched), held), sems)

    @pl.when(pl.program_id(0) == 0)
    def _():
        go(copies)
        ready(copies)

    qkv_ref[...] = (dot(a_ref[...], entry_weight(held)) + b_ref[...]).astype(bf16)


def qkv_half(half, idx, a, b, own, near):
    return pl.pallas_call(
        partial(qkv_body, half),
        grid=(MICRO,),
        in_specs=[
            SMEM,
            pl.BlockSpec((L, D), lambda i: (i, 0)),
            whole((1, 3 * HALF)),
            ANY,
            ANY,
        ],
        out_specs=pl.BlockSpec((L, 3 * HALF), lambda i: (i, 0)),
        out_shape=jax.ShapeDtypeStruct((T, 3 * HALF), bf16),
        scratch_shapes=[pltpu.VMEM(ENTRY_HELD, bf16), pltpu.SemaphoreType.DMA((13,))],
        compiler_params=params("arbitrary"),
        cost_estimate=SHORT,
        name="qkv_half",
    )(idx, a, b, own, near)


def lane_reverse(rows):
    at = lax.broadcasted_iota(jnp.int32, (2 * SEG, 2 * SEG), 0) + lax.broadcasted_iota(jnp.int32, (2 * SEG, 2 * SEG), 1)
    turn = (at == 2 * SEG - 2).astype(f32)
    return lax.dot_general(
        rows, turn, (((1,), (0,)), ((), ())), precision=lax.Precision.HIGHEST, preferred_element_type=f32
    )


def attend_body(long_ref, valid_ref, q_ref, k_ref, v_ref, t_ref, o_ref, p_ref, bias_ref):
    b = pl.program_id(1)

    @pl.when(b == 0)
    def _():
        windows = [t_ref[0, h : h + 1, d * SEG : (d + 2) * SEG] for h in range(2) for d in range(7)]
        windows = lane_reverse(jnp.concatenate(windows + windows[:2], axis=0))
        for h in range(2):
            for d in range(7):
                row = jnp.broadcast_to(windows[h * 7 + d : h * 7 + d + 1, :], (SEG, 2 * SEG))
                bias_ref[h, d] = pltpu.roll(row, SEG + 1, 1, stride=1, stride_axis=0)[:, :SEG]

    is_long = long_ref[b]
    lane = lax.broadcasted_iota(jnp.int32, (L, 2 * HD), 1)
    query = q_ref[...] * jnp.asarray(HD**-0.5, bf16)
    keys = k_ref[...]
    values_t = v_ref[...].T
    outs = []
    for h in range(2):
        mine = (lane < HD) if h == 0 else (lane >= HD)
        key_h = jnp.where(mine, keys, jnp.zeros_like(keys))
        for qb in range(NSEG):
            cols = pl.ds(qb * SEG, SEG)
            scores = dot(key_h, query[qb * SEG : (qb + 1) * SEG, :], 1, 1)
            parts = []
            for kb in range(NSEG):
                open_ = (valid_ref[b, kb] > 0) if kb == qb else ((valid_ref[b, kb] > 0) & (is_long > 0))
                shut = jnp.where(open_, 0.0, -1e30).astype(f32)
                parts.append(scores[kb * SEG : (kb + 1) * SEG, :] + (bias_ref[h, kb - qb + 3] + shut))
            scores = jnp.concatenate(parts, axis=0)
            top = jnp.max(scores, axis=0, keepdims=True)
            expo = jnp.exp(scores - top)
            total = jnp.sum(expo, axis=0, keepdims=True)
            p_ref[0, h, :, cols] = (expo * (1.0 / total)).astype(bf16)
        outs.append(dot(values_t[h * HD : (h + 1) * HD, :], p_ref[0, h]))
    o_ref[...] = jnp.concatenate(outs, axis=0).T.astype(bf16)


def attend(qkv, table, long_flag, valid_seg, cost):
    pairs = 3
    return pl.pallas_call(
        attend_body,
        grid_spec=pltpu.PrefetchScalarGridSpec(
            num_scalar_prefetch=2,
            grid=(pairs, MICRO),
            in_specs=[
                pl.BlockSpec((L, 2 * HD), lambda g, b, *_: (b, g)),
                pl.BlockSpec((L, 2 * HD), lambda g, b, *_: (b, 3 + g)),
                pl.BlockSpec((L, 2 * HD), lambda g, b, *_: (b, 6 + g)),
                pl.BlockSpec((1, 2, 2 * L), lambda g, b, *_: (g, 0, 0)),
            ],
            out_specs=[
                pl.BlockSpec((L, 2 * HD), lambda g, b, *_: (b, g)),
                pl.BlockSpec((1, 2, L, L), lambda g, b, *_: (b, g, 0, 0)),
            ],
            scratch_shapes=[pltpu.VMEM((2, 7, SEG, SEG), f32)],
        ),
        out_shape=[
            jax.ShapeDtypeStruct((T, HALF), bf16),
            pltpu.HBM((MICRO, 6, L, L), bf16),
        ],
        compiler_params=params("arbitrary", "arbitrary"),
        cost_estimate=cost,
        name="attend",
    )(long_flag, valid_seg, qkv, qkv, qkv, table)


def middle_body(idx_ref, o1_ref, o2_ref, b_ref, x_ref, dy_ref, mod_ref, own, fetched, peer,
                h_ref, m_ref, attn_ref, dmlp_ref, db_ref, held, w_ref, sems):
    core = idx_ref[2]
    i = pl.program_id(0)

    @pl.when(i == 0)
    def _():
        copies = bring(
            proj_copies(idx_ref, own, 0, 1 - core, stacked(fetched), held)
            + proj_copies(idx_ref, own, 1, core, stacked(peer), held),
            sems,
        )
        go(copies)
        ready(copies)
        w_ref[...] = proj_weight(held)

    first = pl.multiple_of((1 - core) * HALF, HALF)
    second = pl.multiple_of(core * HALF, HALF)
    attn = dot(o1_ref[...], w_ref[pl.ds(first, HALF), :]) + dot(o2_ref[...], w_ref[pl.ds(second, HALF), :])
    attn = attn + b_ref[...]
    attn_ref[...] = attn.astype(bf16)
    total = jnp.zeros((1, D), f32)
    for s in range(NSEG):
        rows = pl.ds(s * SEG, SEG)
        at = pl.ds(i * NSEG + s, 1)
        hidden = x_ref[rows, :].astype(f32) + mod_ref[2, at, :] * attn[s * SEG : (s + 1) * SEG, :]
        h_ref[rows, :] = hidden
        norm, _ = norm_of(hidden)
        m_ref[rows, :] = (norm * (1.0 + mod_ref[4, at, :]) + mod_ref[3, at, :]).astype(bf16)
        dmlp = (dy_ref[rows, :].astype(f32) * mod_ref[5, at, :]).astype(bf16)
        dmlp_ref[rows, :] = dmlp
        total = total + jnp.sum(dmlp.astype(f32), axis=0, keepdims=True)

    @pl.when(pl.program_id(0) == 0)
    def _():
        db_ref[...] = jnp.zeros_like(db_ref)

    db_ref[0:1, :] += total


def middle(idx, o1, o2, b, x, dy, mods, own, one, two):
    row = lambda i: (i, 0)
    return pl.pallas_call(
        middle_body,
        grid=(MICRO,),
        in_specs=[
            SMEM,
            pl.BlockSpec((L, HALF), row),
            pl.BlockSpec((L, HALF), row),
            whole((1, D)),
            pl.BlockSpec((L, D), row),
            pl.BlockSpec((L, D), row),
            whole((6, MICRO * NSEG, D)),
        ] + [ANY] * 3,
        out_specs=[
            pl.BlockSpec((L, D), row),
            pl.BlockSpec((L, D), row),
            pl.BlockSpec((L, D), row),
            pl.BlockSpec((L, D), row),
            whole((8, D)),
        ],
        out_shape=[
            pltpu.HBM((T, D), f32),
            jax.ShapeDtypeStruct((T, D), bf16),
            pltpu.HBM((T, D), bf16),
            jax.ShapeDtypeStruct((T, D), bf16),
            jax.ShapeDtypeStruct((8, D), f32),
        ],
        scratch_shapes=[
            pltpu.VMEM((2, 4, 4, UR, HALF), bf16),
            pltpu.VMEM((D, D), bf16),
            pltpu.SemaphoreType.DMA((26,)),
        ],
        compiler_params=params("arbitrary"),
        cost_estimate=LONG,
        name="middle",
    )(idx, o1, o2, b, x, dy, mods, own, one, two)


FB = 768


def mlp_body(has_acc, idx_ref, m_ref, dmlp_ref, b_ref, own1, own2, fetched1, fetched2, *refs):
    if has_acc:
        acc_o, acc_d, out_o, out_d, dw1_ref, dw2_ref, db_ref, g_s, du_s, held1, held2, sems = refs
    else:
        out_o, out_d, dw1_ref, dw2_ref, db_ref, g_s, du_s, held1, held2, sems = refs
    f = pl.program_id(0)
    half_index = 1 if has_acc else 0

    @pl.when(f == 0)
    def _():
        copies = bring(
            fc1_copies(idx_ref, own1, half_index, stacked(fetched1), held1)
            + fc2_copies(idx_ref, own2, half_index, stacked(fetched2), held2),
            sems,
        )
        go(copies)
        ready(copies)

    w1 = jnp.concatenate([held1[2 * f + n].reshape(D, HALF) for n in range(2)], axis=1)
    w2 = jnp.concatenate([held2[j, pl.ds(2 * f, 2)].reshape(D, HALF) for j in range(2)], axis=1)
    bias = b_ref[0:1, :]
    chunk = 256
    total = jnp.zeros((1, FB), f32)
    c0 = (2.0 / jnp.pi) ** 0.5
    for r in range(T // chunk):
        rows = pl.ds(r * chunk, chunk)
        u = dot(m_ref[rows, :], w1) + bias
        dg = dot(dmlp_ref[rows, :], w2, 1, 1)
        u2 = u * u
        th = jnp.tanh(u * (c0 + (c0 * 0.044715) * u2))
        half = 0.5 + 0.5 * th
        g_s[rows, :] = (u * half).astype(bf16)
        slope = half + u * (0.5 - 0.5 * th * th) * (c0 + (3.0 * c0 * 0.044715) * u2)
        du = (dg * slope).astype(bf16)
        du_s[rows, :] = du
        total = total + jnp.sum(du.astype(f32), axis=0, keepdims=True)
    db_ref[0:1, :] = total

    @pl.when(f == 0)
    def _():
        if has_acc:
            out_o[...] = acc_o[...] + dot(g_s[...], w2)
            out_d[...] = acc_d[...] + dot(du_s[...], w1, 1, 1)
        else:
            out_o[...] = dot(g_s[...], w2)
            out_d[...] = dot(du_s[...], w1, 1, 1)

    @pl.when(f > 0)
    def _():
        out_o[...] += dot(g_s[...], w2)
        out_d[...] += dot(du_s[...], w1, 1, 1)

    dw2_ref[...] = dot(g_s[...], dmlp_ref[...], 0, 0).astype(bf16)
    dw1_ref[...] = dot(m_ref[...], du_s[...], 0, 0).astype(bf16)


def mlp(idx, m_in, dmlp, b1, own1, own2, fetched1, fetched2, acc=None):
    zero = lambda f: (0, 0)
    col = lambda f: (0, f)
    once = pl.Buffered(1)
    specs = [
        SMEM,
        pl.BlockSpec((T, D), zero, pipeline_mode=once),
        pl.BlockSpec((T, D), zero, pipeline_mode=once),
        pl.BlockSpec((1, FB), col),
    ] + [ANY] * 4
    args = [idx, m_in, dmlp, b1, own1, own2, fetched1, fetched2]
    if acc is not None:
        specs += [pl.BlockSpec((T, D), zero, pipeline_mode=once)] * 2
        args += list(acc)
    return pl.pallas_call(
        partial(mlp_body, acc is not None),
        grid=(FH // FB,),
        in_specs=specs,
        out_specs=[
            pl.BlockSpec((T, D), zero),
            pl.BlockSpec((T, D), zero),
            pl.BlockSpec((D, FB), col),
            pl.BlockSpec((FB, D), lambda f: (f, 0)),
            pl.BlockSpec((8, FB), col),
        ],
        out_shape=[
            jax.ShapeDtypeStruct((T, D), f32),
            jax.ShapeDtypeStruct((T, D), f32),
            pltpu.HBM((D, FH), bf16),
            pltpu.HBM((FH, D), bf16),
            jax.ShapeDtypeStruct((8, FH), f32),
        ],
        scratch_shapes=[
            pltpu.VMEM((T, FB), bf16),
            pltpu.VMEM((T, FB), bf16),
            pltpu.VMEM((4, 4, 4, UR, HALF), bf16),
            pltpu.VMEM((2, 4, 2, 4, UR, HALF), bf16),
            pltpu.SemaphoreType.DMA((39,)),
        ],
        compiler_params=params("arbitrary", size=44),
        cost_estimate=LONG,
        name="mlp",
    )(*args)


def back_middle_body(idx_ref, h_ref, dy_ref, mlp_ref, b2_ref, dm_ref, attn_ref, mod_ref, o1_ref, o2_ref,
                     own, fetched, peer,
                     y_ref, dh_ref, do1_ref, do2_ref, dws_ref, dwk_ref, dmod_ref, db_ref,
                     dattn_s, dw_s, held, w_ref, sems):
    i = pl.program_id(0)
    core = idx_ref[2]
    first = pl.multiple_of((1 - core) * HALF, HALF)
    second = pl.multiple_of(core * HALF, HALF)
    copies = bring(
        proj_copies(idx_ref, own, 0, 1 - core, stacked(fetched), held)
        + proj_copies(idx_ref, own, 1, core, stacked(peer), held),
        sems,
    )

    @pl.when(i == 0)
    def _():
        go(copies)

    total = jnp.zeros((1, D), f32)
    for s in range(NSEG):
        rows = pl.ds(s * SEG, SEG)
        at = pl.ds(i * NSEG + s, 1)
        hidden = h_ref[rows, :]
        dy = dy_ref[rows, :].astype(f32)
        ff = mlp_ref[rows, :] + b2_ref[...]
        y_ref[rows, :] = (hidden + mod_ref[5, at, :] * ff).astype(bf16)
        dmod_ref[5, at, :] = jnp.sum(dy * ff, axis=0, keepdims=True)
        norm, inverse = norm_of(hidden)
        dm = dm_ref[rows, :]
        dmod_ref[3, at, :] = jnp.sum(dm, axis=0, keepdims=True)
        dmod_ref[4, at, :] = jnp.sum(dm * norm, axis=0, keepdims=True)
        dh = dy + norm_back(dm * (1.0 + mod_ref[4, at, :]), norm, inverse)
        dh_ref[rows, :] = dh
        dmod_ref[2, at, :] = jnp.sum(dh * attn_ref[rows, :].astype(f32), axis=0, keepdims=True)
        dattn = (dh * mod_ref[2, at, :]).astype(bf16)
        dattn_s[rows, :] = dattn
        total = total + jnp.sum(dattn.astype(f32), axis=0, keepdims=True)
    dattn = dattn_s[...]

    @pl.when(i == 0)
    def _():
        ready(copies)
        w_ref[...] = proj_weight(held)

    do1_ref[...] = dot(dattn, w_ref[pl.ds(first, HALF), :], 1, 1).astype(bf16)
    do2_ref[...] = dot(dattn, w_ref[pl.ds(second, HALF), :], 1, 1).astype(bf16)

    @pl.when(i == 0)
    def _():
        db_ref[...] = jnp.zeros_like(db_ref)
        dmod_ref[0:2] = jnp.zeros((2, MICRO * NSEG, D), f32)
        dw_s[...] = jnp.zeros_like(dw_s)

    db_ref[0:1, :] += total
    dw_s[pl.ds(first, HALF), :] += dot(o1_ref[...], dattn, 0, 0)
    dw_s[pl.ds(second, HALF), :] += dot(o2_ref[...], dattn, 0, 0)

    @pl.when(i == MICRO - 1)
    def _():
        dws_ref[...] = dw_s[:, pl.ds(first, HALF)].astype(bf16)
        dwk_ref[...] = dw_s[:, pl.ds(second, HALF)].astype(bf16)


def back_middle(idx, h, dy, ff, b2, dm, attn, mods, o1, o2, own, one, two):
    row = lambda i: (i, 0)
    full = pl.BlockSpec((L, D), row)
    part = pl.BlockSpec((L, HALF), row)
    modspec = whole((6, MICRO * NSEG, D))
    return pl.pallas_call(
        back_middle_body,
        grid=(MICRO,),
        in_specs=[SMEM, full, full, full, whole((1, D)), full, full, modspec, part, part] + [ANY] * 3,
        out_specs=[full, full, part, part, whole((D, HALF)), whole((D, HALF)), modspec, whole((8, D))],
        scratch_shapes=[
            pltpu.VMEM((L, D), bf16),
            pltpu.VMEM((D, D), f32),
            pltpu.VMEM((2, 4, 4, UR, HALF), bf16),
            pltpu.VMEM((D, D), bf16),
            pltpu.SemaphoreType.DMA((26,)),
        ],
        out_shape=[
            pltpu.HBM((T, D), bf16),
            pltpu.HBM((T, D), f32),
            jax.ShapeDtypeStruct((T, HALF), bf16),
            jax.ShapeDtypeStruct((T, HALF), bf16),
            jax.ShapeDtypeStruct((D, HALF), bf16),
            jax.ShapeDtypeStruct((D, HALF), bf16),
            jax.ShapeDtypeStruct((6, MICRO * NSEG, D), f32),
            jax.ShapeDtypeStruct((8, D), f32),
        ],
        compiler_params=params("arbitrary", size=28),
        cost_estimate=LONG,
        name="back_middle",
    )(idx, h, dy, ff, b2, dm, attn, mods, o1, o2, own, one, two)


def attend_back_body(q_ref, k_ref, v_ref, p_ref, do_ref, o_ref, dq_ref, dk_ref, dv_ref, dt_ref, db_ref, acc_ref, ds_s):
    b = pl.program_id(1)

    @pl.when(b == 0)
    def _():
        acc_ref[...] = jnp.zeros_like(acc_ref)
        db_ref[...] = jnp.zeros_like(db_ref)

    lane = lax.broadcasted_iota(jnp.int32, (L, 2 * HD), 1)
    query = q_ref[...]
    keys_t = k_ref[...].T
    values = v_ref[...]
    dout = do_ref[...]
    prod = (dout.astype(f32) * o_ref[...].astype(f32)).T
    dqs, dks, dvs = [], [], []
    for h in range(2):
        mine = (lane < HD) if h == 0 else (lane >= HD)
        value_h = jnp.where(mine, values, jnp.zeros_like(values))
        delta = jnp.sum(prod[h * HD : (h + 1) * HD, :], axis=0, keepdims=True)
        for qb in range(NSEG):
            cols = slice(qb * SEG, (qb + 1) * SEG)
            dp = dot(value_h, dout[cols, :], 1, 1)
            ds = (p_ref[0, h, :, cols].astype(f32) * (dp - delta[:, cols])).astype(bf16)
            ds_s[h, :, cols] = ds
            for kb in range(NSEG):
                acc_ref[h, kb - qb + 3] += ds[kb * SEG : (kb + 1) * SEG, :].astype(f32)
        dvs.append(dot(p_ref[0, h], dout))
        dks.append(dot(ds_s[h], query))
        dqs.append(dot(keys_t[h * HD : (h + 1) * HD, :], ds_s[h]))
    low = lane < HD
    scale = HD**-0.5
    dq = (jnp.concatenate(dqs, axis=0).T * scale).astype(bf16)
    dk = (jnp.where(low, dks[0], dks[1]) * scale).astype(bf16)
    dv = jnp.where(low, dvs[0], dvs[1]).astype(bf16)
    dq_ref[...] = dq
    dk_ref[...] = dk
    dv_ref[...] = dv
    db_ref[0:1, :] += jnp.sum(dq.astype(f32), axis=0, keepdims=True)
    db_ref[1:2, :] += jnp.sum(dv.astype(f32), axis=0, keepdims=True)

    @pl.when(b == MICRO - 1)
    def _():
        sums = []
        for h in range(2):
            for d in range(7):
                wide = jnp.concatenate([acc_ref[h, d], jnp.zeros((SEG, SEG), f32)], axis=1)
                rows = SEG
                while rows > 1:
                    rows //= 2
                    wide = pltpu.roll(wide[:rows], rows, 1) + wide[rows:]
                sums.append(wide)
        sums = lane_reverse(jnp.concatenate(sums + sums[:2], axis=0))
        dt_ref[...] = jnp.zeros_like(dt_ref)
        for h in range(2):
            for d in range(7):
                dt_ref[0, h : h + 1, d * SEG : (d + 2) * SEG] += sums[h * 7 + d : h * 7 + d + 1, :]


def attend_back(qkv, p, dout, out, cost):
    col = lambda g, b: (b, g)
    part = pl.BlockSpec((L, 2 * HD), col)
    return pl.pallas_call(
        attend_back_body,
        grid=(3, MICRO),
        in_specs=[
            part,
            pl.BlockSpec((L, 2 * HD), lambda g, b: (b, 3 + g)),
            pl.BlockSpec((L, 2 * HD), lambda g, b: (b, 6 + g)),
            pl.BlockSpec((1, 2, L, L), lambda g, b: (b, g, 0, 0)),
            part,
            part,
        ],
        out_specs=[part, part, part, pl.BlockSpec((1, 8, 2 * L), lambda g, b: (g, 0, 0)),
                   pl.BlockSpec((8, 2 * HD), lambda g, b: (0, g))],
        out_shape=[jax.ShapeDtypeStruct((T, HALF), bf16)] * 3
        + [jax.ShapeDtypeStruct((3, 8, 2 * L), f32), jax.ShapeDtypeStruct((8, HALF), f32)],
        scratch_shapes=[pltpu.VMEM((2, 7, SEG, SEG), f32), pltpu.VMEM((2, L, L), bf16)],
        compiler_params=params("arbitrary", "arbitrary"),
        cost_estimate=cost,
        name="attend_back",
    )(qkv, qkv, qkv, p, dout, out)


def qkv_weight_body(a_ref, dq_ref, dk_ref, dv_ref, proj_ref, out_ref):
    a = a_ref[...]
    grads = jnp.concatenate([dq_ref[...], dk_ref[...]], axis=1)
    out_ref[0] = dot(a, grads, 0, 0).astype(bf16)
    out_ref[1, :, :HALF] = dot(a, dv_ref[...], 0, 0).astype(bf16)
    out_ref[1, :, HALF:] = proj_ref[...]


def qkv_weight(a, dq, dk, dv, proj, cost):
    return pl.pallas_call(
        qkv_weight_body,
        out_shape=jax.ShapeDtypeStruct((2, D, D), bf16),
        compiler_params=params(),
        cost_estimate=cost,
        name="qkv_weight",
    )(a, dq, dk, dv, proj)


def back_entry_body(idx_ref, long_ref, valid_ref, dq1, dk1, dv1, dq2, dk2, dv2, x_ref, dh_ref, mod_ref, mid_ref,
                    own, fetched, peer, dx_ref, out_ref, held1, held2, entry_ref, sems):
    i = pl.program_id(0)

    @pl.when(i == 0)
    def _():
        copies = bring(
            entry_copies(idx_ref, own, 0, stacked(fetched), held1) + entry_copies(idx_ref, own, 1, stacked(peer), held2),
            sems,
        )
        go(copies)
        ready(copies)

    one = jnp.concatenate([dq1[...], dk1[...], dv1[...]], axis=1)
    two = jnp.concatenate([dq2[...], dk2[...], dv2[...]], axis=1)
    da = dot(one, entry_weight(held1), 1, 1) + dot(two, entry_weight(held2), 1, 1)
    for s in range(NSEG):
        rows = pl.ds(s * SEG, SEG)
        at = pl.ds(i * NSEG + s, 1)
        piece = da[s * SEG : (s + 1) * SEG, :]
        norm, inverse = norm_of(x_ref[rows, :].astype(f32))
        entry_ref[0, at, :] = jnp.sum(piece, axis=0, keepdims=True)
        entry_ref[1, at, :] = jnp.sum(piece * norm, axis=0, keepdims=True)
        dx_ref[rows, :] = (
            dh_ref[rows, :] + norm_back(piece * (1.0 + mod_ref[1, at, :]), norm, inverse)
        ).astype(bf16)

    @pl.when(i == MICRO - 1)
    def _():
        slots = MICRO * NSEG
        row = lax.broadcasted_iota(jnp.int32, (slots, 1), 0)
        upper = row < NSEG
        is_long = jnp.where(upper, long_ref[0], long_ref[1]) > 0
        valid = jnp.zeros((slots, 1), f32)
        for n in range(slots):
            valid = jnp.where(row == n, valid_ref[n // NSEG, n % NSEG].astype(f32), valid)
        lead = (row == 0) | (row == NSEG)
        blocks = []
        for j in range(6):
            value = entry_ref[j] if j < 2 else mid_ref[j]
            if j % 3 == 2:
                value = value * valid
            total = jnp.where(
                upper,
                jnp.sum(value[:NSEG], axis=0, keepdims=True),
                jnp.sum(value[NSEG:], axis=0, keepdims=True),
            )
            value = jnp.where(is_long, jnp.where(lead, total, 0.0), value)
            blocks += [value[:, :HALF], value[:, HALF:]]
        blank = jnp.zeros((slots, HALF), f32)
        for z in range(4):
            out_ref[z] = jnp.concatenate(
                [
                    jnp.concatenate(blocks[3 * z : 3 * z + 2], axis=1),
                    jnp.concatenate([blocks[3 * z + 2], blank], axis=1),
                ],
                axis=0,
            ).astype(bf16)


def back_entry(idx, long_flag, valid_seg, parts, x, dh, mods, mid, own, near, peer):
    row = lambda i: (i, 0)
    full = pl.BlockSpec((L, D), row)
    part = pl.BlockSpec((L, HALF), row)
    slots = MICRO * NSEG
    return pl.pallas_call(
        back_entry_body,
        grid=(MICRO,),
        in_specs=[SMEM] * 3 + [part] * 6 + [full, full, whole((6, slots, D)), whole((6, slots, D))] + [ANY] * 3,
        out_specs=[full, whole((4, 2 * slots, D))],
        out_shape=[pltpu.HBM((T, D), bf16), jax.ShapeDtypeStruct((4, 2 * slots, D), bf16)],
        scratch_shapes=[
            pltpu.VMEM(ENTRY_HELD, bf16),
            pltpu.VMEM(ENTRY_HELD, bf16),
            pltpu.VMEM((2, slots, D), f32),
            pltpu.SemaphoreType.DMA((26,)),
        ],
        compiler_params=params("arbitrary", size=24),
        cost_estimate=LONG,
        name="back_entry",
    )(idx, long_flag, valid_seg, *parts, x, dh, mods, mid, own, near, peer)


def cond_share_body(w_ref, d0, d1, d2, d3, out_ref):
    slots = MICRO * NSEG
    rows = [d[...].astype(f32) for d in (d0, d1, d2, d3)]
    rows = [jnp.concatenate([r[:slots], r[slots:, :HALF]], axis=1) for r in rows]
    out_ref[...] = dot(jnp.concatenate(rows, axis=0).astype(bf16), w_ref[...], 1, 1).astype(bf16)


def cond_share(w, blocks):
    return pl.pallas_call(
        cond_share_body,
        in_specs=[VMEM] * 5,
        out_specs=VMEM,
        out_shape=jax.ShapeDtypeStruct((4 * MICRO * NSEG, D), bf16),
        compiler_params=params(),
        cost_estimate=SHORT,
        name="cond_share",
    )(w, *blocks)


def pack_small_body(idx_ref, q1, q2, proj_ref, u1, u2, fc2_ref, t1, t2, out_ref):
    core = idx_ref[2]
    for z in range(4):
        half = z // 2
        tail = []
        for t in range(3):
            n = (z % 2) * 3 + t
            row = jnp.where(core == half, t2[n // 2, n % 2 : n % 2 + 1, :], t1[n // 2, n % 2 : n % 2 + 1, :])
            out_ref[z, t : t + 1, :] = row[:, :D]
            tail.append(row[:, D:])
        out_ref[z, 3:4, :] = jnp.concatenate(tail, axis=1)
        for h in range(2):
            block = slice(z * HALF, (z + 1) * HALF)
            out_ref[z, 4:5, h * HALF : (h + 1) * HALF] = jnp.where(core == h, u2[0:1, block], u1[0:1, block])
        half, kind = z % 2, z // 2
        out_ref[z, 5:6, 0:HALF] = jnp.where(core == half, q2[kind : kind + 1, :], q1[kind : kind + 1, :])
        out_ref[z, 5:6, HALF:] = jnp.zeros((1, HALF), f32)
        out_ref[z, 6:7, :] = proj_ref[0:1, :]
        out_ref[z, 7:8, :] = fc2_ref[0:1, :]


def pack_small(idx, *arrays):
    return pl.pallas_call(
        pack_small_body,
        in_specs=[SMEM] + [VMEM] * 8,
        out_specs=VMEM,
        out_shape=jax.ShapeDtypeStruct((4, 8, D), f32),
        compiler_params=params(),
        cost_estimate=SHORT,
        name="pack_small",
    )(idx, *arrays)


def finish_ff_body(idx_ref, mine_ref, peer_ref, fc1_ref, fc2_ref):
    spot, core = idx_ref[1], idx_ref[2]
    for source, half in ((mine_ref, core), (peer_ref, 1 - core)):
        for j in range(4):
            place_at = lax.bitwise_xor(spot, j)
            row = pl.multiple_of(place_at * 48, 16)
            for z in range(4):
                source_rows = pl.ds(48 * (z // 2), 48)
                block = source[j, source_rows, (z % 2) * HALF : (z % 2 + 1) * HALF]
                column = pl.multiple_of((2 * z + half) * HALF, 128)
                fc1_ref[pl.ds(row, 48), pl.ds(column, HALF)] = block.astype(f32)
            row = pl.multiple_of(half * HALF + place_at * 96, 16)
            fc2_ref[pl.ds(row, 96), :] = source[j, 96:192, :].astype(f32)


def finish_ff(idx, mine, peer):
    vmem = pl.BlockSpec(memory_space=pltpu.VMEM)
    return pl.pallas_call(
        finish_ff_body,
        in_specs=[pl.BlockSpec(memory_space=pltpu.SMEM), vmem, vmem],
        out_specs=[vmem, vmem],
        out_shape=[jax.ShapeDtypeStruct((D // 4, FF), f32), jax.ShapeDtypeStruct((FF // 4, D), f32)],
        compiler_params=params(),
        cost_estimate=SHORT,
        name="finish_ff",
    )(idx, mine, peer)


def finish_attn_body(idx_ref, mine_ref, peer_ref, qkv_ref, proj_ref):
    spot, core = idx_ref[1], idx_ref[2]
    for source, half in ((mine_ref, core), (peer_ref, 1 - core)):
        column = half * HALF
        for j in range(4):
            place_at = lax.bitwise_xor(spot, j)
            row = pl.multiple_of(place_at * 48, 16)
            for t in range(4):
                block = source[j, 48 * (t // 2) : 48 * (t // 2 + 1), (t % 2) * HALF : (t % 2 + 1) * HALF].astype(f32)
                if t < 3:
                    qkv_ref[pl.ds(row, 48), pl.ds(pl.multiple_of(t * D + column, 128), HALF)] = block
                else:
                    proj_ref[pl.ds(row, 48), pl.ds(pl.multiple_of(column, 128), HALF)] = block


def finish_attn(idx, mine, peer):
    vmem = pl.BlockSpec(memory_space=pltpu.VMEM)
    return pl.pallas_call(
        finish_attn_body,
        in_specs=[pl.BlockSpec(memory_space=pltpu.SMEM), vmem, vmem],
        out_specs=[vmem, vmem],
        out_shape=[jax.ShapeDtypeStruct((D // 4, 3 * D), f32), jax.ShapeDtypeStruct((D // 4, D), f32)],
        compiler_params=params(),
        cost_estimate=SHORT,
        name="finish_attn",
    )(idx, mine, peer)


def tail_sum_body(t0, t1, t2, t3, m0, m1, m2, m3, p0, p1, p2, p3, piece_ref, small_ref):
    slots = MICRO * NSEG
    arrived = [t[...].astype(f32) for t in (t0, t1, t2, t3)]
    rows = D // 8
    small_ref[...] = sum(t[rows : rows + 8] for t in arrived)
    blocks = [sum(t[:rows] for t in arrived)]
    for k, (m, p) in enumerate(((m0, p0), (m1, p1), (m2, p2), (m3, p3))):
        total = jnp.zeros((slots, D), f32)
        for j, t in enumerate(arrived):
            at = rows + 8 + (k - j) % 4 * slots
            total = total + t[at : at + slots]
        packet = p[...].astype(f32)
        slope = jnp.concatenate([packet[UR : UR + slots], packet[UR + slots : UR + 2 * slots]], axis=1)
        blocks += [m[...].astype(f32), total * slope]
    piece_ref[...] = jnp.concatenate(blocks, axis=0).astype(bf16)


def tail_sum(arrived, mods, packets):
    return pl.pallas_call(
        tail_sum_body,
        in_specs=[VMEM] * 12,
        out_specs=[VMEM, VMEM],
        out_shape=[jax.ShapeDtypeStruct((D // 4, D), bf16), jax.ShapeDtypeStruct((8, D), f32)],
        compiler_params=params(),
        cost_estimate=SHORT,
        name="tail_sum",
    )(*arrived, *mods, *packets)


def finish_cond_body(n, share, idx_ref, *refs):
    gathered, planes = refs[:n], refs[n : 2 * n]
    ada_ref, bias_ref, time_ref, class_ref = refs[2 * n :]
    slots = MICRO * NSEG
    acts, mods, conds, digits = [], [], [], []
    for g, p in zip(gathered, planes):
        for j in range(4):
            block = g[j, D // 8 :, :].astype(f32)
            for k in range(4):
                at = 3 * slots * k
                mods.append(
                    jnp.concatenate([block[at : at + slots], block[at + slots : at + 2 * slots, :HALF]], axis=1)
                )
                conds.append(block[at + 2 * slots : at + 3 * slots])
                unit = p[j, k].astype(f32)
                acts.append(jnp.concatenate([unit[:slots], unit[slots : 2 * slots]], axis=1))
                digits.append(unit[2 * slots : 3 * slots, :128])
    mods = jnp.concatenate(mods, axis=0)
    bias_ref[...] = jnp.sum(mods, axis=0, keepdims=True)
    ada_ref[...] = dot(jnp.concatenate(acts, axis=0).astype(bf16), mods.astype(bf16), 0, 0)
    conds = jnp.concatenate(conds, axis=0).astype(bf16)
    digits = jnp.concatenate(digits, axis=0)
    wide = (share + 127) // 128 * 128
    lane = lax.broadcasted_iota(jnp.int32, (digits.shape[0], wide), 1).astype(f32)
    first = (idx_ref[0] * share).astype(f32)
    for ref, n in ((time_ref, 0), (class_ref, 2)):
        index = digits[:, n : n + 1] * 32.0 + digits[:, n + 1 : n + 2] - first
        ref[...] = dot((index == lane).astype(bf16), conds, 0, 0)[:share]


def finish_cond(idx, gathered, planes, share, width):
    n = len(gathered)
    return pl.pallas_call(
        partial(finish_cond_body, n, share),
        in_specs=[SMEM] + [VMEM] * (2 * n),
        out_specs=[VMEM] * 4,
        out_shape=[
            jax.ShapeDtypeStruct((D, width), f32),
            jax.ShapeDtypeStruct((1, width), f32),
            jax.ShapeDtypeStruct((share, D), f32),
            jax.ShapeDtypeStruct((share, D), f32),
        ],
        compiler_params=params(size=40),
        cost_estimate=SHORT,
        name="finish_cond",
    )(idx, *gathered, *planes)


def swap(array, bit):
    count = lax.axis_size("dp")
    return lax.ppermute(array, "dp", [(i, i ^ bit) for i in range(count)])


def shift(array, step):
    count = lax.axis_size("mod")
    return lax.ppermute(array, "mod", [(i, (i + step) % count) for i in range(count)])


def take(array, index, size, axis=0):
    return lax.dynamic_slice_in_dim(array, index * size, size, axis)


def after(value, *earlier):
    return lax.optimization_barrier((value, *earlier))[0]


def fence(*values):
    return lax.optimization_barrier(values)


def around(piece):
    return [shift(piece, k) for k in range(1, 4)]


def three(near):
    return [near, swap(near, 2), swap(near, 4), swap(near, 6)]


def add(*terms):
    total = terms[0].astype(f32)
    for term in terms[1:]:
        total = total + term.astype(f32)
    return total.astype(bf16)


def spread_chips(grad):
    bit = 8
    while bit < lax.axis_size("dp"):
        grad = add(grad, swap(grad, bit))
        bit *= 2
    return grad


def pick_mod(grad, index):
    return lax.dynamic_index_in_dim(grad, index, 0, keepdims=False)


def local(
    block_input,
    grad_out,
    long_flag,
    valid_mask,
    labels,
    tsteps,
    time_table,
    class_table,
    w_ada,
    b_ada,
    w_qkv,
    qv_bias,
    w_proj,
    proj_bias,
    w_fc1,
    fc1_bias,
    w_fc2,
    fc2_bias,
    rel_table,
):
    mods_n = lax.axis_size("mod")
    me = lax.axis_index("mod")
    core = lax.axis_index("dp") % 2
    spot = (lax.axis_index("dp") // 2) % 4
    idx = jnp.stack([me, spot, core]).astype(jnp.int32)
    slots_n = MICRO * NSEG
    x = block_input.reshape(T, D)
    dy = grad_out.reshape(T, D)
    long_one = long_flag.reshape(MICRO)
    valid_seg = valid_mask.reshape(MICRO, NSEG, SEG)[:, :, 0]

    step_flat = tsteps.reshape(slots_n)
    label_flat = labels.reshape(slots_n)
    cond = time_table[step_flat].astype(f32) + class_table[label_flat].astype(f32)
    biases = jnp.stack([qv_bias, fc1_bias[:HALF], fc1_bias[HALF:], jnp.concatenate([proj_bias, fc2_bias])])
    own_a, piece_a = pick_entry(idx, w_qkv, w_proj)
    up_a, down_a = shift(piece_a, 1), shift(piece_a, mods_n - 1)
    own_1, own_2, piece_1, piece_2 = pick_ff(idx, w_fc1, w_fc2)
    packet = make_packet(
        idx, tsteps.reshape(MICRO, NSEG), labels.reshape(MICRO, NSEG), cond, biases, rel_table
    )
    up_a, down_a, packet, piece_1, piece_2 = fence(up_a, down_a, packet, piece_1, piece_2)
    far_a = shift(up_a, 1)
    packets = [packet] + around(packet)
    far_a, *packets = fence(far_a, *packets)

    def sides(got, also_x=None, also_y=None):
        near = jnp.concatenate([g[0] for g in got])
        units = near.shape[0]
        outs = []
        for bit, also in ((2, also_x), (4, also_y)):
            outs.append(swap(near if also is None else jnp.concatenate([near, also]), bit))
        return near, outs, jnp.concatenate([g[1] for g in got]), units

    def assemble(near, outs, diag, units):
        return jnp.stack([near, outs[0][:units], outs[1][:units], diag]).reshape(4, 3, units // 3, UR, HALF)

    shared = jnp.stack([p[:UR] for p in packets])
    near_a, side_a, diag_a, units = sides([up_a, far_a, down_a], shared, shared)
    columns = mod_columns(w_ada, b_ada.reshape(1, -1), packets)
    back = [columns[0]] + [shift(columns[k], mods_n - k) for k in range(1, mods_n)]
    mods, qkv_b1, qkv_b2, proj_b, fc1_b1, fc1_b2, fc2_b, rel_1, rel_2 = prepare(
        idx, long_one, valid_seg, back, packets
    )
    piece_1, mods = fence(piece_1, mods)
    up_1, down_1 = shift(piece_1, 1), shift(piece_1, mods_n - 1)
    a = entry_norm(x, mods)
    plane = [shared, side_a[0][units:], side_a[1][units:]]
    set_a = assemble(near_a, side_a, diag_a, units)
    qkv1 = qkv_half(0, idx, a, qkv_b1, own_a, set_a)
    qkv1, a, set_a, up_1, down_1, piece_2 = fence(qkv1, a, set_a, up_1, down_1, piece_2)
    peer_a = swap(set_a, 1)
    far_1 = shift(up_1, 1)
    up_2, down_2 = shift(piece_2, 1), shift(piece_2, mods_n - 1)
    o1, p1 = attend(qkv1, rel_1, long_one, valid_seg, LONG)
    qkv2 = qkv_half(1, idx, after(a, o1), qkv_b2, own_a, peer_a)
    qkv2, far_1, up_2, down_2 = fence(qkv2, far_1, up_2, down_2)
    set_1 = list(sides([up_1, far_1, down_1], None, plane[1]))
    far_2 = shift(up_2, 1)
    o2, p2 = attend(qkv2, rel_2, long_one, valid_seg, LONG)
    o2, far_2, *set_1[1] = fence(o2, far_2, *set_1[1])
    set_2 = list(sides([up_2, far_2, down_2]))
    hidden, m_in, attn, d_mlp, db_fc2 = middle(idx, o1, o2, proj_b, x, dy, mods, own_a, set_a, peer_a)
    m_in, *set_2[1] = fence(m_in, *set_2[1])
    plane = jnp.stack(plane + [set_1[1][1][set_1[3] :]])
    set_1, set_2 = assemble(*set_1), assemble(*set_2)
    peer_1, peer_2 = swap(set_1, 1), swap(set_2, 1)
    acc_o, acc_d, dw1_send, dw2_send, db1_first = mlp(idx, m_in, d_mlp, fc1_b1, own_1, own_2, set_1, set_2)
    acc_o, peer_1, peer_2 = fence(acc_o, peer_1, peer_2)
    from_core = [swap(dw1_send, 1), swap(dw2_send, 1)]
    ff, dm, dw1_keep, dw2_keep, db1_second = mlp(
        idx, m_in, d_mlp, fc1_b2, own_1, own_2, peer_1, peer_2, (acc_o, acc_d)
    )
    ff, dw1_keep, dw2_keep, *from_core = fence(ff, dw1_keep, dw2_keep, *from_core)

    def quarters_of(grads):
        return [g.reshape(g.shape[0], mods_n, 4, -1, g.shape[-1]) for g in grads]

    def mine(grads, other):
        return add(*[lax.dynamic_index_in_dim(g, lax.bitwise_xor(spot, other), 2, keepdims=False) for g in grads])

    dw1 = quarters_of([g[None] for g in (dw1_keep, from_core[0])])
    dw2 = [g.reshape(mods_n, HALF, D) for g in (dw2_keep, from_core[1])]

    def fc2_block(step):
        return [pick_mod(g, (me + step) % mods_n) for g in dw2]

    fc2_far = shift(add(*fc2_block(2)), 1)
    y, d_h, do1, do2, dwp_send, dwp_keep, dmod_mid, db_proj = back_middle(
        idx, hidden, dy, ff, fc2_b, dm, attn, mods, o1, o2, own_a, set_a, peer_a
    )
    do1, fc2_far = fence(do1, fc2_far)
    fc2_up = shift(add(*fc2_block(1), fc2_far), 1)
    fc2_down = shift(add(*fc2_block(mods_n - 1)), mods_n - 1)
    fc1_plane = [swap(mine(dw1, n)[0], 2 * n) for n in (1, 2, 3)]
    dq1, dk1, dv1, dt1, dbq1 = attend_back(qkv1, p1, do1, o1, LONG)
    dw_send = qkv_weight(a, dq1, dk1, dv1, dwp_send, SHORT)
    dq2, dk2, dv2, dt2, dbq2 = attend_back(qkv2, p2, after(do2, dw_send), o2, SHORT)
    dq2, dk2, dv2, dt2, dbq2, dw_send, dwp_keep, fc2_up, fc2_down, *fc1_plane = fence(
        dq2, dk2, dv2, dt2, dbq2, dw_send, dwp_keep, fc2_up, fc2_down, *fc1_plane
    )
    fc1_parts = spread_chips(add(mine(dw1, 0)[0], *fc1_plane))
    fc2_mine = add(*fc2_block(0), fc2_up, fc2_down).reshape(4, -1, D)
    dw_in = swap(dw_send, 1)
    plane_peer = swap(plane, 1)

    def ring(step, total):
        block = pick_mod(fc1_parts, (me + 2 * mods_n - 1 - step) % mods_n)
        return block if total is None else add(block, total)

    ff_ring = shift(ring(0, None), 1)
    dw_keep = qkv_weight(a, dq2, dk2, dv2, dwp_keep, LONG)
    dw_keep, dt2, dbq2, ff_ring, dw_in, plane_peer = fence(dw_keep, dt2, dbq2, ff_ring, dw_in, plane_peer)
    packed = pack_small(idx, dbq1, dbq2, db_proj, db1_first, db1_second, db_fc2, dt1, dt2).astype(bf16)
    packed = add(packed, swap(packed, 1))
    ff_ring = shift(ring(1, ff_ring), 1)
    d_h, ff_ring = fence(d_h, ff_ring)
    ff_ring = shift(ring(2, ff_ring), 1)

    dw = quarters_of([dw_keep, dw_in])

    def quarter(other):
        total = mine(dw, other)
        total = jnp.concatenate([total[0], total[1], packed], axis=1).reshape(-1, D)
        return jnp.concatenate([total, pick_mod(fc2_mine, lax.bitwise_xor(spot, other))])

    from_plane = [swap(quarter(n), 2 * n) for n in (1, 2, 3)]
    dx, d_mod = back_entry(
        idx, long_one, valid_seg, (dq1, dk1, dv1, dq2, dk2, dv2), x, d_h, mods, dmod_mid, own_a, set_a, peer_a
    )
    d_mod, dx, ff_ring = fence(d_mod, dx, ff_ring)
    mod_in = [pick_mod(d_mod, me)] + [shift(pick_mod(d_mod, (me + k) % mods_n), k) for k in range(1, mods_n)]
    share = cond_share(w_ada, mod_in)
    share, *from_plane = fence(share, *from_plane)
    parts = spread_chips(add(quarter(0), *from_plane))
    fc2_part = parts[-D // 8 :]
    parts = parts[: -D // 8].reshape(mods_n, -1, D)
    tail = [jnp.concatenate([pick_mod(parts, (me + k) % mods_n), share]) for k in range(mods_n)]
    tail_in = [shift(tail[k], k) for k in range(1, mods_n)]
    fc1_part = ring(3, ff_ring)
    ff_part = jnp.concatenate([fc1_part[:, :D], fc1_part[:, D:], fc2_part])
    ff_set = [ff_part, swap(ff_part, 2), swap(ff_part, 4)]
    def gather_chips(piece):
        mine = jnp.stack(three(piece))
        return mine, swap(mine, 1)

    *ff_set, tail_in[0], tail_in[1], tail_in[2] = fence(*ff_set, *tail_in)
    piece, small_all = tail_sum([tail[0]] + tail_in, mod_in, packets)
    grad_rel = jnp.concatenate([small_all[:3], small_all[3].reshape(3, 2 * L - D)], axis=1)[:, : rel_table.shape[1]]
    grad_qv, grad_fc1_b = small_all[5, : qv_bias.shape[0]], small_all[4]
    grad_proj_b, grad_fc2_b = take(small_all[6], me, proj_bias.shape[0]), take(small_all[7], me, fc2_bias.shape[0])
    grad_rel, grad_qv, grad_fc1_b, grad_proj_b, grad_fc2_b, *gathered = fence(
        grad_rel, grad_qv, grad_fc1_b, grad_proj_b, grad_fc2_b, *three(piece)
    )
    gathered = jnp.stack(gathered)
    gathered = gathered, swap(gathered, 1)
    ff_set = jnp.stack(ff_set + [swap(ff_part, 6)])
    grad_fc1, grad_fc2 = finish_ff(idx, ff_set, swap(ff_set, 1))
    grad_qkv, grad_proj = finish_attn(idx, *gathered)

    conds, acts = list(gathered), [plane, plane_peer]
    bit = 8
    while bit < lax.axis_size("dp"):
        conds += [swap(c, bit) for c in conds]
        acts += [swap(c, bit) for c in acts]
        bit *= 2
    grad_ada, grad_ada_b, grad_time, grad_class = finish_cond(
        idx, conds, acts, time_table.shape[0] // mods_n, w_ada.shape[1]
    )
    return (
        y.reshape(block_input.shape),
        dx.reshape(block_input.shape),
        grad_time,
        grad_class,
        grad_ada,
        grad_ada_b.reshape(-1),
        grad_qkv,
        grad_qv,
        grad_proj,
        grad_proj_b,
        grad_fc1,
        grad_fc1_b,
        grad_fc2,
        grad_fc2_b,
        grad_rel,
    )


def solution(mesh):
    in_specs = (
        P(None, ("dp", "mod"), None),
        P(None, ("dp", "mod"), None),
        P(None, ("dp", "mod")),
        P(None, ("dp", "mod")),
        P(None, ("dp", "mod")),
        P(None, ("dp", "mod")),
        P(),
        P(),
        P(None, "mod"),
        P("mod"),
        P("mod", None),
        P("mod"),
        P("mod", None),
        P("mod"),
        P("mod", None),
        P("mod"),
        P("mod", None),
        P("mod"),
        P("mod", None),
    )
    out_specs = (
        P(None, ("dp", "mod"), None),
        P(None, ("dp", "mod"), None),
        P("mod", None),
        P("mod", None),
        P(None, "mod"),
        P("mod"),
        P("mod", None),
        P("mod"),
        P("mod", None),
        P("mod"),
        P("mod", None),
        P("mod"),
        P("mod", None),
        P("mod"),
        P("mod", None),
    )
    return jax.shard_map(local, mesh=mesh, in_specs=in_specs, out_specs=out_specs, check_vma=False)
```
